32 devices in a mesh: dp: 4 (over y, x), fsdp: 8 (over z, core).
Axes of the slice: x: 2, y: 2, z: 4, core: 2. Of those that a mesh axis runs over, the one named last changes fastest.
Arguments:
- layer_entering_state: bfloat16 [24576, 1024], P(('dp', 'fsdp')), may hold values from -6 to 6
- exit_cotangent: bfloat16 [24576, 1024], P(('dp', 'fsdp')), may hold values from -6 to 6
- attend_norm_scaling: bfloat16 [1024], P('fsdp'), may hold values from 0.5 to 1.5
- branch_norm_scaling: bfloat16 [1024], P('fsdp'), may hold values from 0.5 to 1.5
- triple_coefficients: bfloat16 [1024, 2048], P('fsdp'), may hold values from -0.1875 to 0.1875
- attend_exit_coefficients: bfloat16 [1024, 1024], P('fsdp'), may hold values from -1.5 to 1.5
- dispatch_coefficients: bfloat16 [1024, 32], P('fsdp'), may hold values from -0.09375 to 0.09375
- branch_widen_coefficients: bfloat16 [32, 1024, 1024], P('dp', 'fsdp'), may hold values from -0.1875 to 0.1875
- branch_contract_coefficients: bfloat16 [32, 512, 1024], P('dp', 'fsdp'), may hold values from -1.5 to 1.5
- triple_plugin_source: bfloat16 [1024, 384], P('fsdp'), may hold values from -0.1875 to 0.1875
- asking_plugin_target: bfloat16 [128, 1024], P(None, 'fsdp'), may hold values from -0.75 to 0.75
- lookup_plugin_target: bfloat16 [128, 512], P(None, 'fsdp'), may hold values from -0.75 to 0.75
- content_plugin_target: bfloat16 [128, 512], P(None, 'fsdp'), may hold values from -0.75 to 0.75
- merge_plugin_source: bfloat16 [1024, 128], P('fsdp'), may hold values from -1.5 to 1.5
- merge_plugin_target: bfloat16 [128, 1024], P(None, 'fsdp'), may hold values from -0.75 to 0.75
- dispatch_plugin_source: bfloat16 [1024, 128], P('fsdp'), may hold values from -0.1875 to 0.1875
- dispatch_plugin_target: bfloat16 [128, 32], P('fsdp'), may hold values from -0.375 to 0.375
- branch_plugin_source: bfloat16 [32, 1024, 256], P('dp', 'fsdp'), may hold values from -0.1875 to 0.1875
- branch_plugin_target: bfloat16 [32, 2, 128, 512], P('dp', None, None, 'fsdp'), may hold values from -0.75 to 0.75
- contract_plugin_source: bfloat16 [32, 512, 128], P('dp', 'fsdp'), may hold values from -0.25 to 0.25
- contract_plugin_target: bfloat16 [32, 128, 1024], P('dp', None, 'fsdp'), may hold values from -4 to 4
- branch_choice_labels: int32 [24576, 8], P(('dp', 'fsdp')), may hold values from 0 to 31, all different within a row; in each aligned block of 384 rows (0 to 383, 384 to 767, ...) at most 108 rows name the same one
- plugin_choice_per_text: int32 [4, 16], P(None, 'fsdp'), may hold values from 0 to 7
- section_labels: int32 [64, 384], P(('dp', 'fsdp')), may hold values from 0 to 2, never falling along the last dimension, each value on 1 to 256 neighbouring positions
Outputs:
- block_out: bfloat16 [24576, 1024], P(('dp', 'fsdp'))
- grad_input: bfloat16 [24576, 1024], P(('dp', 'fsdp'))
- qkv_reduce_grad: float32 [1024, 384], P('fsdp')
- q_expand_grad: float32 [128, 1024], P(None, 'fsdp')
- k_expand_grad: float32 [128, 512], P(None, 'fsdp')
- v_expand_grad: float32 [128, 512], P(None, 'fsdp')
- out_reduce_grad: float32 [1024, 128], P('fsdp')
- out_expand_grad: float32 [128, 1024], P(None, 'fsdp')
- route_reduce_grad: float32 [1024, 128], P('fsdp')
- route_expand_grad: float32 [128, 32], P('fsdp')
- expert_reduce_grad: float32 [32, 1024, 256], P('dp', 'fsdp')
- expert_expand_grad: float32 [32, 2, 128, 512], P('dp', None, None, 'fsdp')
- down_reduce_grad: float32 [32, 512, 128], P('dp', 'fsdp')
- down_expand_grad: float32 [32, 128, 1024], P('dp', None, 'fsdp')
The draws below stay inside these ranges and needn't reach their ends.
Inputs may be any that keep to these rules, and one draw needn't show every extreme that they name: `branch_choice_labels`: each row names 8 different experts. Within the 384 rows of one sequence no expert is named more than 108 times, and in every draw some expert is named exactly 108 times in some sequence. `section_labels`: within each sequence the block numbers never fall, every number from 0 to 2 occurs, and each block holds 1 to 256 positions.
All inputs are finite; a program needn't handle non-finite values.
Results may differ from the reference program's by a relative error of at most 0.023.
Values may be sent and summed in bfloat16 or wider, within the bound.
No kernel may reach another device: no remote copies, remote signals or barrier semaphores. Data moves between devices by JAX's collectives and lax.ppermute only.
A program may use at most 384 MiB of HBM per device.

```python
import math
import jax
import jax.numpy as jnp
import numpy as np
from jax import lax

MODEL_BREADTH = 1024
H = 16
KVH = 8
HD = 64
FEEDFORWARD_SIZE = 512
TOPK = 8
PLUGIN_CHOICES = 8
REDUCED_DIM = 16
BLK = 256
SEQUENCE_TOKENS = 384
MB = 2
BRANCH_NUMBER = 32
CAP = 108
NBLK = 3
SEQS = 64
TOKENS = 24576
N_DP = 4
N_FSDP = 8


def plant(drawn, rng, least, largest):
    index_at = [jax.random.randint(jax.random.fold_in(rng, axis), (), 0, length) for axis, length in enumerate(drawn.shape)]
    longest = drawn.shape.index(max(drawn.shape))
    beside = index_at[:longest] + [(index_at[longest] + 1) % drawn.shape[longest]] + index_at[longest + 1:]
    return drawn.at[tuple(index_at)].set(least).at[tuple(beside)].set(largest)


def block_scale(key, dims, split, least, high):
    loudness, own = 1.0, jax.random.fold_in(key, 6)
    for axis_at, parts in split:
        heights = jnp.exp(jax.random.uniform(jax.random.fold_in(own, axis_at), (parts,), jnp.float32, least / len(split), high / len(split)))
        loudness = loudness * jnp.repeat(heights, dims[axis_at] // parts).reshape([-1 if axis == axis_at else 1 for axis in range(len(dims))])
    return loudness


def profile(count, total, most, slope):
    weights = [(1 << 20) // math.isqrt(rank ** slope) + 1 for rank in range(2, count + 1)]
    spare, holding = total - most - (count - 1), [1] * (count - 1)
    while spare > 0:
        candidates = [i for i in range(count - 1) if holding[i] < most]
        mass, left = sum([weights[i] for i in candidates]), spare
        for i in candidates:
            addition = min(most - holding[i], max(1, left * weights[i] // mass), spare)
            holding[i] = holding[i] + addition
            spare = spare - addition
    return np.array([most] + holding)


def uneven_parts(own_key, amount, total, bound, slope):
    if amount == 2:
        one = jax.random.randint(own_key, (), max(1, total - bound), min(bound, total - 1) + 1)
        return jnp.stack([one, total - one])
    tallies = jnp.asarray(profile(amount, total, bound, slope), jnp.int32)
    pairs = (amount - 1) // 2
    giver, sink = tallies[1:1 + 2 * pairs:2], tallies[2:2 + 2 * pairs:2]
    margin = jnp.minimum(giver - 1, bound - sink)
    shifted = jax.random.randint(jax.random.fold_in(own_key, 1), (pairs,), 0, 1 << 20) % (margin + 1)
    tallies = tallies.at[1:1 + 2 * pairs:2].set(giver - shifted).at[2:2 + 2 * pairs:2].set(sink + shifted)
    return tallies[jax.random.permutation(jax.random.fold_in(own_key, 2), amount)]


def shared_out(stream_key, own, number, rows, number_of, top, reach, slope):
    ranking = jax.random.permutation(stream_key, number_of)
    heavy_load, ordinary = load_shares(number_of, rows * top, reach, slope, True), load_shares(number_of, rows * top, reach, slope, False)
    places = jnp.arange(number_of)

    def named(lengths, turn):
        used = int((lengths > 0).sum())
        fixed = max(1, used // 4)
        shifted = fixed + (places - fixed + turn * (used - fixed)) % max(1, number_of - fixed)
        return jnp.zeros((number_of,), jnp.int32).at[ranking[jnp.where(places < fixed, places, shifted)]].set(jnp.asarray(lengths, jnp.int32))

    lengths = jnp.where(number % 4 == 0, named(heavy_load, number // 4), named(ordinary, number - number // 4 - 1))
    mixed = jax.random.permutation(jax.random.fold_in(own, 3), number_of)
    giver, taker = mixed[0:number_of // 2 * 2:2], mixed[1:number_of // 2 * 2:2]
    room = jnp.minimum(lengths[giver] - 1, reach - lengths[taker]) // 2
    room = jnp.where((giver == ranking[0]) | (taker == ranking[0]) | (lengths[taker] == 0), 0, jnp.maximum(room, 0))
    shifted = jax.random.randint(jax.random.fold_in(own, 4), (number_of // 2,), 0, 1 << 20) % (room + 1)
    lengths = lengths.at[giver].add(-shifted).at[taker].add(shifted)
    members = jnp.searchsorted(jnp.cumsum(lengths), jnp.arange(rows * top), side="right").astype(jnp.int32)
    listing = members.reshape(top, rows).T
    listing = listing[jax.random.permutation(jax.random.fold_in(own, 1), rows)]
    turn = jax.random.randint(jax.random.fold_in(own, 2), (rows, 1), 0, top)
    return jnp.take_along_axis(listing, (jnp.arange(top)[None, :] + turn) % top, axis=1)


def load_shares(number_of, total, bound, skew, full):
    weights = [(1 << 20) // math.isqrt(grade ** skew) + 1 for grade in range(1, number_of + 1)]
    largest = bound if full else min(bound, max(-(-total // number_of), total * weights[0] // sum(weights)))
    least = 1 if total - largest >= number_of - 1 else 0
    given, surplus = [largest] + [least] * (number_of - 1), total - largest - least * (number_of - 1)
    while surplus > 0:
        movable = [i for i in range(1, number_of) if given[i] < largest] or [i for i in range(1, number_of) if given[i] < bound]
        whole, budget = sum([weights[i] for i in movable]), surplus
        for i in movable:
            more = min(bound - given[i], max(1, budget * weights[i] // whole), surplus)
            given[i] = given[i] + more
            surplus = surplus - more
    return np.array(given)


def centred(rng, dims, width, most, cuts=(), held_as=jnp.bfloat16):
    drawn = jax.random.normal(rng, dims, jnp.float32) * width
    if len(cuts) > 0:
        drawn = block_scale(rng, dims, cuts, -0.22, 0.18) * drawn
    return jnp.clip(drawn, min=-most, max=most).astype(held_as)


def setup_inputs(seed: int = 0) -> dict:
    key_list = jax.random.split(jax.random.key(seed), 25)
    layer_entering_state = centred(key_list[0], (TOKENS, MODEL_BREADTH), 1.0, 6.0, ((0, 32),))
    exit_cotangent = centred(key_list[1], (TOKENS, MODEL_BREADTH), 1.0, 6.0, ((0, 32),))
    attend_norm_scaling = jnp.clip(1.0 + 0.1 * jax.random.normal(key_list[2], (MODEL_BREADTH,), jnp.float32), 0.5, 1.5).astype(jnp.bfloat16)
    branch_norm_scaling = jnp.clip(1.0 + 0.1 * jax.random.normal(key_list[3], (MODEL_BREADTH,), jnp.float32), 0.5, 1.5).astype(jnp.bfloat16)
    triple_coefficients = centred(key_list[4], (MODEL_BREADTH, (H + 2 * KVH) * HD), MODEL_BREADTH ** -0.5, 0.1875, ((0, 8),))
    attend_exit_coefficients = centred(key_list[5], (H * HD, MODEL_BREADTH), (H * HD // 64) ** -0.5, 1.5, ((0, 8),))
    dispatch_coefficients = centred(key_list[6], (MODEL_BREADTH, BRANCH_NUMBER), (4 * MODEL_BREADTH) ** -0.5, 0.09375, ((0, 8),))
    branch_widen_coefficients = centred(key_list[7], (BRANCH_NUMBER, MODEL_BREADTH, 2 * FEEDFORWARD_SIZE), MODEL_BREADTH ** -0.5, 0.1875, ((0, 4), (1, 8)))
    branch_contract_coefficients = centred(key_list[8], (BRANCH_NUMBER, FEEDFORWARD_SIZE, MODEL_BREADTH), (FEEDFORWARD_SIZE // 32) ** -0.5, 1.5, ((0, 4), (1, 8)))
    triple_plugin_source = centred(key_list[9], (MODEL_BREADTH, 3 * PLUGIN_CHOICES * REDUCED_DIM), MODEL_BREADTH ** -0.5, 0.1875, ((0, 8),))
    asking_plugin_target = centred(key_list[10], (PLUGIN_CHOICES * REDUCED_DIM, H * HD), (4 * REDUCED_DIM) ** -0.5, 0.75, ((1, 8),))
    lookup_plugin_target = centred(key_list[11], (PLUGIN_CHOICES * REDUCED_DIM, KVH * HD), (4 * REDUCED_DIM) ** -0.5, 0.75, ((1, 8),))
    content_plugin_target = centred(key_list[12], (PLUGIN_CHOICES * REDUCED_DIM, KVH * HD), (4 * REDUCED_DIM) ** -0.5, 0.75, ((1, 8),))
    merge_plugin_source = centred(key_list[13], (H * HD, PLUGIN_CHOICES * REDUCED_DIM), (H * HD // 64) ** -0.5, 1.5, ((0, 8),))
    merge_plugin_target = centred(key_list[14], (PLUGIN_CHOICES * REDUCED_DIM, MODEL_BREADTH), (4 * REDUCED_DIM) ** -0.5, 0.75, ((1, 8),))
    dispatch_plugin_source = centred(key_list[15], (MODEL_BREADTH, PLUGIN_CHOICES * REDUCED_DIM), MODEL_BREADTH ** -0.5, 0.1875, ((0, 8),))
    dispatch_plugin_target = centred(key_list[16], (PLUGIN_CHOICES * REDUCED_DIM, BRANCH_NUMBER), (16 * REDUCED_DIM) ** -0.5, 0.375, ((0, 8),))
    branch_plugin_source = centred(key_list[17], (BRANCH_NUMBER, MODEL_BREADTH, 2 * PLUGIN_CHOICES * REDUCED_DIM), MODEL_BREADTH ** -0.5, 0.1875, ((0, 4), (1, 8)))
    branch_plugin_target = centred(key_list[18], (BRANCH_NUMBER, 2, PLUGIN_CHOICES * REDUCED_DIM, FEEDFORWARD_SIZE), (4 * REDUCED_DIM) ** -0.5, 0.75, ((0, 4), (3, 8)))
    contract_plugin_source = centred(key_list[19], (BRANCH_NUMBER, FEEDFORWARD_SIZE, PLUGIN_CHOICES * REDUCED_DIM), FEEDFORWARD_SIZE ** -0.5, 0.25, ((0, 4), (1, 8)))
    contract_plugin_target = centred(key_list[20], (BRANCH_NUMBER, PLUGIN_CHOICES * REDUCED_DIM, MODEL_BREADTH), (REDUCED_DIM // 8) ** -0.5, 4.0, ((0, 4), (2, 8)))
    branch_choice_labels_keys = jax.random.split(jax.random.fold_in(key_list[21], 1), TOKENS // SEQUENCE_TOKENS)
    branch_choice_labels_turns = jax.random.permutation(jax.random.fold_in(key_list[21], 3), TOKENS // SEQUENCE_TOKENS)
    branch_choice_labels = jax.vmap(lambda own, number: shared_out(jax.random.fold_in(key_list[21], 2), own, number, SEQUENCE_TOKENS, BRANCH_NUMBER, TOPK, CAP, 1))(branch_choice_labels_keys, branch_choice_labels_turns).reshape((TOKENS, TOPK))
    plugin_choice_per_text = plant(jax.random.randint(key_list[22], (N_DP, N_FSDP * MB), 0, PLUGIN_CHOICES), jax.random.fold_in(key_list[22], 1), 0, PLUGIN_CHOICES - 1).astype(jnp.int32)
    section_labels = jax.vmap(lambda own: jnp.searchsorted(jnp.cumsum(uneven_parts(own, NBLK, SEQUENCE_TOKENS, BLK, 0)), jnp.arange(SEQUENCE_TOKENS), side="right"))(jax.random.split(key_list[23], SEQS)).reshape((SEQS, SEQUENCE_TOKENS)).astype(jnp.int32)
    return dict(layer_entering_state=layer_entering_state, exit_cotangent=exit_cotangent, attend_norm_scaling=attend_norm_scaling, branch_norm_scaling=branch_norm_scaling, triple_coefficients=triple_coefficients, attend_exit_coefficients=attend_exit_coefficients, dispatch_coefficients=dispatch_coefficients, branch_widen_coefficients=branch_widen_coefficients, branch_contract_coefficients=branch_contract_coefficients, triple_plugin_source=triple_plugin_source, asking_plugin_target=asking_plugin_target, lookup_plugin_target=lookup_plugin_target, content_plugin_target=content_plugin_target, merge_plugin_source=merge_plugin_source, merge_plugin_target=merge_plugin_target, dispatch_plugin_source=dispatch_plugin_source, dispatch_plugin_target=dispatch_plugin_target, branch_plugin_source=branch_plugin_source, branch_plugin_target=branch_plugin_target, contract_plugin_source=contract_plugin_source, contract_plugin_target=contract_plugin_target, branch_choice_labels=branch_choice_labels, plugin_choice_per_text=plugin_choice_per_text, section_labels=section_labels)


eps_norm = 1e-06
rope_base = 10000.0
per_step = 8
highest = lax.Precision.HIGHEST

@jax.custom_vjp
def thin_update_forward(v):
    return lax.optimization_barrier(v.astype(jnp.bfloat16)).astype(jnp.float32)

@jax.custom_vjp
def thin_update_reverse(v):
    return v

def low_keep(v):
    return (thin_update_forward(v), None)

def low_pass(kept, grad):
    return (grad,)

def back_keep(v):
    return (v, None)

def back_low(kept, grad):
    return (thin_update_forward(grad),)
thin_update_forward.defvjp(low_keep, low_pass)
thin_update_reverse.defvjp(back_keep, back_low)

def product_result(operand, factor):
    return jnp.dot(operand, factor, precision=highest)

def layered_times_effect(pattern, operand, factor):
    return jnp.einsum(pattern, operand, factor, precision=highest)

def norm_scale(values, gain_vec):
    inverse = lax.rsqrt(lax.optimization_barrier(jnp.mean(values * values, axis=-1, keepdims=True)) + eps_norm)
    return values * inverse * gain_vec

def rotation(length, head_size):
    half_size = head_size // 2
    frequency = rope_base ** (-(2.0 * jnp.arange(half_size, dtype=jnp.float32)) / head_size)
    angles = jnp.arange(length, dtype=jnp.float32)[:, None] * frequency[None, :]
    return (jnp.cos(angles)[:, None, :], jnp.sin(angles)[:, None, :])

def rotate(values, cos_table, sin_table):
    half_size = values.shape[-1] // 2
    leading = values[..., :half_size]
    trailing = values[..., half_size:]
    return jnp.concatenate([leading * cos_table - trailing * sin_table, trailing * cos_table + leading * sin_table], axis=-1)

def group_layer(frozen, plugin_modules, grouped_hidden, adapter_group, block_group, index_group, place_group, expert_group):
    attend_norm_scaling, branch_norm_scaling, triple_coefficients, attend_exit_coefficients, dispatch_coefficients, branch_widen_coefficients, branch_contract_coefficients = frozen
    triple_plugin_source, asking_plugin_target, lookup_plugin_target, content_plugin_target, merge_plugin_source, merge_plugin_target, dispatch_plugin_source, dispatch_plugin_target, branch_plugin_source, branch_plugin_target, contract_plugin_source, contract_plugin_target = plugin_modules
    sequence_group_size = grouped_hidden.shape[0]
    adapter_width = PLUGIN_CHOICES * REDUCED_DIM
    query_width = H * HD
    key_value_width = KVH * HD
    repeat = H // KVH
    column_holder = jnp.arange(adapter_width, dtype=jnp.int32) // REDUCED_DIM
    sequence_mask = (column_holder[None, :] == adapter_group[:, None]).astype(jnp.float32)
    normalized_input = thin_update_forward(norm_scale(grouped_hidden, attend_norm_scaling))
    query_key_value_mask = jnp.tile(sequence_mask, (1, 3))[:, None, :]
    adapter_query_key_value = thin_update_forward(query_key_value_mask * thin_update_reverse(product_result(normalized_input, triple_plugin_source)))
    adapter_pieces = jnp.concatenate([product_result(adapter_query_key_value[..., :adapter_width], asking_plugin_target), product_result(adapter_query_key_value[..., adapter_width:2 * adapter_width], lookup_plugin_target), product_result(adapter_query_key_value[..., 2 * adapter_width:], content_plugin_target)], axis=-1)
    projected_rows = thin_update_reverse(product_result(normalized_input, triple_coefficients) + adapter_pieces)
    cos_table, sin_table = rotation(SEQUENCE_TOKENS, HD)
    queries = thin_update_forward(rotate(projected_rows[..., :query_width].reshape(sequence_group_size, SEQUENCE_TOKENS, H, HD), cos_table, sin_table))
    keys_rot = thin_update_forward(rotate(projected_rows[..., query_width:query_width + key_value_width].reshape(sequence_group_size, SEQUENCE_TOKENS, KVH, HD), cos_table, sin_table))
    values_r = thin_update_forward(projected_rows[..., query_width + key_value_width:].reshape(sequence_group_size, SEQUENCE_TOKENS, KVH, HD))
    grouped = queries.reshape(sequence_group_size, SEQUENCE_TOKENS, KVH, repeat, HD)
    scores = thin_update_reverse(layered_times_effect('gqnrd,gknd->gnrqk', grouped, keys_rot) * HD ** (-0.5))
    allowed = block_group[:, None, :] <= block_group[:, :, None]
    scores = jnp.where(allowed[:, None, None], scores, -1e+30)
    weights = thin_update_forward(jax.nn.softmax(scores, axis=-1))
    attention_output = layered_times_effect('gnrqk,gknd->gqnrd', weights, values_r).reshape(sequence_group_size, SEQUENCE_TOKENS, query_width)
    attention_output = thin_update_forward(thin_update_reverse(attention_output))
    adapter_output_maps = thin_update_forward(sequence_mask[:, None, :] * thin_update_reverse(product_result(attention_output, merge_plugin_source)))
    residual_stream = grouped_hidden + thin_update_reverse(product_result(attention_output, attend_exit_coefficients) + product_result(adapter_output_maps, merge_plugin_target))
    mixture_input = thin_update_forward(norm_scale(residual_stream, branch_norm_scaling))
    adapter_router_result = thin_update_forward(sequence_mask[:, None, :] * thin_update_reverse(product_result(mixture_input, dispatch_plugin_source)))
    router_logits = thin_update_reverse(product_result(mixture_input, dispatch_coefficients) + product_result(adapter_router_result, dispatch_plugin_target)).reshape(sequence_group_size * SEQUENCE_TOKENS, BRANCH_NUMBER)
    chosen = jnp.take_along_axis(router_logits, expert_group, axis=1)
    gate_weights = jax.nn.softmax(chosen, axis=-1)
    flat_in = jnp.concatenate([mixture_input.reshape(sequence_group_size * SEQUENCE_TOKENS, MODEL_BREADTH), jnp.zeros((1, MODEL_BREADTH), jnp.float32)], axis=0)
    expert_input_rows = thin_update_reverse(flat_in[index_group])
    slot_seq = jnp.arange(sequence_group_size * CAP, dtype=jnp.int32) // CAP
    slot_legit_filter = sequence_mask[slot_seq]
    adapter_input_maps = thin_update_forward(jnp.tile(slot_legit_filter, (1, 2))[None] * thin_update_reverse(layered_times_effect('gom,gms->gos', expert_input_rows, branch_plugin_source)))
    gate_up_product = layered_times_effect('erd,edf->erf', expert_input_rows, branch_widen_coefficients)
    gate_up_product = gate_up_product + jnp.concatenate([layered_times_effect('dwa,dat->dwt', adapter_input_maps[..., :adapter_width], branch_plugin_target[:, 0]), layered_times_effect('dwa,dat->dwt', adapter_input_maps[..., adapter_width:], branch_plugin_target[:, 1])], axis=-1)
    gate_up_product = thin_update_reverse(gate_up_product)
    between_curved_array = thin_update_forward(jax.nn.silu(gate_up_product[..., :FEEDFORWARD_SIZE]) * gate_up_product[..., FEEDFORWARD_SIZE:])
    thin_contracted_effect = thin_update_forward(slot_legit_filter[None] * thin_update_reverse(layered_times_effect('uri,uih->urh', between_curved_array, contract_plugin_source)))
    branch_produced_parts = layered_times_effect('bqn,bnw->bqw', between_curved_array, branch_contract_coefficients) + layered_times_effect('acn,anp->acp', thin_contracted_effect, contract_plugin_target)
    branch_produced_parts = thin_update_forward(thin_update_reverse(branch_produced_parts)).reshape(BRANCH_NUMBER * sequence_group_size * CAP, MODEL_BREADTH)
    returned = branch_produced_parts[place_group].reshape(sequence_group_size * SEQUENCE_TOKENS, TOPK, MODEL_BREADTH)
    mixture = lax.optimization_barrier(jnp.sum(gate_weights[:, :, None] * returned, axis=1))
    return residual_stream + mixture.reshape(sequence_group_size, SEQUENCE_TOKENS, MODEL_BREADTH)

def reference(layer_entering_state, exit_cotangent, attend_norm_scaling, branch_norm_scaling, triple_coefficients, attend_exit_coefficients, dispatch_coefficients, branch_widen_coefficients, branch_contract_coefficients, triple_plugin_source, asking_plugin_target, lookup_plugin_target, content_plugin_target, merge_plugin_source, merge_plugin_target, dispatch_plugin_source, dispatch_plugin_target, branch_plugin_source, branch_plugin_target, contract_plugin_source, contract_plugin_target, branch_choice_labels, plugin_choice_per_text, section_labels):
    seq_count = plugin_choice_per_text.shape[0] * plugin_choice_per_text.shape[1]
    group_count = seq_count // per_step
    pair_count = SEQUENCE_TOKENS * TOPK
    flat_ids = branch_choice_labels.reshape(seq_count, pair_count).astype(jnp.int32)
    hit_table = (flat_ids[:, :, None] == jnp.arange(BRANCH_NUMBER, dtype=jnp.int32)[None, None, :]).astype(jnp.int32)
    slot_index = lax.optimization_barrier(jnp.sum((jnp.cumsum(hit_table, axis=1) - hit_table) * hit_table, axis=2)).astype(jnp.int32)
    seq_index = jnp.arange(seq_count, dtype=jnp.int32)[:, None]
    seq_in_group = seq_index % per_step
    group_index = jnp.broadcast_to(seq_index // per_step, (seq_count, pair_count)).astype(jnp.int32)
    token_row = (seq_in_group * SEQUENCE_TOKENS + jnp.arange(pair_count, dtype=jnp.int32)[None, :] // TOPK).astype(jnp.int32)
    slot_pos = (seq_in_group * CAP + slot_index).astype(jnp.int32)
    index_table = jnp.full((group_count, BRANCH_NUMBER, per_step * CAP), per_step * SEQUENCE_TOKENS, jnp.int32).at[group_index, flat_ids, slot_pos].set(token_row)
    place_table = (flat_ids * (per_step * CAP) + slot_pos).astype(jnp.int32).reshape(group_count, per_step * pair_count)
    frozen = tuple((coefficients_entering.astype(jnp.float32) for coefficients_entering in (attend_norm_scaling, branch_norm_scaling, triple_coefficients, attend_exit_coefficients, dispatch_coefficients, branch_widen_coefficients, branch_contract_coefficients)))
    plugin_modules = tuple((coefficients_entering.astype(jnp.float32) for coefficients_entering in (triple_plugin_source, asking_plugin_target, lookup_plugin_target, content_plugin_target, merge_plugin_source, merge_plugin_target, dispatch_plugin_source, dispatch_plugin_target, branch_plugin_source, branch_plugin_target, contract_plugin_source, contract_plugin_target)))
    hidden = layer_entering_state.astype(jnp.float32).reshape(group_count, per_step, SEQUENCE_TOKENS, MODEL_BREADTH)
    adapter_groups = plugin_choice_per_text.reshape(group_count, per_step).astype(jnp.int32)
    block_groups = section_labels.reshape(group_count, per_step, SEQUENCE_TOKENS).astype(jnp.int32)
    expert_groups = branch_choice_labels.reshape(group_count, per_step * SEQUENCE_TOKENS, TOPK).astype(jnp.int32)

    def forward(hidden_all, adapters_all):

        def scan_step(carried, sliced):
            grouped_hidden, adapter_group, block_group, index_group, place_group, expert_group = sliced
            return (carried, group_layer(frozen, adapters_all, grouped_hidden, adapter_group, block_group, index_group, place_group, expert_group))
        checked = jax.checkpoint(scan_step)
        unused, stacked = lax.scan(checked, jnp.zeros((), jnp.float32), (hidden_all, adapter_groups, block_groups, index_table, place_table, expert_groups))
        return stacked
    block_out, pullback = jax.vjp(forward, hidden, plugin_modules)
    grad_hidden, grad_adapters = pullback(exit_cotangent.astype(jnp.float32).reshape(hidden.shape))
    return (block_out.reshape(-1, MODEL_BREADTH).astype(jnp.bfloat16), grad_hidden.reshape(-1, MODEL_BREADTH).astype(jnp.bfloat16), grad_adapters[0], grad_adapters[1], grad_adapters[2], grad_adapters[3], grad_adapters[4], grad_adapters[5], grad_adapters[6], grad_adapters[7], grad_adapters[8], grad_adapters[9], grad_adapters[10], grad_adapters[11])
```

```python
import functools

import jax
import jax.numpy as jnp
from jax import lax
from jax.experimental import pallas as pl
from jax.experimental.pallas import tpu as pltpu
from jax.sharding import PartitionSpec as P

H = 16
KVH = 8
HD = 64
FEEDFORWARD_SIZE = 512
PLUGIN_CHOICES = 8
REDUCED_DIM = 16

eps_norm = 1e-06
rope_base = 10000.0

LANES = 128
SHARDS = 8
CHUNKS = (2, 2, 2, 2)
VMEM = 60 * 1024 * 1024

f32 = jnp.float32
bf16 = jnp.bfloat16


def nn(a, b):
    return lax.dot_general(a, b, (((1,), (0,)), ((), ())), preferred_element_type=f32)


def nt(a, b):
    return lax.dot_general(a, b, (((1,), (1,)), ((), ())), preferred_element_type=f32)


def tn(a, b):
    return lax.dot_general(a, b, (((0,), (0,)), ((), ())), preferred_element_type=f32)


matrix_product = nn
matrix_product_transposed = nt
outer_product_sum = tn


def layered_times_effect(pattern, operand, factor):
    return jnp.einsum(pattern, operand, factor, preferred_element_type=f32)


def norm_scale(values, gain_vec):
    inverse = lax.rsqrt(jnp.mean(values * values, axis=-1, keepdims=True) + eps_norm)
    return (values * inverse * gain_vec, inverse)


def norm_back(values, inverse, gain_vec, upstream):
    scaled = gain_vec * upstream
    feature_count = values.shape[-1]
    weighted_sum = jnp.sum(values * scaled, axis=-1, keepdims=True)
    return inverse * scaled - values * (inverse * inverse * inverse) * weighted_sum / feature_count


def rotation(length, head_size):
    half_size = head_size // 2
    frequency = rope_base ** (-(2.0 * jnp.arange(half_size, dtype=f32)) / head_size)
    angles = jnp.arange(length, dtype=f32)[:, None] * frequency[None, :]
    return (jnp.cos(angles)[:, None, :], jnp.sin(angles)[:, None, :])


def rotate(values, cos_table, sin_table):
    half_size = values.shape[-1] // 2
    leading = values[..., :half_size]
    trailing = values[..., half_size:]
    return jnp.concatenate(
        [leading * cos_table - trailing * sin_table, trailing * cos_table + leading * sin_table],
        axis=-1,
    )


def rotate_back(values, cos_table, sin_table):
    half_size = values.shape[-1] // 2
    leading = values[..., :half_size]
    trailing = values[..., half_size:]
    return jnp.concatenate(
        [leading * cos_table + trailing * sin_table, trailing * cos_table - leading * sin_table],
        axis=-1,
    )


def columns_to_rows(a):
    r, c = a.shape[-2:]
    b = c // LANES
    a = a.reshape(a.shape[:-1] + (b, LANES))
    return jnp.swapaxes(a, -3, -2).reshape(a.shape[:-3] + (b * r, LANES))


def rows_to_columns(a, blocks):
    n, br, _ = a.shape
    r = br // blocks
    return a.reshape(n, blocks, r, LANES).transpose(0, 2, 1, 3).reshape(n * r, blocks * LANES)


def pad_lanes(a):
    return jnp.pad(a, ((0, 0), (0, LANES - a.shape[-1])))


def expert_segments(width, inner):
    ru, rd = width // SHARDS, inner // SHARDS
    return (ru * width // LANES, rd * width // LANES, 2 * ru, 2 * rd, rd, ru)


def pack_experts(widen, contract, up_source, up_target, down_source, down_target):
    count = widen.shape[0]
    return jnp.concatenate(
        [
            columns_to_rows(widen),
            columns_to_rows(contract),
            columns_to_rows(up_source),
            jnp.swapaxes(up_target, 2, 3).reshape(count, -1, LANES),
            down_source,
            jnp.swapaxes(down_target, 1, 2),
        ],
        axis=1,
    )


def regroup(gathered, width, inner):
    n, count = gathered.shape[:2]
    if n == SHARDS:
        return gathered
    per = n // SHARDS
    pieces, at = [], 0
    ru, rd = width // n, inner // n
    blocks = ((width // LANES, ru), (width // LANES, rd), (2, ru), (2, rd), (1, rd), (1, ru))
    for b, r in blocks:
        piece = gathered[:, :, at : at + b * r].reshape(SHARDS, per, count, b, r, LANES)
        at += b * r
        pieces.append(piece.transpose(0, 2, 3, 1, 4, 5).reshape(SHARDS, count, b * per * r, LANES))
    return jnp.concatenate(pieces, axis=2)


def hits_of(rank_row, capacity):
    rows = lax.broadcasted_iota(jnp.int32, (capacity, rank_row.shape[1]), 0)
    return rows == rank_row


def dispatch_kernel(capacity, x_ref, c_ref, rank_ref, gate_ref, xs_ref, cs_ref, gs_ref):
    count = rank_ref.shape[1]
    hot = []
    for e in range(count):
        hits = hits_of(rank_ref[0, e : e + 1, :], capacity)
        hot.append(jnp.where(hits, 1.0, 0.0).astype(bf16))
        gate = jnp.sum(jnp.where(hits, gate_ref[0, e : e + 1, :], 0.0), axis=1, keepdims=True)
        gs_ref[0, e] = jnp.broadcast_to(gate, (capacity, LANES))
    hot = jnp.concatenate(hot, axis=0)
    shape = xs_ref.shape[1:]
    xs_ref[0] = nn(hot, x_ref[...]).astype(bf16).reshape(shape)
    cs_ref[0] = nn(hot, c_ref[...]).astype(bf16).reshape(shape)


def dispatch(rows, cotangent, rank, gate, capacity):
    micro, count, length = rank.shape
    width = rows.shape[1]
    row_spec = pl.BlockSpec((length, width), lambda m: (m, 0))
    table = pl.BlockSpec((1, count, length), lambda m: (m, 0, 0))
    out_spec = pl.BlockSpec((1, count, capacity, width), lambda m: (m, 0, 0, 0))
    slots = micro * count * capacity
    return pl.pallas_call(
        functools.partial(dispatch_kernel, capacity),
        grid=(micro,),
        in_specs=[row_spec, row_spec, table, table],
        out_specs=[
            out_spec,
            out_spec,
            pl.BlockSpec((1, count, capacity, LANES), lambda m: (m, 0, 0, 0)),
        ],
        out_shape=[
            jax.ShapeDtypeStruct((micro, count, capacity, width), bf16),
            jax.ShapeDtypeStruct((micro, count, capacity, width), bf16),
            jax.ShapeDtypeStruct((micro, count, capacity, LANES), f32),
        ],
        compiler_params=pltpu.CompilerParams(vmem_limit_bytes=VMEM),
        cost_estimate=pl.CostEstimate(
            flops=4 * slots * length * width, bytes_accessed=8 * slots * width, transcendentals=0
        ),
        name="dispatch",
    )(rows, cotangent, rank, gate)


def expert_kernel(groups, *refs):
    n = groups
    x_refs, c_refs, g_refs = refs[:n], refs[n : 2 * n], refs[2 * n : 3 * n]
    w_ref, mask_ref = refs[3 * n : 3 * n + 2]
    outs = refs[3 * n + 2 :]
    y_refs, m_refs, gg_refs = outs[:n], outs[n : 2 * n], outs[2 * n : 3 * n]
    grad_ref = outs[3 * n]
    wide, deep, source, sums_a, sums_b, sums_c, sums_d, sums_e = outs[3 * n + 1 :]
    micro, _, capacity, width = x_refs[0].shape
    inner_width = deep.shape[0]
    ru, rd = width // SHARDS, inner_width // SHARDS
    blocks = width // LANES
    at = 0

    def part(rows):
        nonlocal at
        value = w_ref[:, 0, at : at + rows, :].reshape(SHARDS * rows, LANES)
        at += rows
        return value

    for j in range(blocks):
        wide[:, j * LANES : (j + 1) * LANES] = part(ru)
    for j in range(blocks):
        deep[:, j * LANES : (j + 1) * LANES] = part(rd)
    for j in range(2):
        source[:, j * LANES : (j + 1) * LANES] = part(ru)
    target_gate, target_up = part(rd), part(rd)
    down_source = part(rd)
    down_target = part(ru)

    step = 2
    for first in range(0, n, step):
        ks = range(first, first + step)

        def rows_of(rs):
            return jnp.concatenate(
                [rs[k][:, 0].reshape(micro * capacity, rs[k].shape[3]) for k in ks], axis=0
            )

        x = rows_of(x_refs)
        cot = rows_of(c_refs)
        gate_of_slot = rows_of(g_refs)[:, :1]
        mask = jnp.concatenate(
            [
                jnp.broadcast_to(mask_ref[k, m : m + 1, :], (capacity, LANES))
                for k in ks
                for m in range(micro)
            ],
            axis=0,
        )
        mask2 = jnp.concatenate([mask, mask], axis=1)
        lora = (nn(x, source[...]) * mask2).astype(bf16)
        gate_up = nn(x, wide[...])
        gate = gate_up[:, :inner_width] + nt(lora[:, :LANES], target_gate)
        up = gate_up[:, inner_width:] + nt(lora[:, LANES:], target_up)
        sig = jax.nn.sigmoid(gate)
        silu = gate * sig
        inner = (silu * up).astype(bf16)
        down_lora = (nn(inner, down_source) * mask).astype(bf16)
        rows = (nn(inner, deep[...]) + nt(down_lora, down_target)).astype(bf16)
        rows_f = rows.astype(f32)
        cot_f = cot.astype(f32)
        product = jnp.sum(rows_f * cot_f, axis=1, keepdims=True)
        weighted = (rows_f * gate_of_slot).astype(bf16)
        row_grad = (cot_f * gate_of_slot).astype(bf16)
        down_lora_grad = (nn(row_grad, down_target) * mask).astype(bf16)
        inner_grad = nt(row_grad, deep[...]) + nt(down_lora_grad, down_source)
        gate_grad = (inner_grad * up * (sig * (1.0 + gate * (1.0 - sig)))).astype(bf16)
        up_grad = (inner_grad * silu).astype(bf16)
        lora_grad = (
            jnp.concatenate([nn(gate_grad, target_gate), nn(up_grad, target_up)], axis=1) * mask2
        ).astype(bf16)
        back = (
            nt(gate_grad, wide[:, :inner_width])
            + nt(up_grad, wide[:, inner_width:])
            + nt(lora_grad, source[...])
        ).astype(bf16)
        for i, k in enumerate(ks):
            size = micro * capacity
            here = slice(i * size, (i + 1) * size)
            y_refs[k][:, 0] = weighted[here].reshape(micro, capacity, width)
            m_refs[k][:, 0] = back[here].reshape(micro, capacity, width)
            gg_refs[k][:, 0] = jnp.broadcast_to(product[here], (size, LANES)).reshape(
                micro, capacity, LANES
            )
        terms = (
            tn(lora_grad, x),
            tn(lora[:, :LANES], gate_grad),
            tn(lora[:, LANES:], up_grad),
            tn(down_lora_grad, inner),
            tn(down_lora, row_grad),
        )
        held = (sums_a, sums_b, sums_c, sums_d, sums_e)
        for ref, term in zip(held, terms):
            ref[...] = term if first == 0 else ref[...] + term
    out = 0
    for s in range(SHARDS):
        grad_ref[s, 0, : 2 * LANES] = sums_a[:, s * ru : (s + 1) * ru].astype(bf16)
    out = 2 * LANES
    for ref in (sums_b, sums_c, sums_d):
        turned = ref[...].T.astype(bf16).reshape(SHARDS, rd, LANES)
        grad_ref[:, 0, out : out + rd] = turned
        out += rd
    for s in range(SHARDS):
        grad_ref[s, 0, out : out + LANES] = sums_e[:, s * ru : (s + 1) * ru].astype(bf16)


def expert_chunk(xs, cs, gs, weights, masks, first, inner_width):
    n = len(xs)
    micro, _, capacity, width = xs[0].shape
    count = weights.shape[1]
    rows = weights.shape[2]
    rd = inner_width // SHARDS
    grad_rows = 2 * LANES + 3 * rd + LANES

    def slot_spec(lanes, at):
        return pl.BlockSpec((micro, 1, capacity, lanes), lambda e: (0, at + e, 0, 0))

    slots = n * micro * capacity
    return pl.pallas_call(
        functools.partial(expert_kernel, n),
        grid=(count,),
        in_specs=[slot_spec(width, first)] * (2 * n)
        + [slot_spec(LANES, first)] * n
        + [
            pl.BlockSpec((SHARDS, 1, rows, LANES), lambda e: (0, e, 0, 0)),
            pl.BlockSpec(masks.shape, lambda e: (0, 0, 0)),
        ],
        out_specs=[slot_spec(width, 0)] * (2 * n)
        + [slot_spec(LANES, 0)] * n
        + [pl.BlockSpec((SHARDS, 1, grad_rows, LANES), lambda e: (0, e, 0, 0))],
        out_shape=[jax.ShapeDtypeStruct((micro, count, capacity, width), bf16)] * (2 * n)
        + [jax.ShapeDtypeStruct((micro, count, capacity, LANES), f32)] * n
        + [jax.ShapeDtypeStruct((SHARDS, count, grad_rows, LANES), bf16)],
        scratch_shapes=[
            pltpu.VMEM((width, 2 * inner_width), bf16),
            pltpu.VMEM((inner_width, width), bf16),
            pltpu.VMEM((width, 2 * LANES), bf16),
            pltpu.VMEM((2 * LANES, width), f32),
            pltpu.VMEM((LANES, inner_width), f32),
            pltpu.VMEM((LANES, inner_width), f32),
            pltpu.VMEM((LANES, inner_width), f32),
            pltpu.VMEM((LANES, width), f32),
        ],
        compiler_params=pltpu.CompilerParams(vmem_limit_bytes=VMEM),
        cost_estimate=pl.CostEstimate(
            flops=10 * 1000 * 1000 * slots * count,
            bytes_accessed=count * (8 * slots * width + 6 * rows * LANES * SHARDS),
            transcendentals=slots * count * inner_width,
        ),
        name="experts",
    )(*xs, *cs, *gs, weights, masks)


def combine_kernel(chunks, with_product, *refs):
    n = chunks
    row_refs = refs[:n]
    gg_refs = refs[n : 2 * n] if with_product else ()
    rank_ref = refs[2 * n if with_product else n]
    outs = refs[(2 * n if with_product else n) + 1 :]
    capacity, width = row_refs[0].shape[2:]
    total = None
    e = 0
    for c in range(n):
        hot = []
        here = row_refs[c].shape[1]
        for i in range(here):
            hits = hits_of(rank_ref[0, e : e + 1, :], capacity)
            hot.append(jnp.where(hits, 1.0, 0.0).astype(bf16))
            if with_product:
                outs[1][0, e : e + 1, :] = jnp.sum(
                    jnp.where(hits, gg_refs[c][0, i, :, :1], 0.0), axis=0, keepdims=True
                )
            e += 1
        term = tn(jnp.concatenate(hot, axis=0), row_refs[c][0].reshape(here * capacity, width))
        total = term if total is None else total + term
    outs[0][...] = total.astype(bf16)


def combine(rows, products, rank):
    micro, count, length = rank.shape
    capacity, width = rows[0].shape[2:]
    with_product = products is not None

    def chunk_spec(a):
        return pl.BlockSpec((1,) + a.shape[1:], lambda m: (m, 0, 0, 0))

    table = pl.BlockSpec((1, count, length), lambda m: (m, 0, 0))
    out_specs = [pl.BlockSpec((length, width), lambda m: (m, 0))]
    out_shape = [jax.ShapeDtypeStruct((micro * length, width), bf16)]
    operands = list(rows)
    if with_product:
        operands += list(products)
        out_specs.append(table)
        out_shape.append(jax.ShapeDtypeStruct((micro, count, length), f32))
    slots = micro * count * capacity
    return pl.pallas_call(
        functools.partial(combine_kernel, len(rows), with_product),
        grid=(micro,),
        in_specs=[chunk_spec(a) for a in operands] + [table],
        out_specs=out_specs,
        out_shape=out_shape,
        compiler_params=pltpu.CompilerParams(vmem_limit_bytes=VMEM),
        cost_estimate=pl.CostEstimate(
            flops=2 * slots * length * width, bytes_accessed=3 * slots * width, transcendentals=0
        ),
        name="combine",
    )(*operands, rank)


def exchange(a, k):
    if k == 0:
        return a
    size = lax.axis_size("dp")
    return lax.ppermute(a, "dp", [(i, i ^ k) for i in range(size)])


def local(
    layer_entering_state,
    exit_cotangent,
    attend_norm_scaling,
    branch_norm_scaling,
    triple_coefficients,
    attend_exit_coefficients,
    dispatch_coefficients,
    branch_widen_coefficients,
    branch_contract_coefficients,
    triple_plugin_source,
    asking_plugin_target,
    lookup_plugin_target,
    content_plugin_target,
    merge_plugin_source,
    merge_plugin_target,
    dispatch_plugin_source,
    dispatch_plugin_target,
    branch_plugin_source,
    branch_plugin_target,
    contract_plugin_source,
    contract_plugin_target,
    branch_choice_labels,
    plugin_choice_per_text,
    section_labels,
):
    dp_count = lax.axis_size("dp")
    shard_count = lax.axis_size("fsdp")
    dp_rank = lax.axis_index("dp")
    micro_count, seq_len = section_labels.shape
    local_experts = branch_widen_coefficients.shape[0]
    expert_count = local_experts * dp_count
    top_count = branch_choice_labels.shape[1]
    most = seq_len * top_count * 9 // (expert_count * 8)
    capacity = -(-most // 16) * 16
    model_width = layer_entering_state.shape[1]
    inner_width = contract_plugin_source.shape[1] * shard_count
    adapter_width = PLUGIN_CHOICES * REDUCED_DIM
    query_width = H * HD
    key_value_width = KVH * HD
    repeat = H // KVH
    score_scale = HD ** (-0.5)
    cos_table, sin_table = rotation(seq_len, HD)
    column_holder = jnp.arange(adapter_width, dtype=jnp.int32) // REDUCED_DIM
    peers = range(dp_count)

    ru = model_width // shard_count
    packed_parts = [
        (columns_to_rows(triple_coefficients), query_width // LANES + 2 * key_value_width // LANES),
        (columns_to_rows(attend_exit_coefficients), model_width // LANES),
        (columns_to_rows(triple_plugin_source), 3),
        (asking_plugin_target.T, 1),
        (lookup_plugin_target.T, 1),
        (content_plugin_target.T, 1),
        (merge_plugin_source, 1),
        (merge_plugin_target.T, 1),
        (dispatch_plugin_source, 1),
        (pad_lanes(dispatch_coefficients), 1),
        (pad_lanes(dispatch_plugin_target), 1),
        (pad_lanes(attend_norm_scaling[None]), 1),
        (pad_lanes(branch_norm_scaling[None]), 1),
    ]
    attn_packed = jnp.concatenate([a for a, _ in packed_parts], axis=0)
    attn_all = lax.all_gather(attn_packed, "fsdp", axis=0)
    full = []
    at = 0
    for a, blocks in packed_parts:
        full.append(rows_to_columns(attn_all[:, at : at + a.shape[0]], blocks))
        at += a.shape[0]
    (
        full_qkv,
        full_exit,
        full_qkv_in,
        q_out_t,
        k_out_t,
        v_out_t,
        full_merge_in,
        merge_out_t,
        full_route_in,
        route_padded,
        route_out_padded,
        gain_attn,
        gain_moe,
    ) = full
    full_route = route_padded[:, :expert_count]
    full_route_out = route_out_padded[:, :expert_count]
    attn_gain_f = gain_attn[:, :ru].reshape(model_width).astype(f32)
    moe_gain_f = gain_moe[:, :ru].reshape(model_width).astype(f32)

    chunk_weights = []
    first = 0
    for size in CHUNKS:
        here = slice(first, first + size)
        packed = pack_experts(
            branch_widen_coefficients[here],
            branch_contract_coefficients[here],
            branch_plugin_source[here],
            branch_plugin_target[here],
            contract_plugin_source[here],
            contract_plugin_target[here],
        )
        chunk_weights.append(
            regroup(lax.all_gather(packed, "fsdp", axis=0), model_width, inner_width)
        )
        first += size

    labels = branch_choice_labels.reshape(micro_count, seq_len, top_count)
    expert_range = jnp.arange(expert_count, dtype=jnp.int32)
    picked = labels[..., None] == expert_range
    chosen = jnp.any(picked, axis=2)
    before = jnp.tril(jnp.ones((seq_len, seq_len), bf16), -1)
    rank = jnp.einsum("mse,ts->met", chosen.astype(bf16), before, preferred_element_type=f32)
    chosen_t = jnp.swapaxes(chosen, 1, 2)
    rank = jnp.where(chosen_t, rank.astype(jnp.int32), -1)

    def of_group(a, k):
        return lax.dynamic_slice_in_dim(a, (dp_rank ^ k) * local_experts, local_experts, 1)

    rank_from = [exchange(of_group(rank, k), k) for k in peers]
    cot_from = [exchange(exit_cotangent, k) for k in peers]

    adapters = [plugin_choice_per_text[dp_rank ^ k] for k in peers]
    masks = jnp.stack(
        [(column_holder[None, :] == own[:, None]).astype(f32) for own in adapters]
    )

    saved = []
    for m in range(micro_count):
        rows_here = slice(m * seq_len, (m + 1) * seq_len)
        hidden_float = layer_entering_state[rows_here].astype(f32)
        block_rows = section_labels[m]
        mask = masks[0, m]
        mask3 = jnp.tile(mask, 3)
        normed_f, inverse_attn = norm_scale(hidden_float, attn_gain_f)
        normed = normed_f.astype(bf16)
        qkv_lora = (nn(normed, full_qkv_in) * mask3).astype(bf16)
        adapter_pieces = jnp.concatenate(
            [
                nt(qkv_lora[:, :adapter_width], q_out_t),
                nt(qkv_lora[:, adapter_width : 2 * adapter_width], k_out_t),
                nt(qkv_lora[:, 2 * adapter_width :], v_out_t),
            ],
            axis=1,
        )
        projected = nn(normed, full_qkv) + adapter_pieces
        queries = rotate(
            projected[:, :query_width].reshape(seq_len, H, HD), cos_table, sin_table
        ).astype(bf16)
        keys = rotate(
            projected[:, query_width : query_width + key_value_width].reshape(seq_len, KVH, HD),
            cos_table,
            sin_table,
        ).astype(bf16)
        values = projected[:, query_width + key_value_width :].reshape(seq_len, KVH, HD)
        values = values.astype(bf16)
        grouped = queries.reshape(seq_len, KVH, repeat, HD)
        allowed = block_rows[None, :] <= block_rows[:, None]
        raw = layered_times_effect("qnrd,knd->nrqk", grouped, keys) * score_scale
        scores = jnp.where(allowed, raw, -1e30)
        row_peak = jnp.max(scores, axis=-1, keepdims=True)
        shifted_exp = jnp.exp(scores - row_peak)
        row_total = jnp.sum(shifted_exp, axis=-1, keepdims=True)
        log_total = row_peak + jnp.log(row_total)
        probs_b = (shifted_exp / row_total).astype(bf16)
        attended = (
            layered_times_effect("nrqk,knd->qnrd", probs_b, values)
            .reshape(seq_len, query_width)
            .astype(bf16)
        )
        out_lora = (nn(attended, full_merge_in) * mask).astype(bf16)
        residual = hidden_float + nn(attended, full_exit) + nt(out_lora, merge_out_t)
        moe_f, inverse_moe = norm_scale(residual, moe_gain_f)
        moe_in = moe_f.astype(bf16)
        route_lora = (nn(moe_in, full_route_in) * mask).astype(bf16)
        logits = nn(moe_in, full_route) + nn(route_lora, full_route_out)
        shown = jnp.where(chosen[m], logits, -jnp.inf)
        weight = jnp.exp(shown - jnp.max(shown, axis=1, keepdims=True))
        gates = weight / jnp.sum(weight, axis=1, keepdims=True)
        saved.append(
            (normed, inverse_attn, qkv_lora, queries, keys, values, allowed, log_total, attended)
            + (out_lora, residual, inverse_moe, moe_in, route_lora, gates)
        )
    moe_rows = jnp.concatenate([s[12] for s in saved], axis=0)
    gates_t = jnp.stack([s[14].T for s in saved])

    gate_from = [exchange(of_group(gates_t, k), k) for k in peers]
    rows_from = [exchange(moe_rows, k) for k in peers]
    sent = [
        dispatch(rows_from[k], cot_from[k], rank_from[k], gate_from[k], capacity) for k in peers
    ]
    xs, cs, gs = [s[0] for s in sent], [s[1] for s in sent], [s[2] for s in sent]
    outs = []
    first = 0
    for size, weights in zip(CHUNKS, chunk_weights):
        outs.append(expert_chunk(xs, cs, gs, weights, masks, first, inner_width))
        first += size
    n = dp_count
    order = [3, 1, 2, 0] if n == 4 else list(peers)[::-1]
    grads_home, products_home, mixture_home = {}, {}, {}
    for k in order:
        back, product = combine([o[n + k] for o in outs], [o[2 * n + k] for o in outs], rank_from[k])
        products_home[k] = exchange(product, k)
        grads_home[k] = exchange(back, k)
    for k in order:
        (mix,) = combine([o[k] for o in outs], None, rank_from[k])
        mixture_home[k] = exchange(mix, k)

    adapter_sums = []
    for o in outs:
        g = o[3 * n]
        if shard_count == SHARDS:
            adapter_sums.append(lax.psum_scatter(g, "fsdp", scatter_dimension=0, tiled=False))
        else:
            adapter_sums.append(g)
    rd = inner_width // SHARDS
    wide_rows = 2 * LANES
    if shard_count == SHARDS:
        g = jnp.concatenate(adapter_sums, axis=0).astype(f32)
        cuts = [wide_rows + i * rd for i in range(4)]
        expert_reduce = jnp.swapaxes(g[:, :wide_rows], 1, 2)
        expert_expand = jnp.stack(
            [jnp.swapaxes(g[:, cuts[i] : cuts[i + 1]], 1, 2) for i in range(2)], axis=1
        )
        down_reduce = g[:, cuts[2] : cuts[3]]
        down_expand = g[:, cuts[3] :]
    else:
        g = jnp.concatenate(adapter_sums, axis=1).astype(f32)
        cuts = [wide_rows + i * rd for i in range(4)]

        def rows_joined(a):
            return jnp.swapaxes(a, 0, 1).reshape(a.shape[1], -1, LANES)

        wide = g[:, :, :wide_rows].transpose(1, 0, 3, 2).reshape(local_experts, -1, wide_rows)
        expand = jnp.stack(
            [jnp.swapaxes(rows_joined(g[:, :, cuts[i] : cuts[i + 1]]), 1, 2) for i in range(2)],
            axis=1,
        )
        deep = rows_joined(g[:, :, cuts[2] : cuts[3]])
        last = g[:, :, cuts[3] :].transpose(1, 2, 0, 3).reshape(local_experts, LANES, -1)
        expert_reduce = lax.psum_scatter(wide, "fsdp", scatter_dimension=1, tiled=True)
        expert_expand = lax.psum_scatter(expand, "fsdp", scatter_dimension=3, tiled=True)
        down_reduce = lax.psum_scatter(deep, "fsdp", scatter_dimension=1, tiled=True)
        down_expand = lax.psum_scatter(last, "fsdp", scatter_dimension=2, tiled=True)

    product_t = jnp.stack([products_home[k] for k in peers])
    product_t = jnp.take(product_t, dp_rank ^ jnp.arange(dp_count), axis=0)
    product_t = jnp.swapaxes(product_t, 0, 1).reshape(micro_count, expert_count, seq_len)
    weighted = gates_t * product_t
    select_t = weighted - gates_t * jnp.sum(weighted, axis=1, keepdims=True)
    logit_grads = jnp.swapaxes(select_t, 1, 2).astype(bf16)

    outputs, input_grads, grad_sums = [], [], None
    for m in range(micro_count):
        rows_here = slice(m * seq_len, (m + 1) * seq_len)
        (
            normed,
            inverse_attn,
            qkv_lora,
            queries,
            keys,
            values,
            allowed,
            log_total,
            attended,
            out_lora,
            residual,
            inverse_moe,
            moe_in,
            route_lora,
            gates,
        ) = saved[m]
        mask = masks[0, m]
        mask3 = jnp.tile(mask, 3)
        hidden_float = layer_entering_state[rows_here].astype(f32)
        grad_rows = exit_cotangent[rows_here].astype(f32)
        grouped = queries.reshape(seq_len, KVH, repeat, HD)
        mixture = sum(mixture_home[k][rows_here].astype(f32) for k in peers)
        outputs.append((residual + mixture).astype(bf16))
        logit_grad = logit_grads[m]
        route_lora_grad = (nt(logit_grad, full_route_out) * mask).astype(bf16)
        moe_grad = (
            sum(grads_home[k][rows_here].astype(f32) for k in peers)
            + nt(logit_grad, full_route)
            + nt(route_lora_grad, full_route_in)
        )
        residual_grad = grad_rows + norm_back(residual, inverse_moe, moe_gain_f, moe_grad)
        att_grad = residual_grad.astype(bf16)
        out_lora_grad = (nn(att_grad, merge_out_t) * mask).astype(bf16)
        attended_grad = (nt(att_grad, full_exit) + nt(out_lora_grad, full_merge_in)).astype(bf16)
        head_grad = attended_grad.reshape(seq_len, KVH, repeat, HD)
        raw = layered_times_effect("qnrd,knd->nrqk", grouped, keys) * score_scale
        probs = jnp.exp(jnp.where(allowed, raw, -1e30) - log_total)
        probs_b = probs.astype(bf16)
        prob_grad = layered_times_effect("qnrd,knd->nrqk", head_grad, values)
        score_grad = (
            probs * (prob_grad - jnp.sum(probs * prob_grad, axis=-1, keepdims=True))
        ).astype(bf16)
        query_grad = (
            layered_times_effect("nrqk,knd->qnrd", score_grad, keys).reshape(seq_len, H, HD)
            * score_scale
        )
        key_grad = layered_times_effect("nrqk,qnrd->knd", score_grad, grouped) * score_scale
        value_grad = layered_times_effect("nrqk,qnrd->knd", probs_b, head_grad)
        proj_grad = jnp.concatenate(
            [
                rotate_back(query_grad, cos_table, sin_table).reshape(seq_len, query_width),
                rotate_back(key_grad, cos_table, sin_table).reshape(seq_len, key_value_width),
                value_grad.reshape(seq_len, key_value_width),
            ],
            axis=1,
        ).astype(bf16)
        q_grad = proj_grad[:, :query_width]
        k_grad = proj_grad[:, query_width : query_width + key_value_width]
        v_grad = proj_grad[:, query_width + key_value_width :]
        qkv_lora_grad = (
            jnp.concatenate([nn(q_grad, q_out_t), nn(k_grad, k_out_t), nn(v_grad, v_out_t)], axis=1)
            * mask3
        ).astype(bf16)
        normed_grad = nt(proj_grad, full_qkv) + nt(qkv_lora_grad, full_qkv_in)
        input_grads.append(
            (
                residual_grad + norm_back(hidden_float, inverse_attn, attn_gain_f, normed_grad)
            ).astype(bf16)
        )
        terms = (
            tn(normed, qkv_lora_grad),
            tn(qkv_lora[:, :adapter_width], q_grad),
            tn(k_grad, qkv_lora[:, adapter_width : 2 * adapter_width]),
            tn(v_grad, qkv_lora[:, 2 * adapter_width :]),
            tn(attended, out_lora_grad),
            tn(out_lora, att_grad),
            tn(moe_in, route_lora_grad),
            tn(route_lora, logit_grad),
        )
        grad_sums = terms if grad_sums is None else tuple(a + b for a, b in zip(grad_sums, terms))

    def by_rows(a):
        return columns_to_rows(a.reshape(shard_count, -1, a.shape[1]))

    def by_columns(a):
        part = a.reshape(a.shape[0], shard_count, -1).transpose(1, 0, 2)
        return jnp.pad(part, ((0, 0), (0, 0), (0, LANES - part.shape[2])))

    sizes = [3 * ru, adapter_width, key_value_width // shard_count, key_value_width // shard_count]
    sizes += [ru, adapter_width, ru, adapter_width // shard_count]
    to_sum = jnp.concatenate(
        [
            by_rows(grad_sums[0]),
            by_columns(grad_sums[1]),
            by_rows(grad_sums[2]),
            by_rows(grad_sums[3]),
            by_rows(grad_sums[4]),
            by_columns(grad_sums[5]),
            by_rows(grad_sums[6]),
            by_rows(pad_lanes(grad_sums[7])),
        ],
        axis=1,
    ).astype(bf16)
    shard_sum = lax.psum_scatter(to_sum, "fsdp", scatter_dimension=0, tiled=False)
    total = sum(exchange(shard_sum, k).astype(f32) for k in peers)
    pieces, at = [], 0
    for size in sizes:
        pieces.append(total[at : at + size])
        at += size
    query_cols = query_width // shard_count
    return (
        jnp.concatenate(outputs, axis=0),
        jnp.concatenate(input_grads, axis=0),
        pieces[0].reshape(3, ru, LANES).transpose(1, 0, 2).reshape(ru, 3 * LANES),
        pieces[1][:, :query_cols],
        pieces[2].T,
        pieces[3].T,
        pieces[4],
        pieces[5][:, :ru],
        pieces[6],
        pieces[7][:, :expert_count],
        expert_reduce,
        expert_expand,
        down_reduce,
        down_expand,
    )


def solution(mesh):
    placed = (
        P(("dp", "fsdp"), None),
        P(("dp", "fsdp"), None),
        P("fsdp"),
        P("fsdp"),
        P("fsdp", None),
        P("fsdp", None),
        P("fsdp", None),
        P("dp", "fsdp", None),
        P("dp", "fsdp", None),
        P("fsdp", None),
        P(None, "fsdp"),
        P(None, "fsdp"),
        P(None, "fsdp"),
        P("fsdp", None),
        P(None, "fsdp"),
        P("fsdp", None),
        P("fsdp", None),
        P("dp", "fsdp", None),
        P("dp", None, None, "fsdp"),
        P("dp", "fsdp", None),
        P("dp", None, "fsdp"),
        P(("dp", "fsdp"), None),
        P(None, "fsdp"),
        P(("dp", "fsdp"), None),
    )
    return jax.shard_map(
        local,
        mesh=mesh,
        in_specs=placed,
        out_specs=(
            P(("dp", "fsdp"), None),
            P(("dp", "fsdp"), None),
            P("fsdp", None),
            P(None, "fsdp"),
            P(None, "fsdp"),
            P(None, "fsdp"),
            P("fsdp", None),
            P(None, "fsdp"),
            P("fsdp", None),
            P("fsdp", None),
            P("dp", "fsdp", None),
            P("dp", None, None, "fsdp"),
            P("dp", "fsdp", None),
            P("dp", None, "fsdp"),
        ),
        check_vma=False,
    )
```

```python
import functools

import jax
import jax.numpy as jnp
from jax import lax
from jax.experimental import pallas as pl
from jax.experimental.pallas import tpu as pltpu
from jax.sharding import PartitionSpec as P

H = 16
KVH = 8
HD = 64
FEEDFORWARD_SIZE = 512
PLUGIN_CHOICES = 8
REDUCED_DIM = 16

eps_norm = 1e-06
rope_base = 10000.0

LANES = 128
SHARDS = 8
CHUNKS = (4, 2, 2)
EXTRA = 16
VMEM = 60 * 1024 * 1024

f32 = jnp.float32
bf16 = jnp.bfloat16


def nn(a, b):
    return lax.dot_general(a, b, (((1,), (0,)), ((), ())), preferred_element_type=f32)


def nt(a, b):
    return lax.dot_general(a, b, (((1,), (1,)), ((), ())), preferred_element_type=f32)


def tn(a, b):
    return lax.dot_general(a, b, (((0,), (0,)), ((), ())), preferred_element_type=f32)


def rotation(length):
    half_size = HD // 2
    frequency = rope_base ** (-(2.0 * jnp.arange(half_size, dtype=f32)) / HD)
    angles = jnp.arange(length, dtype=f32)[:, None] * frequency[None, :]
    return tuple(jnp.tile(f(angles), (1, LANES // half_size)) for f in (jnp.cos, jnp.sin))


def columns_to_rows(a):
    r, c = a.shape[-2:]
    b = c // LANES
    a = a.reshape(a.shape[:-1] + (b, LANES))
    return jnp.swapaxes(a, -3, -2).reshape(a.shape[:-3] + (b * r, LANES))


def pad_lanes(a):
    return jnp.pad(a, ((0, 0), (0, LANES - a.shape[-1])))


def pack_experts(widen, contract, up_source, up_target, down_source, down_target):
    count = widen.shape[0]
    return jnp.concatenate(
        [
            columns_to_rows(widen),
            columns_to_rows(contract),
            columns_to_rows(up_source),
            jnp.swapaxes(up_target, 2, 3).reshape(count, -1, LANES),
            down_source,
            jnp.swapaxes(down_target, 1, 2),
        ],
        axis=1,
    )


def regroup(gathered, width, inner):
    n, count = gathered.shape[:2]
    if n == SHARDS:
        return gathered
    per = n // SHARDS
    pieces, at = [], 0
    ru, rd = width // n, inner // n
    blocks = ((width // LANES, ru), (width // LANES, rd), (2, ru), (2, rd), (1, rd), (1, ru))
    for b, r in blocks:
        piece = gathered[:, :, at : at + b * r].reshape(SHARDS, per, count, b, r, LANES)
        at += b * r
        pieces.append(piece.transpose(0, 2, 3, 1, 4, 5).reshape(SHARDS, count, b * per * r, LANES))
    return jnp.concatenate(pieces, axis=2)


def hits_of(rank_row, capacity):
    rows = lax.broadcasted_iota(jnp.int32, (capacity, rank_row.shape[1]), 0)
    return rows == rank_row.astype(jnp.int32)


def pieces_of(value):
    high = value.astype(bf16).astype(f32)
    rest = value - high
    middle = rest.astype(bf16).astype(f32)
    return [high, middle, rest - middle]


def put_extra(ref, rows, length, value):
    spare = 2 * EXTRA - value.shape[0]
    if spare:
        value = jnp.concatenate([value, jnp.zeros((spare, length), f32)], axis=0)
    value = value.astype(bf16)
    for i in range(2):
        ref[rows : rows + EXTRA, i * length : (i + 1) * length] = value[i * EXTRA : (i + 1) * EXTRA]
    ref[rows : rows + EXTRA, 2 * length :] = jnp.zeros((EXTRA, ref.shape[1] - 2 * length), bf16)


def get_extra(ref, rows, length):
    return jnp.concatenate(
        [ref[rows : rows + EXTRA, i * length : (i + 1) * length] for i in range(2)], axis=0
    ).astype(f32)


def dispatch_kernel(peers, capacity, *refs):
    x_refs, cots = refs[:peers], refs[peers : 2 * peers]
    xs_ref, cs_ref, gs_ref, rank_ref = refs[2 * peers :]
    count, _, width = xs_ref.shape[1:]
    length = cots[0].shape[0]
    shape = xs_ref.shape[1:]
    for i in range(peers):

        @pl.when(pl.program_id(0) == i)
        def _():
            table = get_extra(x_refs[i], length, length)
            rank_ref[0] = table[:count]
            gates = table[count : 2 * count] + table[2 * count : 3 * count] + table[3 * count :]
            hot = []
            for e in range(count):
                hits = hits_of(table[e : e + 1], capacity)
                hot.append(jnp.where(hits, 1.0, 0.0).astype(bf16))
                gate = jnp.sum(jnp.where(hits, gates[e : e + 1], 0.0), axis=1, keepdims=True)
                gs_ref[0, e] = jnp.broadcast_to(gate, (capacity, LANES))
            hot = jnp.concatenate(hot, axis=0)
            xs_ref[0] = nn(hot, x_refs[i][:length]).astype(bf16).reshape(shape)
            cs_ref[0] = nn(hot, cots[i][...]).astype(bf16).reshape(shape)


def dispatch(rows, cots, count, capacity):
    peers = len(rows)
    length, width = cots[0].shape

    def out_spec(lanes):
        return pl.BlockSpec((1, count, capacity, lanes), lambda k: (k, 0, 0, 0))

    def shaped(lanes, dtype):
        return jax.ShapeDtypeStruct((peers, count, capacity, lanes), dtype)

    slots = peers * count * capacity
    return pl.pallas_call(
        functools.partial(dispatch_kernel, peers, capacity),
        grid=(peers,),
        in_specs=[pl.BlockSpec(a.shape, lambda k: (0, 0)) for a in (*rows, *cots)],
        out_specs=[
            out_spec(width),
            out_spec(width),
            out_spec(LANES),
            pl.BlockSpec((1, count, length), lambda k: (k, 0, 0)),
        ],
        out_shape=[
            shaped(width, bf16),
            shaped(width, bf16),
            shaped(LANES, f32),
            jax.ShapeDtypeStruct((peers, count, length), f32),
        ],
        compiler_params=pltpu.CompilerParams(vmem_limit_bytes=VMEM),
        cost_estimate=pl.CostEstimate(
            flops=4 * slots * length * width, bytes_accessed=8 * slots * width, transcendentals=0
        ),
        name="dispatch",
    )(*rows, *cots)


def expert_kernel(first, micro, held, add, final, *refs):
    tables, x_refs, c_refs, g_refs = (refs[i * micro : (i + 1) * micro] for i in range(4))
    w_ref, mask_ref = refs[4 * micro : 4 * micro + 2]
    n, _, capacity, width = x_refs[0].shape
    at = 4 * micro + 2
    old_products = refs[at : at + held]
    old_grads = refs[at + held]
    outs = refs[at + held + 1 :]
    y_refs, m_refs = outs[:n], outs[n : 2 * n]
    grad_ref = outs[2 * n]
    prod_refs = outs[2 * n + 1 : 2 * n + 1 + micro]
    wide, deep, source, sums_a, sums_b, sums_c, sums_d, sums_e = outs[2 * n + 1 + micro :]
    expert = pl.program_id(0)
    if held:

        @pl.when(expert == 0)
        def _():
            for old, new in zip(old_products, prod_refs):
                new[...] = old[...]

    inner_width = deep.shape[0]
    ru, rd = width // SHARDS, inner_width // SHARDS
    blocks = width // LANES
    at = 0

    def part(rows):
        nonlocal at
        value = w_ref[:, 0, at : at + rows, :].reshape(SHARDS * rows, LANES)
        at += rows
        return value

    for j in range(blocks):
        wide[:, j * LANES : (j + 1) * LANES] = part(ru)
    for j in range(blocks):
        deep[:, j * LANES : (j + 1) * LANES] = part(rd)
    for j in range(2):
        source[:, j * LANES : (j + 1) * LANES] = part(ru)
    target_gate, target_up = part(rd), part(rd)
    down_source = part(rd)
    down_target = part(ru)

    size = n * capacity
    for m in range(micro):
        x = x_refs[m][:, 0].reshape(size, width)
        cot = c_refs[m][:, 0].reshape(size, width)
        gate_of_slot = g_refs[m][:, 0].reshape(size, LANES)[:, :1]
        mask = jnp.concatenate(
            [jnp.broadcast_to(mask_ref[m, k : k + 1, :], (capacity, LANES)) for k in range(n)],
            axis=0,
        )
        mask2 = jnp.concatenate([mask, mask], axis=1)
        lora = (nn(x, source[...]) * mask2).astype(bf16)
        gate_up = nn(x, wide[...])
        gate = gate_up[:, :inner_width] + nt(lora[:, :LANES], target_gate)
        up = gate_up[:, inner_width:] + nt(lora[:, LANES:], target_up)
        sig = jax.nn.sigmoid(gate)
        silu = gate * sig
        inner = (silu * up).astype(bf16)
        down_lora = (nn(inner, down_source) * mask).astype(bf16)
        rows = (nn(inner, deep[...]) + nt(down_lora, down_target)).astype(bf16)
        rows_f = rows.astype(f32)
        cot_f = cot.astype(f32)
        product = jnp.sum(rows_f * cot_f, axis=1, keepdims=True)
        weighted = (rows_f * gate_of_slot).astype(bf16)
        row_grad = (cot_f * gate_of_slot).astype(bf16)
        down_lora_grad = (nn(row_grad, down_target) * mask).astype(bf16)
        inner_grad = nt(row_grad, deep[...]) + nt(down_lora_grad, down_source)
        gate_grad = (inner_grad * up * (sig * (1.0 + gate * (1.0 - sig)))).astype(bf16)
        up_grad = (inner_grad * silu).astype(bf16)
        lora_grad = (
            jnp.concatenate([nn(gate_grad, target_gate), nn(up_grad, target_up)], axis=1) * mask2
        ).astype(bf16)
        back = (
            nt(gate_grad, wide[:, :inner_width])
            + nt(up_grad, wide[:, inner_width:])
            + nt(lora_grad, source[...])
        ).astype(bf16)
        for k in range(n):
            here = slice(k * capacity, (k + 1) * capacity)
            y_refs[k][m, 0] = weighted[here]
            if final:
                place = pl.ds(pl.multiple_of(expert * capacity, EXTRA), capacity)
                m_refs[k][place, :] = back[here]
            else:
                m_refs[k][m, 0] = back[here]
            hits = hits_of(tables[m][k, pl.ds(first + expert, 1), :], capacity)
            prod_refs[m][k, pl.ds(first + expert, 1), :] = jnp.sum(
                jnp.where(hits, product[here], 0.0), axis=0, keepdims=True
            )
        terms = (
            tn(lora_grad, x),
            tn(lora[:, :LANES], gate_grad),
            tn(lora[:, LANES:], up_grad),
            tn(down_lora_grad, inner),
            tn(down_lora, row_grad),
        )
        for ref, term in zip((sums_a, sums_b, sums_c, sums_d, sums_e), terms):
            ref[...] = term if m == 0 else ref[...] + term
    if final:

        @pl.when(expert == pl.num_programs(0) - 1)
        def _():
            for k in range(n):
                rows = m_refs[k].shape[0] - EXTRA
                value = jnp.concatenate(pieces_of(prod_refs[0][k]), axis=0)
                put_extra(m_refs[k], rows, value.shape[1], value)

    def put(place, value):
        if add:
            value = value + old_grads[place].astype(f32)
        grad_ref[place] = value.astype(bf16)

    for s in range(SHARDS):
        put((s, 0, slice(0, 2 * LANES)), sums_a[:, s * ru : (s + 1) * ru])
    out = 2 * LANES
    for ref in (sums_b, sums_c, sums_d):
        put((slice(None), 0, slice(out, out + rd)), ref[...].T.reshape(SHARDS, rd, LANES))
        out += rd
    for s in range(SHARDS):
        put((s, 0, slice(out, out + LANES)), sums_e[:, s * ru : (s + 1) * ru])


def expert_chunk(
    slots, weights, masks, first, inner_width, grad_at, grad_count, grads, products, add, final
):
    micro = len(slots)
    tables = [t[3] for t in slots]
    n, local_count, capacity, width = slots[0][0].shape
    count, rows = weights.shape[1:3]
    rd = inner_width // SHARDS
    grad_rows = 2 * LANES + 3 * rd + LANES
    prod_shape = (n, local_count, tables[0].shape[2])

    def slot_spec(lanes):
        return pl.BlockSpec((n, 1, capacity, lanes), lambda e: (0, first + e, 0, 0))

    out_spec = pl.BlockSpec((micro, 1, capacity, width), lambda e: (0, e, 0, 0))
    out_shape = jax.ShapeDtypeStruct((micro, count, capacity, width), bf16)
    back_spec, back_shape = out_spec, out_shape
    if final:
        back_shape = jax.ShapeDtypeStruct((count * capacity + EXTRA, width), bf16)
        back_spec = pl.BlockSpec(back_shape.shape, lambda e: (0, 0))
    grad_spec = pl.BlockSpec((SHARDS, 1, grad_rows, LANES), lambda e: (0, grad_at + e, 0, 0))
    prod_spec = pl.BlockSpec(prod_shape, lambda e: (0, 0, 0))
    work = n * micro * capacity * count
    held = products or []
    kept = jnp.zeros((8, LANES), f32) if grads is None else grads
    return pl.pallas_call(
        functools.partial(expert_kernel, first, micro, len(held), add, final),
        grid=(count,),
        in_specs=[pl.BlockSpec(tables[0].shape, lambda e: (0, 0, 0))] * micro
        + [slot_spec(width)] * (2 * micro)
        + [slot_spec(LANES)] * micro
        + [
            pl.BlockSpec((SHARDS, 1, rows, LANES), lambda e: (0, e, 0, 0)),
            pl.BlockSpec(masks.shape, lambda e: (0, 0, 0)),
        ]
        + [prod_spec] * len(held)
        + [grad_spec if add else pl.BlockSpec(memory_space=pl.ANY)],
        out_specs=[out_spec] * n + [back_spec] * n + [grad_spec] + [prod_spec] * micro,
        out_shape=[out_shape] * n
        + [back_shape] * n
        + [jax.ShapeDtypeStruct((SHARDS, grad_count, grad_rows, LANES), bf16)]
        + [jax.ShapeDtypeStruct(prod_shape, f32)] * micro,
        scratch_shapes=[
            pltpu.VMEM((width, 2 * inner_width), bf16),
            pltpu.VMEM((inner_width, width), bf16),
            pltpu.VMEM((width, 2 * LANES), bf16),
            pltpu.VMEM((2 * LANES, width), f32),
            pltpu.VMEM((LANES, inner_width), f32),
            pltpu.VMEM((LANES, inner_width), f32),
            pltpu.VMEM((LANES, inner_width), f32),
            pltpu.VMEM((LANES, width), f32),
        ],
        compiler_params=pltpu.CompilerParams(vmem_limit_bytes=VMEM),
        cost_estimate=pl.CostEstimate(
            flops=10 * 1000 * 1000 * work,
            bytes_accessed=8 * work * width + 6 * count * rows * LANES * SHARDS,
            transcendentals=work * inner_width,
        ),
        input_output_aliases={} if grads is None else {2 + 4 * micro + len(held): 2 * n},
        name="experts",
    )(
        *tables, *[t[0] for t in slots], *[t[1] for t in slots], *[t[2] for t in slots],
        weights, masks, *held, kept,
    )


def combine_kernel(peer, chunks, micro, added, *refs):
    tables, row_refs = refs[:micro], refs[micro : micro + chunks]
    outs = refs[micro + chunks + (added is not None) :]
    capacity, width = row_refs[0].shape[2:]
    length = tables[0].shape[2]
    for m in range(micro):
        total = None
        e = 0
        for ref in row_refs:
            hot = []
            here = ref.shape[1]
            for i in range(here):
                hits = hits_of(tables[m][peer, e : e + 1, :], capacity)
                hot.append(jnp.where(hits, 1.0, 0.0).astype(bf16))
                e += 1
            term = tn(jnp.concatenate(hot, axis=0), ref[m].reshape(here * capacity, width))
            total = term if total is None else total + term
        if added == m:
            total = total + refs[micro + chunks][...].astype(f32)
        if len(outs) > 1:
            outs[m][...] = total.astype(bf16)
        else:
            outs[0][m * length : (m + 1) * length, :] = total.astype(bf16)


def combine(slots, rows, peer, apart=False, added=None, add=None):
    tables = [t[3] for t in slots]
    micro, length = len(tables), tables[0].shape[2]
    capacity, width = rows[0].shape[2:]
    work = micro * sum(a.shape[1] for a in rows) * capacity
    whole = pl.BlockSpec(memory_space=pltpu.VMEM)
    shapes = [(length, width)] * micro if apart else [(micro * length, width)]
    operands = [*tables, *rows] + ([] if add is None else [add])
    out = pl.pallas_call(
        functools.partial(combine_kernel, peer, len(rows), micro, added),
        in_specs=[whole] * len(operands),
        out_specs=[whole] * len(shapes),
        out_shape=[jax.ShapeDtypeStruct(shape, bf16) for shape in shapes],
        compiler_params=pltpu.CompilerParams(vmem_limit_bytes=VMEM),
        cost_estimate=pl.CostEstimate(
            flops=2 * work * length * width, bytes_accessed=3 * work * width, transcendentals=0
        ),
        name="combine",
    )(*operands)
    return out if apart else out[0]


GROUP = 4
HALF = HD // 2
SPAN = GROUP * HD
REPEAT = H // KVH
NGROUPS = KVH // GROUP


def query_order():
    return [
        (g * GROUP + n) * REPEAT + r
        for g in range(NGROUPS)
        for r in range(REPEAT)
        for n in range(GROUP)
    ]


def halves_order(heads_in_group):
    return [
        heads[n] * 2 + t for heads in heads_in_group for t in range(2) for n in range(GROUP)
    ]


def query_halves():
    order = query_order()
    return halves_order([order[i : i + GROUP] for i in range(0, H, GROUP)])


def key_halves():
    return halves_order([list(range(g * GROUP, (g + 1) * GROUP)) for g in range(NGROUPS)])


def take_rows(a, order, size):
    return jnp.concatenate([a[o * size : (o + 1) * size] for o in order], axis=0)


def put_rows(a, order, size):
    inverse = sorted(range(len(order)), key=lambda i: order[i])
    return take_rows(a, inverse, size)


def lay_out_columns(a):
    rows = a.shape[0]
    q = a[:, : H * HD].reshape(rows, NGROUPS, GROUP, REPEAT, 2, HALF)
    k = a[:, H * HD : (H + KVH) * HD].reshape(rows, NGROUPS, GROUP, 2, HALF)
    q = q.transpose(0, 1, 3, 4, 2, 5).reshape(rows, H * HD)
    k = k.transpose(0, 1, 3, 2, 4).reshape(rows, KVH * HD)
    return jnp.concatenate([q, k, a[:, (H + KVH) * HD :]], axis=1)


def rope(a, cos, sin, sign):
    out = []
    for at in range(0, a.shape[1], SPAN):
        lead, trail = a[:, at : at + LANES], a[:, at + LANES : at + SPAN]
        out.append(lead * cos - sign * (trail * sin))
        out.append(trail * cos + sign * (lead * sin))
    return jnp.concatenate(out, axis=1)


def lanes_like(a):
    return lax.broadcasted_iota(jnp.int32, a.shape, 1)


def key_of(a, n):
    return jnp.where((lanes_like(a) % LANES) // HALF == n, a, jnp.zeros_like(a))


def value_of(a, n):
    return jnp.where(lanes_like(a) // HD == n, a, jnp.zeros_like(a))


def unpack_kernel(peers, me_ref, *refs):
    own, near, far = refs[0], refs[1:peers], refs[peers : 2 * peers - 1]
    qkv_ref, exit_ref, other_ref = refs[2 * peers - 1 :]
    width = qkv_ref.shape[0]
    shards = own.shape[0]
    ru, half = width // shards, width // 2
    a, b = qkv_ref.shape[1] // LANES // peers, exit_ref.shape[1] // LANES // peers
    c = other_ref.shape[0] // peers
    order = [n * REPEAT + r for r in range(REPEAT) for n in range(GROUP)]

    def place(part, h, q):
        def block(j):
            return part[:, j * ru : (j + 1) * ru, :].reshape(half, LANES)

        rows = pl.ds(pl.multiple_of(h * half, half), half)
        for j in range(a):
            columns = pl.ds(pl.multiple_of((q * a + j) * LANES, LANES), LANES)
            qkv_ref[rows, columns] = block(j)
        for j in range(b):
            columns = pl.ds(pl.multiple_of((q * b + j) * LANES, LANES), LANES)
            exit_ref[rows, columns] = take_rows(block(a + j), order, HD)
        for j in range(c):
            other_ref[q * c + j, rows, :] = block(a + b + j)

    me, core = me_ref[0], me_ref[1]
    for h in range(2):
        place(own.at[h * shards // 2 : (h + 1) * shards // 2], h, me)
    for k in range(1, peers):
        place(near[k - 1], core, me ^ k)
        place(far[k - 1], 1 - core, me ^ k)


def unpack(me, own, near, far, width, qkv_width, others):
    whole = pl.BlockSpec(memory_space=pltpu.VMEM)
    packed = [own, *near, *far]
    return pl.pallas_call(
        functools.partial(unpack_kernel, len(near) + 1),
        in_specs=[pl.BlockSpec(memory_space=pltpu.SMEM)] + [whole] * len(packed),
        out_specs=[whole] * 3,
        out_shape=[
            jax.ShapeDtypeStruct((width, qkv_width), bf16),
            jax.ShapeDtypeStruct((width, width), bf16),
            jax.ShapeDtypeStruct((others, width, LANES), bf16),
        ],
        compiler_params=pltpu.CompilerParams(vmem_limit_bytes=VMEM),
        name="unpack",
    )(me, *packed)


def scale_rows(values):
    return lax.rsqrt(jnp.mean(values * values, axis=-1, keepdims=True) + eps_norm)


def attn_forward_kernel(
    me_ref, x_ref, chosen_ref, rank_ref, row_ref, col_ref, mask_ref, cos_ref, sin_ref, qkv_ref,
    exit_ref, oth_ref, kout_ref, vout_ref, rout_ref, gain_ref,
    res_ref, q_ref, k_ref, v_ref, lse_ref, att_ref, lora_ref, olora_ref, rlora_ref, gate_ref,
    *sent_refs,
):
    length, width = x_ref.shape
    qw, kw = H * HD, KVH * HD
    mask = mask_ref[0]
    cos, sin = cos_ref[...], sin_ref[...]
    hidden = x_ref[...].astype(f32)
    normed = (hidden * scale_rows(hidden) * gain_ref[0:1, :]).astype(bf16)
    lora = [(nn(normed, oth_ref[i]) * mask).astype(bf16) for i in range(3)]
    for i in range(3):
        lora_ref[:, i * LANES : (i + 1) * LANES] = lora[i]
    q_out = take_rows(oth_ref[3], query_halves(), HALF)
    k_out = take_rows(kout_ref[...], key_halves(), HALF)
    q = nn(normed, qkv_ref[:, :qw]) + nt(lora[0], q_out)
    q_ref[...] = (rope(q, cos, sin, 1.0) * HD ** (-0.5)).astype(bf16)
    k = nn(normed, qkv_ref[:, qw : qw + kw]) + nt(lora[1], k_out)
    k_ref[...] = rope(k, cos, sin, 1.0).astype(bf16)
    v_ref[...] = (nn(normed, qkv_ref[:, qw + kw :]) + nt(lora[2], vout_ref[...])).astype(bf16)
    shut = jnp.where(row_ref[0] <= col_ref[0], 0.0, -1e30)
    lane = lax.broadcasted_iota(jnp.int32, (length, LANES), 1)
    logs = jnp.zeros((length, LANES), f32)
    for g in range(NGROUPS):
        kg = k_ref[:, g * SPAN : (g + 1) * SPAN]
        vg = v_ref[:, g * SPAN : (g + 1) * SPAN]
        totals = [None] * REPEAT
        for n in range(GROUP):
            kn, vn = key_of(kg, n), value_of(vg, n)
            for r in range(REPEAT):
                at = g * REPEAT + r
                s = nt(q_ref[:, at * SPAN : (at + 1) * SPAN], kn) + shut
                peak = jnp.max(s, axis=-1, keepdims=True)
                p = jnp.exp(s - peak)
                total = jnp.sum(p, axis=-1, keepdims=True)
                logs = jnp.where(lane == at * GROUP + n, peak + jnp.log(total), logs)
                probs = (p * (1.0 / total)).astype(bf16)
                term = nn(probs, vn)
                totals[r] = term if n == 0 else totals[r] + term
        for r in range(REPEAT):
            at = g * REPEAT + r
            att_ref[:, at * SPAN : (at + 1) * SPAN] = totals[r].astype(bf16)
    lse_ref[...] = logs
    att = att_ref[...]
    merge_in = take_rows(oth_ref[5], query_order(), HD)
    out_lora = (nn(att, merge_in) * mask).astype(bf16)
    olora_ref[...] = out_lora
    residual = hidden + nn(att, exit_ref[...]) + nt(out_lora, oth_ref[6])
    res_ref[...] = residual
    moe = (residual * scale_rows(residual) * gain_ref[1:2, :]).astype(bf16)
    for ref in sent_refs:
        ref[:length] = moe
    route_lora = (nn(moe, oth_ref[7]) * mask).astype(bf16)
    rlora_ref[...] = route_lora
    logits = nn(moe, oth_ref[8]) + nn(route_lora, rout_ref[...])
    shown = jnp.where(chosen_ref[...] > 0, logits, -1e30)
    weight = jnp.where(
        chosen_ref[...] > 0, jnp.exp(shown - jnp.max(shown, axis=1, keepdims=True)), 0.0
    )
    gates = weight / jnp.sum(weight, axis=1, keepdims=True)
    gate_ref[0] = gates.T[: gate_ref.shape[1]]
    own = gate_ref.shape[1] // len(sent_refs)
    for k, ref in enumerate(sent_refs):
        group = pl.ds(pl.multiple_of((me_ref[0] ^ k) * own, own), own)
        value = jnp.concatenate(
            [rank_ref[0, group, :], *pieces_of(gate_ref[0, group, :])], axis=0
        )
        put_extra(ref, length, length, value)


def attn_forward(step, me, hidden, chosen, rank, rows, cols, mask, cos, sin, weights, peers):
    _, experts, length = rank.shape
    width = hidden.shape[1]

    def by_row(a):
        return pl.BlockSpec((length, a.shape[1]), lambda i: (step, 0))

    def by_step(a):
        return pl.BlockSpec((1,) + a.shape[1:], lambda i: (step,) + (0,) * (a.ndim - 1))

    def whole(a):
        return pl.BlockSpec(a.shape, lambda i: (0,) * a.ndim)

    qw, kw = H * HD, KVH * HD
    shapes = [
        ((length, width), f32), ((length, qw), bf16), ((length, kw), bf16), ((length, kw), bf16),
         ((length, LANES), f32), ((length, qw), bf16), ((length, 3 * LANES), bf16),
        ((length, LANES), bf16), ((length, LANES), bf16), ((1, experts, length), f32),
    ] + [((length + EXTRA, width), bf16)] * peers
    shapes = [jax.ShapeDtypeStruct(*shape) for shape in shapes]
    return pl.pallas_call(
        attn_forward_kernel,
        grid=(1,),
        in_specs=[pl.BlockSpec(memory_space=pltpu.SMEM), by_row(hidden), by_row(chosen)]
        + [by_step(a) for a in (rank, rows, cols, mask)]
        + [whole(a) for a in (cos, sin, *weights)],
        out_specs=[whole(a) for a in shapes],
        out_shape=shapes,
        compiler_params=pltpu.CompilerParams(vmem_limit_bytes=VMEM),
        cost_estimate=pl.CostEstimate(
            flops=2 * length * (5 * width * width + 4 * H * HD * length),
            bytes_accessed=20 * width * width,
            transcendentals=H * length * length,
        ),
        name="attention_forward",
    )(me, hidden, chosen, rank, rows, cols, mask, cos, sin, *weights)


def last_hits(rank_ref, count, capacity):
    return [hits_of(rank_ref[0, i : i + 1, :], capacity) for i in range(count)]


def attn_backward_kernel(
    peers, last, parts, older, me_ref, x_ref, cot_ref, row_ref, col_ref, mask_ref, cos_ref, sin_ref,
    qkv_ref, exit_ref, oth_ref, kout_ref, vout_ref, rout_ref, gain_ref,
    res_ref, q_ref, k_ref, v_ref, lse_ref, att_ref, lora_ref, olora_ref, rlora_ref, gate_ref, moe_ref,
    rank_ref, *refs,
):
    part_refs, tail_refs = refs[:parts], refs[parts : parts + peers]
    at = parts + peers
    old_grads = refs[at : at + older]
    out_ref, grad_ref, product_ref, dq_ref, dk_ref, dv_ref = refs[at + 2 * older :]
    length, width = x_ref.shape
    experts = gate_ref.shape[1]
    own = experts // peers
    capacity = (tail_refs[0].shape[0] - EXTRA) // last
    qw, kw = H * HD, KVH * HD
    mask = mask_ref[0]
    cos, sin = cos_ref[...], sin_ref[...]

    hits = last_hits(rank_ref, peers * last, capacity)
    hot = jnp.concatenate([jnp.where(h, 1.0, 0.0).astype(bf16) for h in hits], axis=0)
    tails = jnp.concatenate([ref[: last * capacity] for ref in tail_refs], axis=0)
    upstream = tn(hot, tails)
    for ref in part_refs:
        upstream = upstream + ref[...].astype(f32)
    for k in range(peers):
        group = pl.ds(pl.multiple_of((me_ref[0] ^ k) * own, own), own)
        value = get_extra(tail_refs[k], last * capacity, length)
        product_ref[group, :] = value[:own] + value[own : 2 * own] + value[2 * own : 3 * own]
    product = product_ref[...]
    gates = gate_ref[0]
    weighted = gates * product
    select = weighted - gates * jnp.sum(weighted, axis=0, keepdims=True)
    select = jnp.concatenate([select, jnp.zeros((LANES - experts, length), f32)], axis=0)
    logit_grad = select.T.astype(bf16)

    route_lora_grad = (nt(logit_grad, rout_ref[...]) * mask).astype(bf16)
    upstream = upstream + nt(logit_grad, oth_ref[8]) + nt(route_lora_grad, oth_ref[7])
    residual = res_ref[...]
    scale = scale_rows(residual)
    scaled = gain_ref[1:2, :] * upstream
    inner = jnp.sum(residual * scaled, axis=-1, keepdims=True) * (1.0 / width)
    res_grad = cot_ref[...].astype(f32) + scale * scaled - residual * (scale * scale * scale * inner)
    att_grad = res_grad.astype(bf16)
    merge_out = oth_ref[6]
    merge_in = take_rows(oth_ref[5], query_order(), HD)
    out_lora_grad = (nn(att_grad, merge_out) * mask).astype(bf16)
    head_grad = (nt(att_grad, exit_ref[...]) + nt(out_lora_grad, merge_in)).astype(bf16)

    shut = jnp.where(row_ref[0] <= col_ref[0], 0.0, -1e30)
    logs = lse_ref[...]
    for g in range(NGROUPS):
        kg = k_ref[:, g * SPAN : (g + 1) * SPAN]
        vg = v_ref[:, g * SPAN : (g + 1) * SPAN]
        dq = [None] * REPEAT
        qs = [q_ref[:, (g * REPEAT + r) * SPAN : (g * REPEAT + r + 1) * SPAN] for r in range(REPEAT)]
        dos = [
            head_grad[:, (g * REPEAT + r) * SPAN : (g * REPEAT + r + 1) * SPAN]
            for r in range(REPEAT)
        ]
        qts = [a.T for a in qs]
        dots = [a.T for a in dos]
        lead, trail, dvs = [], [], []
        for n in range(GROUP):
            kn, vn = key_of(kg, n), value_of(vg, n)
            dk, dv = None, None
            for r in range(REPEAT):
                at = (g * REPEAT + r) * GROUP + n
                s = nt(qs[r], kn) + (shut - logs[:, at : at + 1])
                p = jnp.exp(s)
                dp = nt(dos[r], vn)
                weight = p * dp
                ds = (weight - p * jnp.sum(weight, axis=-1, keepdims=True)).astype(bf16)
                term = nn(ds, kn)
                dq[r] = term if n == 0 else dq[r] + term
                qt = jnp.concatenate(
                    [
                        qts[r][n * HALF : (n + 1) * HALF],
                        qts[r][LANES + n * HALF : LANES + (n + 1) * HALF],
                    ],
                    axis=0,
                )
                term = nn(qt, ds)
                dk = term if r == 0 else dk + term
                term = nn(dots[r][n * HD : (n + 1) * HD], p.astype(bf16))
                dv = term if r == 0 else dv + term
            lead.append(dk[:HALF])
            trail.append(dk[HALF:])
            dvs.append(dv)
        for r in range(REPEAT):
            at = g * REPEAT + r
            back = rope(dq[r] * HD ** (-0.5), cos, sin, -1.0)
            dq_ref[:, at * SPAN : (at + 1) * SPAN] = back.astype(bf16)
        dk = jnp.concatenate(lead + trail, axis=0).T
        dk_ref[:, g * SPAN : (g + 1) * SPAN] = rope(dk, cos, sin, -1.0).astype(bf16)
        dv_ref[:, g * SPAN : (g + 1) * SPAN] = jnp.concatenate(dvs, axis=0).T.astype(bf16)

    dq, dk, dv = dq_ref[...], dk_ref[...], dv_ref[...]
    q_out = take_rows(oth_ref[3], query_halves(), HALF)
    k_out = take_rows(kout_ref[...], key_halves(), HALF)
    lora_grads = [
        (nn(dq, q_out) * mask).astype(bf16),
        (nn(dk, k_out) * mask).astype(bf16),
        (nn(dv, vout_ref[...]) * mask).astype(bf16),
    ]
    back = (
        nt(dq, qkv_ref[:, :qw]) + nt(dk, qkv_ref[:, qw : qw + kw]) + nt(dv, qkv_ref[:, qw + kw :])
    )
    for i in range(3):
        back = back + nt(lora_grads[i], oth_ref[i])
    hidden = x_ref[...].astype(f32)
    scale = scale_rows(hidden)
    normed = (hidden * scale * gain_ref[0:1, :]).astype(bf16)
    scaled = gain_ref[0:1, :] * back
    inner = jnp.sum(hidden * scaled, axis=-1, keepdims=True) * (1.0 / width)
    out_ref[...] = (
        res_grad + scale * scaled - hidden * (scale * scale * scale * inner)
    ).astype(bf16)

    lora = [lora_ref[:, i * LANES : (i + 1) * LANES] for i in range(3)]
    terms = (
        tn(jnp.concatenate(lora_grads, axis=1), normed),
        tn(lora[0], dq),
        tn(lora[1], dk),
        tn(lora[2], dv),
        tn(out_lora_grad, att_ref[...]),
        tn(olora_ref[...], att_grad),
        tn(route_lora_grad, moe_ref[...]),
        tn(rlora_ref[...], logit_grad),
    )
    ru = width // SHARDS

    def put(place, value):
        if older:
            value = value + old_grads[0][place].astype(f32)
        grad_ref[place] = value.astype(bf16)

    def put_columns(at, value):
        for s in range(SHARDS):
            put((s, slice(at, at + value.shape[0])), value[:, s * ru : (s + 1) * ru])

    def put_rows_at(at, value):
        size = value.shape[0] // SHARDS
        put((slice(None), slice(at, at + size)), value.reshape(SHARDS, size, LANES))

    at = 0
    sizes = attn_grad_rows(width)
    turned = {
        1: lambda a: put_rows(a.T, query_halves(), HALF),
        2: lambda a: put_rows(a.T, key_halves(), HALF),
        3: lambda a: a.T,
        4: lambda a: put_rows(a.T, query_order(), HD),
        7: lambda a: a,
    }
    for i, (size, term) in enumerate(zip(sizes, terms)):
        if i in turned:
            put_rows_at(at, turned[i](term))
        else:
            put_columns(at, term)
        at += size


def attn_grad_rows(width):
    ru, qs, ks = width // SHARDS, H * HD // SHARDS, KVH * HD // SHARDS
    return (3 * LANES, qs, ks, ks, qs, LANES, LANES, LANES // SHARDS)


def attn_backward(
    step, last, me, hidden, cotangent, rows, cols, mask, cos, sin, weights, saved, moe, rank, parts, tails, older
):
    length = rows.shape[2]
    width = hidden.shape[1]
    peers = len(tails)
    experts = saved[-1].shape[1]
    grads = jax.ShapeDtypeStruct((SHARDS, sum(attn_grad_rows(width)), LANES), bf16)

    def by_row(a):
        return pl.BlockSpec((length, a.shape[1]), lambda i: (step, 0))

    def by_step(a):
        return pl.BlockSpec((1,) + a.shape[1:], lambda i: (step,) + (0,) * (a.ndim - 1))

    def whole(a):
        return pl.BlockSpec(a.shape, lambda i: (0,) * a.ndim)

    qw, kw = H * HD, KVH * HD
    ahead = 8 + len(weights) + len(saved) + 2 + len(parts) + peers
    return pl.pallas_call(
        functools.partial(attn_backward_kernel, peers, last, len(parts), len(older) // 2),
        grid=(1,),
        in_specs=[pl.BlockSpec(memory_space=pltpu.SMEM), by_row(hidden), by_row(cotangent)]
        + [by_step(a) for a in (rows, cols, mask)]
        + [whole(a) for a in (cos, sin, *weights, *saved)]
        + [pl.BlockSpec((length, width), lambda i: (0, 0)), by_step(rank)]
        + [by_row(a) for a in parts]
        + [whole(a) for a in tails]
        + ([whole(older[0]), pl.BlockSpec(memory_space=pl.ANY)] if older else []),
        out_specs=[by_row(hidden), whole(grads)],
        out_shape=[jax.ShapeDtypeStruct(hidden.shape, bf16), grads],
        scratch_shapes=[
            pltpu.VMEM((experts, length), f32),
            pltpu.VMEM((length, qw), bf16),
            pltpu.VMEM((length, kw), bf16),
            pltpu.VMEM((length, kw), bf16),
        ],
        compiler_params=pltpu.CompilerParams(vmem_limit_bytes=VMEM),
        cost_estimate=pl.CostEstimate(
            flops=2 * length * (6 * width * width + 10 * H * HD * length),
            bytes_accessed=30 * width * width,
            transcendentals=H * length * length,
        ),
        input_output_aliases={ahead + 1: 0} if older else {},
        name="attention_backward",
    )(
        me, hidden, cotangent, rows, cols, mask, cos, sin, *weights, *saved, moe, rank, *parts, *tails, *older
    )


def mixture_kernel(peers, count, last, res_ref, rank_ref, *refs):
    parts, tails, out_ref = refs[:count], refs[count : count + peers], refs[-1]
    capacity, width = tails[0].shape[2:]
    hits = last_hits(rank_ref, peers * last, capacity)
    hot = jnp.concatenate([jnp.where(h, 1.0, 0.0).astype(bf16) for h in hits], axis=0)
    rows = jnp.concatenate([ref[0].reshape(last * capacity, width) for ref in tails], axis=0)
    total = tn(hot, rows)
    for ref in parts:
        total = total + ref[...].astype(f32)
    out_ref[...] = (res_ref[...] + total).astype(bf16)


def add_mixture(step, residual, rank, parts, tails, older):
    length = rank.shape[2]
    width = residual.shape[1]

    def by_row(a):
        return pl.BlockSpec((length, a.shape[1]), lambda i: (step, 0))

    def by_step(a):
        return pl.BlockSpec((1,) + a.shape[1:], lambda i: (step,) + (0,) * (a.ndim - 1))

    def whole(a):
        return pl.BlockSpec(a.shape, lambda i: (0,) * a.ndim)

    return pl.pallas_call(
        functools.partial(mixture_kernel, len(tails), len(parts), tails[0].shape[1]),
        grid=(1,),
        in_specs=[whole(residual), by_step(rank)]
        + [by_row(a) for a in parts]
        + [whole(a) for a in tails]
        + [pl.BlockSpec(memory_space=pl.ANY)] * len(older),
        out_specs=by_row(parts[0]),
        out_shape=jax.ShapeDtypeStruct(parts[0].shape, bf16),
        compiler_params=pltpu.CompilerParams(vmem_limit_bytes=VMEM),
        cost_estimate=pl.CostEstimate(
            flops=2 * length * 1000 * width, bytes_accessed=20 * length * width, transcendentals=0
        ),
        input_output_aliases={2 + len(parts) + len(tails): 0} if older else {},
        name="mixture",
    )(residual, rank, *parts, *tails, *older)


def finish_experts_kernel(chunks, *refs):
    parts = refs[:chunks]
    reduce_ref, expand_ref, deep_ref, last_ref = refs[chunks:]
    wide = reduce_ref.shape[2]
    rd = deep_ref.shape[1]
    e = 0
    for ref in parts:
        for i in range(ref.shape[0]):
            g = ref[i].astype(f32)
            reduce_ref[e] = g[:wide].T
            for j in range(2):
                expand_ref[e, j] = g[wide + j * rd : wide + (j + 1) * rd].T
            deep_ref[e] = g[wide + 2 * rd : wide + 3 * rd]
            last_ref[e] = g[wide + 3 * rd :]
            e += 1


def finish_experts(parts, width, inner_width):
    count = sum(a.shape[0] for a in parts)
    ru, rd = width // SHARDS, inner_width // SHARDS
    whole = pl.BlockSpec(memory_space=pltpu.VMEM)
    return pl.pallas_call(
        functools.partial(finish_experts_kernel, len(parts)),
        in_specs=[whole] * len(parts),
        out_specs=[whole] * 4,
        out_shape=[
            jax.ShapeDtypeStruct((count, ru, 2 * LANES), f32),
            jax.ShapeDtypeStruct((count, 2, LANES, rd), f32),
            jax.ShapeDtypeStruct((count, rd, LANES), f32),
            jax.ShapeDtypeStruct((count, LANES, ru), f32),
        ],
        compiler_params=pltpu.CompilerParams(vmem_limit_bytes=VMEM),
        name="finish_experts",
    )(*parts)


def finish_attention_kernel(sizes, peers, *refs):
    parts, outs = refs[:peers], refs[peers:]
    total = parts[0][...].astype(f32)
    for ref in parts[1:]:
        total = total + ref[...].astype(f32)
    at = 0
    for i, (size, ref) in enumerate(zip(sizes, outs)):
        piece = total[at : at + size]
        at += size
        if i in (0, 1, 2, 3, 6):
            ref[...] = piece.T
        else:
            ref[...] = piece[:, : ref.shape[1]]


def finish_attention(parts, sizes, experts):
    shapes = [
        (LANES, sizes[0]), (LANES, sizes[1]), (LANES, sizes[2]), (LANES, sizes[3]),
        (sizes[4], LANES), (sizes[5], LANES), (LANES, sizes[6]), (sizes[7], experts),
    ]
    whole = pl.BlockSpec(memory_space=pltpu.VMEM)
    return pl.pallas_call(
        functools.partial(finish_attention_kernel, sizes, len(parts)),
        in_specs=[whole] * len(parts),
        out_specs=[whole] * len(shapes),
        out_shape=[jax.ShapeDtypeStruct(s, f32) for s in shapes],
        compiler_params=pltpu.CompilerParams(vmem_limit_bytes=VMEM),
        name="finish_attention",
    )(*parts)


def exchange(a, k):
    if k == 0:
        return a
    size = lax.axis_size("dp")
    return lax.ppermute(a, "dp", [(i, i ^ k) for i in range(size)])


def local(
    layer_entering_state,
    exit_cotangent,
    attend_norm_scaling,
    branch_norm_scaling,
    triple_coefficients,
    attend_exit_coefficients,
    dispatch_coefficients,
    branch_widen_coefficients,
    branch_contract_coefficients,
    triple_plugin_source,
    asking_plugin_target,
    lookup_plugin_target,
    content_plugin_target,
    merge_plugin_source,
    merge_plugin_target,
    dispatch_plugin_source,
    dispatch_plugin_target,
    branch_plugin_source,
    branch_plugin_target,
    contract_plugin_source,
    contract_plugin_target,
    branch_choice_labels,
    plugin_choice_per_text,
    section_labels,
):
    dp_count = lax.axis_size("dp")
    shard_count = lax.axis_size("fsdp")
    dp_rank = lax.axis_index("dp")
    micro_count, seq_len = section_labels.shape
    local_experts = branch_widen_coefficients.shape[0]
    expert_count = local_experts * dp_count
    top_count = branch_choice_labels.shape[1]
    most = seq_len * top_count * 9 // (expert_count * 8)
    capacity = -(-most // 16) * 16
    model_width = layer_entering_state.shape[1]
    inner_width = contract_plugin_source.shape[1] * shard_count
    adapter_width = PLUGIN_CHOICES * REDUCED_DIM
    cos_table, sin_table = rotation(seq_len)
    column_holder = jnp.arange(adapter_width, dtype=jnp.int32) // REDUCED_DIM
    peers = range(dp_count)
    last = CHUNKS[-1]
    core = lax.axis_index("fsdp") % 2
    me = jnp.stack([dp_rank, core]).astype(jnp.int32)
    cot_rows = [exit_cotangent[m * seq_len : (m + 1) * seq_len] for m in range(micro_count)]
    cot_from = [[exchange(cot_rows[0], k)] for k in peers]

    labels = branch_choice_labels.reshape(micro_count, seq_len, top_count)
    lane_range = jnp.arange(LANES, dtype=jnp.int32)
    chosen = jnp.any(labels[..., None] == lane_range, axis=2)
    before = jnp.tril(jnp.ones((seq_len, seq_len), bf16), -1)
    chosen_e = chosen[..., :expert_count]
    rank = jnp.einsum("mse,ts->met", chosen_e.astype(bf16), before, preferred_element_type=f32)
    rank = jnp.where(jnp.swapaxes(chosen_e, 1, 2), rank, -1.0)
    chosen = chosen.astype(f32).reshape(micro_count * seq_len, LANES)

    def of_group(a, k):
        return lax.dynamic_slice_in_dim(a, (dp_rank ^ k) * local_experts, local_experts, 1)

    rank_last = jnp.concatenate([of_group(rank, k)[:, -last:] for k in peers], axis=1)
    adapters = [plugin_choice_per_text[dp_rank ^ k] for k in peers]
    masks = jnp.stack(
        [(column_holder[None, :] == own[:, None]).astype(f32) for own in adapters], axis=1
    )
    own_mask = masks[:, :1]
    section_rows = section_labels[:, None, :]
    section_cols = section_labels[:, :, None]

    ru = model_width // shard_count
    kv_cols = lookup_plugin_target.shape[1]
    route_rows = dispatch_plugin_target.shape[0]
    small = jnp.concatenate(
        [
            pad_lanes(dispatch_plugin_target),
            pad_lanes(attend_norm_scaling[None]),
            pad_lanes(branch_norm_scaling[None]),
        ],
        axis=0,
    )
    small = jnp.pad(small, ((0, ru - small.shape[0]), (0, 0)))
    others = jnp.concatenate(
        [
            columns_to_rows(triple_plugin_source),
            asking_plugin_target.T,
            lookup_plugin_target.T,
            content_plugin_target.T,
            merge_plugin_source,
            merge_plugin_target.T,
            dispatch_plugin_source,
            pad_lanes(dispatch_coefficients),
            small,
        ],
        axis=0,
    )
    other_count = others.shape[0] // ru
    other_slots = -(-other_count // dp_count) * dp_count
    others = jnp.pad(others, ((0, (other_slots - other_count) * ru), (0, 0)))

    def own_part(a, axis):
        size = a.shape[axis] // dp_count
        return lax.dynamic_slice_in_dim(a, dp_rank * size, size, axis)

    part = jnp.concatenate(
        [
            columns_to_rows(own_part(lay_out_columns(triple_coefficients), 1)),
            columns_to_rows(own_part(attend_exit_coefficients, 1)),
            own_part(others, 0),
        ],
        axis=0,
    )
    part_all = lax.all_gather(part, "fsdp", axis=0)
    (part_all, cot_from, rank, chosen, masks, own_mask, section_cols, cos_table, sin_table) = (
        lax.optimization_barrier(
            (part_all, cot_from, rank, chosen, masks, own_mask, section_cols, cos_table, sin_table)
        )
    )
    mine = lax.dynamic_slice_in_dim(part_all, core * (shard_count // 2), shard_count // 2, 0)
    near = [exchange(mine, k) for k in peers[1:]]
    pairs = [(i, i ^ 1) for i in range(shard_count)]
    far = [lax.ppermute(a, "fsdp", pairs) for a in near]

    chunk_weights = []
    first = 0
    before_it = part
    for size in CHUNKS:
        here = slice(first, first + size)
        shards = (
            branch_widen_coefficients[here],
            branch_contract_coefficients[here],
            branch_plugin_source[here],
            branch_plugin_target[here],
            contract_plugin_source[here],
            contract_plugin_target[here],
        )
        if first:
            shards, cot_from = lax.optimization_barrier((shards, cot_from))
        shards, before_it = lax.optimization_barrier((shards, before_it))
        before_it = pack_experts(*shards)
        gathered = lax.all_gather(before_it, "fsdp", axis=0)
        chunk_weights.append(regroup(gathered, model_width, inner_width))
        first += size

    later, near = lax.optimization_barrier((cot_rows[1:], near))
    for k in peers:
        cot_from[k] += [exchange(a, k) for a in later]

    qkv, exit_full, other_full = unpack(
        me, part_all, near, far, model_width, triple_coefficients.shape[1], other_slots
    )
    kv_out = other_full[4].reshape(shard_count, 2, kv_cols, LANES)
    k_out = kv_out[:, 0].reshape(-1, LANES)
    v_out = kv_out[:, 1].reshape(-1, LANES)
    small_full = other_full[9].reshape(shard_count, ru, LANES)
    route_out = small_full[:, :route_rows].reshape(adapter_width, LANES)
    gains = jnp.stack(
        [small_full[:, route_rows + i, :ru].reshape(model_width) for i in range(2)]
    ).astype(f32)
    weights = (qkv, exit_full, other_full, k_out, v_out, route_out, gains)

    micro = range(micro_count)
    saved, sent, slots = [], [], []
    me_then = me
    for m in micro:
        if m > 0:
            me_then, sent[-1] = lax.optimization_barrier((me_then, sent[-1]))
        out = attn_forward(
            m, me_then, layer_entering_state, chosen, rank, section_rows, section_cols, own_mask,
            cos_table, sin_table, weights, dp_count,
        )
        saved.append(out[:-dp_count])
        sent.append(list(out[-dp_count:]))
    first_rows, cot_from = lax.optimization_barrier((sent[0], cot_from))
    sent[0] = first_rows
    rows_from = None
    for m in micro:
        if m > 0:
            sent[m], rows_from = lax.optimization_barrier((sent[m], rows_from))
        rows_from = [exchange(sent[m][k], k) for k in peers]
        cots = [cot_from[k][m] for k in peers]
        slots.append(dispatch(rows_from, cots, local_experts, capacity))

    n = dp_count
    head = CHUNKS[0]
    outs, first, grads, products = [], 0, None, None
    for size, chunk in zip(CHUNKS[:-1], chunk_weights):
        at = first if first < head else first - head
        count = head if first < head else local_experts - head
        outs.append(
            expert_chunk(
                slots, chunk, masks, first, inner_width, at, count, grads, products, False, False
            )
        )
        grads, products = outs[-1][2 * n], list(outs[-1][2 * n + 1 :])
        if first == 0:
            head_grads, grads = grads, None
        first += size
    if shard_count == SHARDS:
        head_sum = lax.psum_scatter(head_grads, "fsdp", scatter_dimension=0, tiled=False)
    else:
        head_sum = head_grads

    def rows_of(place):
        return [o[place] for o in outs]

    far_backs = combine(slots, rows_of(n + 3), 3, apart=True)
    passed = [exchange(far_backs[0], 1), exchange(far_backs[1], 2)]
    far_mixes = combine(slots, rows_of(3), 3, apart=True)
    far_mixes, passed = lax.optimization_barrier((far_mixes, passed))
    backs = {
        1: combine(slots, rows_of(n + 1), 1, added=1, add=passed[1]),
        2: combine(slots, rows_of(n + 2), 2, added=0, add=passed[0]),
    }
    passed_mixes = [exchange(far_mixes[0], 1), exchange(far_mixes[1], 2)]
    backs[0] = combine(slots, rows_of(n), 0)
    back_home = [backs[0], exchange(backs[1], 1), exchange(backs[2], 2)]
    mixes = {
        0: combine(slots, rows_of(0), 0),
        1: combine(slots, rows_of(1), 1, added=1, add=passed_mixes[1]),
        2: combine(slots, rows_of(2), 2, added=0, add=passed_mixes[0]),
    }
    chunk, _ = lax.optimization_barrier((chunk_weights[-1], (backs, mixes)))
    tails = []
    for m in micro:
        if m == micro_count - 1:
            chunk, back_home = lax.optimization_barrier((chunk, back_home))
        out = expert_chunk(
            [slots[m]], chunk, masks[m : m + 1], first, inner_width, first - head,
            local_experts - head, grads, [products[m]], m > 0, True,
        )
        grads = out[2 * n]
        tails.append(out)
    back_last = []
    for m in micro:
        tail = list(tails[m][n : 2 * n])
        if m == 0:
            tail, back_home = lax.optimization_barrier((tail, back_home))
        else:
            tail, back_last[-1] = lax.optimization_barrier((tail, back_last[-1]))
        back_last.append([exchange(tail[k], k) for k in peers])
    grads, back_last[0] = lax.optimization_barrier((grads, back_last[0]))
    if shard_count == SHARDS:
        tail_sum = lax.psum_scatter(grads, "fsdp", scatter_dimension=0, tiled=False)
    else:
        tail_sum = grads
    older = []
    for m in micro:
        if m == micro_count - 1:
            mixes, mix_tails, back_last[m], head_sum, older = lax.optimization_barrier(
                (mixes, [list(t[:n]) for t in tails], back_last[m], head_sum, older)
            )
        grad_input, attn_grads = attn_backward(
            m, last, me, layer_entering_state, exit_cotangent, section_rows, section_cols, own_mask,
            cos_table, sin_table, weights, saved[m], sent[m][0], rank_last, back_home, back_last[m],
            older,
        )
        older = [attn_grads, grad_input]
    mix_home = [mixes[0], exchange(mixes[1], 1), exchange(mixes[2], 2)]
    mix_last = [[exchange(t[k], k) for k in peers] for t in mix_tails]
    attn_grads, mix_home, tail_sum = lax.optimization_barrier((attn_grads, mix_home, tail_sum))
    block_out = []
    for m in micro:
        block_out = [add_mixture(m, saved[m][0], rank_last, mix_home, mix_last[m], block_out)]

    sizes = attn_grad_rows(model_width)
    if shard_count == SHARDS:
        expert_out = finish_experts([head_sum, tail_sum], model_width, inner_width)
        own_sum = lax.psum_scatter(attn_grads, "fsdp", scatter_dimension=0, tiled=False)
        attn_out = finish_attention([exchange(own_sum, k) for k in peers], sizes, expert_count)
    else:
        expert_out = scatter_experts([head_sum, tail_sum], inner_width)
        attn_out = scatter_attention(attn_grads, sizes, expert_count)
    return (*block_out, grad_input, *attn_out, *expert_out)


def scatter_experts(parts, inner_width):
    g = jnp.concatenate(parts, axis=1).astype(f32)
    count, rd, wide = g.shape[1], inner_width // SHARDS, 2 * LANES
    cuts = [wide + i * rd for i in range(4)]

    def rows_joined(a):
        return jnp.swapaxes(a, 0, 1).reshape(a.shape[1], -1, LANES)

    reduce = g[:, :, :wide].transpose(1, 0, 3, 2).reshape(count, -1, wide)
    expand = jnp.stack(
        [jnp.swapaxes(rows_joined(g[:, :, cuts[i] : cuts[i + 1]]), 1, 2) for i in range(2)],
        axis=1,
    )
    deep = rows_joined(g[:, :, cuts[2] : cuts[3]])
    last = g[:, :, cuts[3] :].transpose(1, 2, 0, 3).reshape(count, LANES, -1)
    return (
        lax.psum_scatter(reduce, "fsdp", scatter_dimension=1, tiled=True),
        lax.psum_scatter(expand, "fsdp", scatter_dimension=3, tiled=True),
        lax.psum_scatter(deep, "fsdp", scatter_dimension=1, tiled=True),
        lax.psum_scatter(last, "fsdp", scatter_dimension=2, tiled=True),
    )


def scatter_attention(packed, sizes, experts):
    pieces, at = [], 0
    for size in sizes:
        pieces.append(packed[:, at : at + size].astype(f32))
        at += size

    def by_rows(a):
        return a.reshape(-1, LANES)

    def by_columns(a):
        return jnp.swapaxes(a, 0, 1).reshape(a.shape[1], -1)

    full = (
        (by_columns(pieces[0]).T, 0),
        (by_rows(pieces[1]).T, 1),
        (by_rows(pieces[2]).T, 1),
        (by_rows(pieces[3]).T, 1),
        (by_rows(pieces[4]), 0),
        (by_columns(pieces[5]), 1),
        (by_columns(pieces[6]).T, 0),
        (by_rows(pieces[7])[:, :experts], 0),
    )
    return [
        lax.psum(lax.psum_scatter(a, "fsdp", scatter_dimension=d, tiled=True), "dp")
        for a, d in full
    ]


def solution(mesh):
    placed = (
        P(("dp", "fsdp"), None),
        P(("dp", "fsdp"), None),
        P("fsdp"),
        P("fsdp"),
        P("fsdp", None),
        P("fsdp", None),
        P("fsdp", None),
        P("dp", "fsdp", None),
        P("dp", "fsdp", None),
        P("fsdp", None),
        P(None, "fsdp"),
        P(None, "fsdp"),
        P(None, "fsdp"),
        P("fsdp", None),
        P(None, "fsdp"),
        P("fsdp", None),
        P("fsdp", None),
        P("dp", "fsdp", None),
        P("dp", None, None, "fsdp"),
        P("dp", "fsdp", None),
        P("dp", None, "fsdp"),
        P(("dp", "fsdp"), None),
        P(None, "fsdp"),
        P(("dp", "fsdp"), None),
    )
    return jax.shard_map(
        local,
        mesh=mesh,
        in_specs=placed,
        out_specs=(
            P(("dp", "fsdp"), None),
            P(("dp", "fsdp"), None),
            P("fsdp", None),
            P(None, "fsdp"),
            P(None, "fsdp"),
            P(None, "fsdp"),
            P("fsdp", None),
            P(None, "fsdp"),
            P("fsdp", None),
            P("fsdp", None),
            P("dp", "fsdp", None),
            P("dp", None, None, "fsdp"),
            P("dp", "fsdp", None),
            P("dp", None, "fsdp"),
        ),
        check_vma=False,
    )
```

```python
import functools

import jax
import jax.numpy as jnp
import numpy as np
from jax import lax
from jax.experimental import pallas as pl
from jax.experimental.pallas import tpu as pltpu
from jax.sharding import PartitionSpec as P

H = 16
KVH = 8
HD = 64
FEEDFORWARD_SIZE = 512
PLUGIN_CHOICES = 8
REDUCED_DIM = 16

eps_norm = 1e-06
rope_base = 10000.0

LANES = 128
SHARDS = 8
CHUNKS = (4, 2, 2)
EXTRA = 16
VMEM = 60 * 1024 * 1024

f32 = jnp.float32
bf16 = jnp.bfloat16


def nn(a, b):
    return lax.dot_general(a, b, (((1,), (0,)), ((), ())), preferred_element_type=f32)


def nt(a, b):
    return lax.dot_general(a, b, (((1,), (1,)), ((), ())), preferred_element_type=f32)


def tn(a, b):
    return lax.dot_general(a, b, (((0,), (0,)), ((), ())), preferred_element_type=f32)


def rotation(length):
    half_size = HD // 2
    frequency = rope_base ** (-2.0 * np.arange(half_size) / HD)
    angles = np.arange(length)[:, None] * frequency[None, :]
    return tuple(
        jnp.asarray(np.tile(f(angles), (1, LANES // half_size)), f32) for f in (np.cos, np.sin)
    )


def columns_to_rows(a):
    r, c = a.shape[-2:]
    b = c // LANES
    a = a.reshape(a.shape[:-1] + (b, LANES))
    return jnp.swapaxes(a, -3, -2).reshape(a.shape[:-3] + (b * r, LANES))


def pad_lanes(a):
    return jnp.pad(a, ((0, 0), (0, LANES - a.shape[-1])))


def pack_experts(widen, contract, up_source, up_target, down_source, down_target):
    count = widen.shape[0]
    return jnp.concatenate(
        [
            columns_to_rows(widen),
            columns_to_rows(contract),
            columns_to_rows(up_source),
            jnp.swapaxes(up_target, 2, 3).reshape(count, -1, LANES),
            down_source,
            jnp.swapaxes(down_target, 1, 2),
        ],
        axis=1,
    )


def regroup(gathered, width, inner):
    n, count = gathered.shape[:2]
    if n == SHARDS:
        return gathered
    per = n // SHARDS
    pieces, at = [], 0
    ru, rd = width // n, inner // n
    blocks = ((width // LANES, ru), (width // LANES, rd), (2, ru), (2, rd), (1, rd), (1, ru))
    for b, r in blocks:
        piece = gathered[:, :, at : at + b * r].reshape(SHARDS, per, count, b, r, LANES)
        at += b * r
        pieces.append(piece.transpose(0, 2, 3, 1, 4, 5).reshape(SHARDS, count, b * per * r, LANES))
    return jnp.concatenate(pieces, axis=2)


def hits_of(rank_row, capacity):
    rows = lax.broadcasted_iota(jnp.int32, (capacity, rank_row.shape[1]), 0)
    return rows == rank_row.astype(jnp.int32)


def pieces_of(value):
    high = value.astype(bf16).astype(f32)
    rest = value - high
    middle = rest.astype(bf16).astype(f32)
    return [high, middle, rest - middle]


def put_extra(ref, rows, length, value):
    spare = 2 * EXTRA - value.shape[0]
    if spare:
        value = jnp.concatenate([value, jnp.zeros((spare, length), f32)], axis=0)
    value = value.astype(bf16)
    for i in range(2):
        ref[rows : rows + EXTRA, i * length : (i + 1) * length] = value[i * EXTRA : (i + 1) * EXTRA]
    ref[rows : rows + EXTRA, 2 * length :] = jnp.zeros((EXTRA, ref.shape[1] - 2 * length), bf16)


def get_extra(ref, rows, length):
    return jnp.concatenate(
        [ref[rows : rows + EXTRA, i * length : (i + 1) * length] for i in range(2)], axis=0
    ).astype(f32)


def dispatch_kernel(peers, capacity, *refs):
    x_refs, cots = refs[: peers + 1], refs[peers + 1 : 2 * peers + 1]
    xs_ref, cs_ref, gs_ref, rank_ref, column_ref = refs[2 * peers + 1 :]
    count, _, width = xs_ref.shape[1:]
    length = cots[0].shape[0]
    shape = xs_ref.shape[1:]
    for i in range(peers):

        @pl.when(pl.program_id(0) == i)
        def _():
            if i < peers - 1:
                table = get_extra(x_refs[i], EXTRA + length, length)
                x = x_refs[i][EXTRA : EXTRA + length]
            else:
                table = get_extra(x_refs[i], 0, length)
                x = jnp.concatenate([x_refs[i][EXTRA:], x_refs[i + 1][...]], axis=0)
            rank_ref[0] = table[:count]
            spare = jnp.zeros((LANES - count, length), f32)
            column_ref[0] = jnp.concatenate([table[:count], spare], axis=0).T
            gates = table[count : 2 * count] + table[2 * count : 3 * count] + table[3 * count :]
            hot = []
            for e in range(count):
                hits = hits_of(table[e : e + 1], capacity)
                hot.append(jnp.where(hits, 1.0, 0.0).astype(bf16))
                gate = jnp.sum(jnp.where(hits, gates[e : e + 1], 0.0), axis=1, keepdims=True)
                gs_ref[0, e] = jnp.broadcast_to(gate, (capacity, LANES))
            hot = jnp.concatenate(hot, axis=0)
            xs_ref[0] = nn(hot, x).astype(bf16).reshape(shape)
            cs_ref[0] = nn(hot, cots[i][...]).astype(bf16).reshape(shape)


def dispatch(rows, cots, count, capacity):
    peers = len(cots)
    length, width = cots[0].shape

    def out_spec(lanes):
        return pl.BlockSpec((1, count, capacity, lanes), lambda k: (k, 0, 0, 0))

    def shaped(lanes, dtype):
        return jax.ShapeDtypeStruct((peers, count, capacity, lanes), dtype)

    slots = peers * count * capacity
    return pl.pallas_call(
        functools.partial(dispatch_kernel, peers, capacity),
        grid=(peers,),
        in_specs=[pl.BlockSpec(a.shape, lambda k: (0, 0)) for a in (*rows, *cots)],
        out_specs=[
            out_spec(width),
            out_spec(width),
            out_spec(LANES),
            pl.BlockSpec((1, count, length), lambda k: (k, 0, 0)),
            pl.BlockSpec((1, length, LANES), lambda k: (k, 0, 0)),
        ],
        out_shape=[
            shaped(width, bf16),
            shaped(width, bf16),
            shaped(LANES, f32),
            jax.ShapeDtypeStruct((peers, count, length), f32),
            jax.ShapeDtypeStruct((peers, length, LANES), f32),
        ],
        compiler_params=pltpu.CompilerParams(vmem_limit_bytes=VMEM),
        cost_estimate=pl.CostEstimate(
            flops=4 * slots * length * width, bytes_accessed=8 * slots * width, transcendentals=0
        ),
        name="dispatch",
    )(*rows, *cots)


def expert_kernel(first, micro, held, add, final, filled, *refs):
    tables, x_refs, c_refs, g_refs = (refs[i * micro : (i + 1) * micro] for i in range(4))
    w_ref, mask_ref = refs[4 * micro : 4 * micro + 2]
    n, _, capacity, width = x_refs[0].shape
    at = 4 * micro + 2
    old_products = refs[at : at + held]
    old_grads = refs[at + held]
    outs = refs[at + held + 1 + filled :]
    y_refs, m_refs = outs[:n], outs[n : 2 * n]
    grad_ref = outs[2 * n]
    prod_refs = outs[2 * n + 1 : 2 * n + 1 + micro]
    wide, deep, source, sums_a, sums_b, sums_c, sums_d, sums_e = outs[2 * n + 1 + micro :]
    expert = pl.program_id(0)
    if held:

        @pl.when(expert == 0)
        def _():
            for old, new in zip(old_products, prod_refs):
                new[...] = old[...]

    inner_width = deep.shape[0]
    ru, rd = width // SHARDS, inner_width // SHARDS
    blocks = width // LANES
    at = 0

    def part(rows):
        nonlocal at
        value = w_ref[:, 0, at : at + rows, :].reshape(SHARDS * rows, LANES)
        at += rows
        return value

    for j in range(blocks):
        wide[:, j * LANES : (j + 1) * LANES] = part(ru)
    for j in range(blocks):
        deep[:, j * LANES : (j + 1) * LANES] = part(rd)
    for j in range(2):
        source[:, j * LANES : (j + 1) * LANES] = part(ru)
    target_gate, target_up = part(rd), part(rd)
    down_source = part(rd)
    down_target = part(ru)

    size = n * capacity
    for m in range(micro):
        x = x_refs[m][:, 0].reshape(size, width)
        cot = c_refs[m][:, 0].reshape(size, width)
        gate_of_slot = g_refs[m][:, 0].reshape(size, LANES)[:, :1]
        mask = jnp.concatenate(
            [jnp.broadcast_to(mask_ref[m, k : k + 1, :], (capacity, LANES)) for k in range(n)],
            axis=0,
        )
        mask2 = jnp.concatenate([mask, mask], axis=1)
        lora = (nn(x, source[...]) * mask2).astype(bf16)
        gate_up = nn(x, wide[...])
        gate = gate_up[:, :inner_width] + nt(lora[:, :LANES], target_gate)
        up = gate_up[:, inner_width:] + nt(lora[:, LANES:], target_up)
        sig = jax.nn.sigmoid(gate)
        silu = gate * sig
        inner = (silu * up).astype(bf16)
        down_lora = (nn(inner, down_source) * mask).astype(bf16)
        rows = (nn(inner, deep[...]) + nt(down_lora, down_target)).astype(bf16)
        rows_f = rows.astype(f32)
        cot_f = cot.astype(f32)
        product = jnp.sum(rows_f * cot_f, axis=1, keepdims=True)
        weighted = (rows_f * gate_of_slot).astype(bf16)
        row_grad = (cot_f * gate_of_slot).astype(bf16)
        down_lora_grad = (nn(row_grad, down_target) * mask).astype(bf16)
        inner_grad = nt(row_grad, deep[...]) + nt(down_lora_grad, down_source)
        gate_grad = (inner_grad * up * (sig * (1.0 + gate * (1.0 - sig)))).astype(bf16)
        up_grad = (inner_grad * silu).astype(bf16)
        lora_grad = (
            jnp.concatenate([nn(gate_grad, target_gate), nn(up_grad, target_up)], axis=1) * mask2
        ).astype(bf16)
        back = (
            nt(gate_grad, wide[:, :inner_width])
            + nt(up_grad, wide[:, inner_width:])
            + nt(lora_grad, source[...])
        ).astype(bf16)
        for k in range(n):
            here = slice(k * capacity, (k + 1) * capacity)
            y_refs[k][m, 0] = weighted[here]
            if final:
                place = pl.ds(pl.multiple_of(expert * capacity, EXTRA), capacity)
                m_refs[k][place, :] = back[here]
            else:
                m_refs[k][m, 0] = back[here]
            hits = hits_of(tables[m][k, pl.ds(first + expert, 1), :], capacity)
            prod_refs[m][k, pl.ds(first + expert, 1), :] = jnp.sum(
                jnp.where(hits, product[here], 0.0), axis=0, keepdims=True
            )
        terms = (
            tn(lora_grad, x),
            tn(lora[:, :LANES], gate_grad),
            tn(lora[:, LANES:], up_grad),
            tn(down_lora_grad, inner),
            tn(down_lora, row_grad),
        )
        for ref, term in zip((sums_a, sums_b, sums_c, sums_d, sums_e), terms):
            ref[...] = term if m == 0 else ref[...] + term
    if final:

        @pl.when(expert == pl.num_programs(0) - 1)
        def _():
            for k in range(n):
                rows = m_refs[k].shape[0] - EXTRA
                value = jnp.concatenate(pieces_of(prod_refs[0][k]), axis=0)
                put_extra(m_refs[k], rows, value.shape[1], value)

    def put(place, value):
        if add:
            value = value + old_grads[place].astype(f32)
        grad_ref[place] = value.astype(bf16)

    for s in range(SHARDS):
        put((s, 0, slice(0, 2 * LANES)), sums_a[:, s * ru : (s + 1) * ru])
    out = 2 * LANES
    for ref in (sums_b, sums_c, sums_d):
        put((slice(None), 0, slice(out, out + rd)), ref[...].T.reshape(SHARDS, rd, LANES))
        out += rd
    for s in range(SHARDS):
        put((s, 0, slice(out, out + LANES)), sums_e[:, s * ru : (s + 1) * ru])


def expert_chunk(
    slots, weights, masks, first, inner_width, grad_at, grad_count, grads, products, add, final=None, filled=()
):
    micro = len(slots)
    tables = [t[3] for t in slots]
    n, local_count, capacity, width = slots[0][0].shape
    count, rows = weights.shape[1:3]
    rd = inner_width // SHARDS
    grad_rows = 2 * LANES + 3 * rd + LANES
    prod_shape = (n, local_count, tables[0].shape[2])

    def slot_spec(lanes):
        return pl.BlockSpec((n, 1, capacity, lanes), lambda e: (0, first + e, 0, 0))

    out_spec = pl.BlockSpec((micro, 1, capacity, width), lambda e: (0, e, 0, 0))
    out_shape = jax.ShapeDtypeStruct((micro, count, capacity, width), bf16)
    back_spec, back_shape = out_spec, out_shape
    if final:
        total, step = final
        out_shape = jax.ShapeDtypeStruct((total, count, capacity, width), bf16)
        out_spec = pl.BlockSpec((1, 1, capacity, width), lambda e: (step, e, 0, 0))
        back_shape = jax.ShapeDtypeStruct((count * capacity + EXTRA, width), bf16)
        back_spec = pl.BlockSpec(back_shape.shape, lambda e: (0, 0))
    grad_spec = pl.BlockSpec((SHARDS, 1, grad_rows, LANES), lambda e: (0, grad_at + e, 0, 0))
    prod_spec = pl.BlockSpec(prod_shape, lambda e: (0, 0, 0))
    work = n * micro * capacity * count
    held = products or []
    kept = jnp.zeros((8, LANES), f32) if grads is None else grads
    at = 2 + 4 * micro + len(held)
    aliases = {} if grads is None else {at: 2 * n}
    aliases.update({at + 1 + k: k for k in range(len(filled))})
    return pl.pallas_call(
        functools.partial(expert_kernel, first, micro, len(held), add, bool(final), len(filled)),
        grid=(count,),
        in_specs=[pl.BlockSpec(tables[0].shape, lambda e: (0, 0, 0))] * micro
        + [slot_spec(width)] * (2 * micro)
        + [slot_spec(LANES)] * micro
        + [
            pl.BlockSpec((SHARDS, 1, rows, LANES), lambda e: (0, e, 0, 0)),
            pl.BlockSpec(masks.shape, lambda e: (0, 0, 0)),
        ]
        + [prod_spec] * len(held)
        + [grad_spec if add else pl.BlockSpec(memory_space=pl.ANY)]
        + [pl.BlockSpec(memory_space=pl.ANY)] * len(filled),
        out_specs=[out_spec] * n + [back_spec] * n + [grad_spec] + [prod_spec] * micro,
        out_shape=[out_shape] * n
        + [back_shape] * n
        + [jax.ShapeDtypeStruct((SHARDS, grad_count, grad_rows, LANES), bf16)]
        + [jax.ShapeDtypeStruct(prod_shape, f32)] * micro,
        scratch_shapes=[
            pltpu.VMEM((width, 2 * inner_width), bf16),
            pltpu.VMEM((inner_width, width), bf16),
            pltpu.VMEM((width, 2 * LANES), bf16),
            pltpu.VMEM((2 * LANES, width), f32),
            pltpu.VMEM((LANES, inner_width), f32),
            pltpu.VMEM((LANES, inner_width), f32),
            pltpu.VMEM((LANES, inner_width), f32),
            pltpu.VMEM((LANES, width), f32),
        ],
        compiler_params=pltpu.CompilerParams(vmem_limit_bytes=VMEM),
        cost_estimate=pl.CostEstimate(
            flops=10 * 1000 * 1000 * work,
            bytes_accessed=8 * work * width + 6 * count * rows * LANES * SHARDS,
            transcendentals=work * inner_width,
        ),
        input_output_aliases=aliases,
        name="experts",
    )(
        *tables, *[t[0] for t in slots], *[t[1] for t in slots], *[t[2] for t in slots],
        weights, masks, *held, kept, *filled,
    )


def combine_kernel(chunks, jobs, added, *refs):
    columns, refs = refs[:jobs], refs[jobs:]
    row_refs, refs = refs[: jobs * chunks], refs[jobs * chunks :]
    outs = refs[added is not None :]
    capacity, width = row_refs[0].shape[2:]
    length = columns[0].shape[1]
    slot = lax.broadcasted_iota(jnp.int32, (length, LANES), 1)
    spare = jnp.zeros((LANES - capacity, width), bf16)
    for job in range(jobs):
        place = columns[job][0].astype(jnp.int32)
        hot, rows = [], []
        for ref in row_refs[job * chunks : (job + 1) * chunks]:
            for i in range(ref.shape[1]):
                e = len(hot)
                hits = slot == place[:, e : e + 1]
                hot.append(jnp.where(hits, 1.0, 0.0).astype(bf16))
                rows += [ref[0, i], spare]
        total = nn(jnp.concatenate(hot, axis=1), jnp.concatenate(rows, axis=0))
        if added == job:
            total = total + refs[0][...].astype(f32)
        if len(outs) > 1:
            outs[job][...] = total.astype(bf16)
        else:
            outs[0][job * length : (job + 1) * length] = total.astype(bf16)


def combine(slots, jobs, apart=False, add=None):
    columns = [slots[m][4] for _, _, m in jobs]
    length = columns[0].shape[1]
    chunks = len(jobs[0][1])
    capacity, width = jobs[0][1][0].shape[2:]
    work = len(jobs) * sum(a.shape[1] for a in jobs[0][1]) * capacity

    def at(place, a):
        return pl.BlockSpec((1,) + a.shape[1:], lambda i: (place,) + (0,) * (a.ndim - 1))

    added, spec, operand = None, [], []
    if add is not None:
        added, block, place = add
        operand = [block]
        spec = [pl.BlockSpec((length, width), lambda i: (place, 0))]
    shapes = [(length, width)] * len(jobs) if apart else [(len(jobs) * length, width)]
    out = pl.pallas_call(
        functools.partial(combine_kernel, chunks, len(jobs), added),
        grid=(1,),
        in_specs=[at(job[0], a) for job, a in zip(jobs, columns)]
        + [at(m, a) for _, rows, m in jobs for a in rows]
        + spec,
        out_specs=[pl.BlockSpec(shape, lambda i: (0, 0)) for shape in shapes],
        out_shape=[jax.ShapeDtypeStruct(shape, bf16) for shape in shapes],
        compiler_params=pltpu.CompilerParams(vmem_limit_bytes=VMEM),
        cost_estimate=pl.CostEstimate(
            flops=2 * work * length * width, bytes_accessed=3 * work * width, transcendentals=0
        ),
        name="combine",
    )(*columns, *[a for _, rows, _ in jobs for a in rows], *operand)
    return out if apart else out[0]


GROUP = 4
HALF = HD // 2
SPAN = GROUP * HD
REPEAT = H // KVH
NGROUPS = KVH // GROUP
GRAD_ROWS = 9 * REDUCED_DIM


def query_order():
    return [
        (g * GROUP + n) * REPEAT + r
        for g in range(NGROUPS)
        for r in range(REPEAT)
        for n in range(GROUP)
    ]


def halves_order(heads_in_group):
    return [
        heads[n] * 2 + t for heads in heads_in_group for t in range(2) for n in range(GROUP)
    ]


def query_halves():
    order = query_order()
    return halves_order([order[i : i + GROUP] for i in range(0, H, GROUP)])


def key_halves():
    return halves_order([list(range(g * GROUP, (g + 1) * GROUP)) for g in range(NGROUPS)])


def take_rows(a, order, size):
    return jnp.concatenate([a[o * size : (o + 1) * size] for o in order], axis=0)


def columns_back(a, order, size):
    inverse = sorted(range(len(order)), key=lambda i: order[i])
    return jnp.concatenate([a[:, o * size : (o + 1) * size] for o in inverse], axis=1)


def lay_out_columns(a):
    rows = a.shape[0]
    q = a[:, : H * HD].reshape(rows, NGROUPS, GROUP, REPEAT, 2, HALF)
    k = a[:, H * HD : (H + KVH) * HD].reshape(rows, NGROUPS, GROUP, 2, HALF)
    q = q.transpose(0, 1, 3, 4, 2, 5).reshape(rows, H * HD)
    k = k.transpose(0, 1, 3, 2, 4).reshape(rows, KVH * HD)
    return jnp.concatenate([q, k, a[:, (H + KVH) * HD :]], axis=1)


def rope(a, cos, sin, sign):
    out = []
    for at in range(0, a.shape[1], SPAN):
        lead, trail = a[:, at : at + LANES], a[:, at + LANES : at + SPAN]
        out.append(lead * cos - sign * (trail * sin))
        out.append(trail * cos + sign * (lead * sin))
    return jnp.concatenate(out, axis=1)


def lanes_like(a):
    return lax.broadcasted_iota(jnp.int32, a.shape, 1)


def key_of(a, n):
    return jnp.where((lanes_like(a) % LANES) // HALF == n, a, jnp.zeros_like(a))


def value_of(a, n):
    return jnp.where(lanes_like(a) // HD == n, a, jnp.zeros_like(a))


def unpack_kernel(peers, places, me_ref, *refs):
    packed = refs[: len(places)]
    qkv_ref, exit_ref, other_ref = refs[len(places) :]
    width = qkv_ref.shape[0]
    a, b = qkv_ref.shape[1] // LANES // peers, exit_ref.shape[1] // LANES // peers
    c = other_ref.shape[0] // peers
    ru = packed[0].shape[1] // (a + b + c)
    step = min(ru, HD)
    me, core, chip = me_ref[0], me_ref[1], me_ref[2]
    for (k, other_core, first), part in zip(places, packed):
        q = me ^ k
        for i in range(part.shape[0]):
            shard = (chip ^ (first + i)) * 2 + (core ^ other_core)

            def block(j):
                return part[i, j * ru : (j + 1) * ru, :]

            def columns(j):
                return pl.ds(pl.multiple_of(j * LANES, LANES), LANES)

            rows = pl.ds(pl.multiple_of(shard * ru, ru), ru)
            for j in range(a):
                qkv_ref[rows, columns(q * a + j)] = block(j)
            for sub in range(ru // step):
                row = shard * ru + sub * step
                head, within = row // HD, row % HD
                g, n, r = head // (GROUP * REPEAT), head // REPEAT % GROUP, head % REPEAT
                row = ((g * REPEAT + r) * GROUP + n) * HD + within
                rows_out = pl.ds(pl.multiple_of(row, step), step)
                for j in range(b):
                    exit_ref[rows_out, columns(q * b + j)] = block(a + j)[
                        sub * step : (sub + 1) * step
                    ]
            for j in range(c):
                other_ref[q * c + j, rows, :] = block(a + b + j)


def unpack(me, packed, places, peers, width, qkv_width, others):
    whole = pl.BlockSpec(memory_space=pltpu.VMEM)
    return pl.pallas_call(
        functools.partial(unpack_kernel, peers, places),
        in_specs=[pl.BlockSpec(memory_space=pltpu.SMEM)] + [whole] * len(packed),
        out_specs=[whole] * 3,
        out_shape=[
            jax.ShapeDtypeStruct((width, qkv_width), bf16),
            jax.ShapeDtypeStruct((width, width), bf16),
            jax.ShapeDtypeStruct((others, width, LANES), bf16),
        ],
        compiler_params=pltpu.CompilerParams(vmem_limit_bytes=VMEM),
        name="unpack",
    )(me, *packed)


def scale_rows(values):
    return lax.rsqrt(jnp.mean(values * values, axis=-1, keepdims=True) + eps_norm)


def shut_of(labels):
    labels = labels.astype(f32)
    of_query = jnp.broadcast_to(labels, (LANES, labels.shape[1])).T[:, :1]
    return jnp.where(labels <= of_query, 0.0, -1e30)


def attn_forward_kernel(
    me_ref, x_ref, chosen_ref, rank_ref, row_ref, mask_ref, cos_ref, sin_ref, qkv_ref,
    exit_ref, oth_ref, kout_ref, vout_ref, rout_ref, gain_ref,
    res_ref, q_ref, k_ref, v_ref, lse_ref, att_ref, lora_ref, olora_ref, rlora_ref, gate_ref,
    *sent_refs,
):
    length, width = x_ref.shape
    qw, kw = H * HD, KVH * HD
    mask = mask_ref[0]
    cos, sin = cos_ref[...], sin_ref[...]
    hidden = x_ref[...].astype(f32)
    normed = (hidden * scale_rows(hidden) * gain_ref[0:1, :]).astype(bf16)
    lora = [(nn(normed, oth_ref[i]) * mask).astype(bf16) for i in range(3)]
    for i in range(3):
        lora_ref[:, i * LANES : (i + 1) * LANES] = lora[i]
    q_out = take_rows(oth_ref[3], query_halves(), HALF)
    k_out = take_rows(kout_ref[...], key_halves(), HALF)
    q = nn(normed, qkv_ref[:, :qw]) + nt(lora[0], q_out)
    q_ref[...] = (rope(q, cos, sin, 1.0) * HD ** (-0.5)).astype(bf16)
    k = nn(normed, qkv_ref[:, qw : qw + kw]) + nt(lora[1], k_out)
    k_ref[...] = rope(k, cos, sin, 1.0).astype(bf16)
    v_ref[...] = (nn(normed, qkv_ref[:, qw + kw :]) + nt(lora[2], vout_ref[...])).astype(bf16)
    shut = shut_of(row_ref[0])
    lane = lax.broadcasted_iota(jnp.int32, (length, LANES), 1)
    logs = jnp.zeros((length, LANES), f32)
    for g in range(NGROUPS):
        kg = k_ref[:, g * SPAN : (g + 1) * SPAN]
        vg = v_ref[:, g * SPAN : (g + 1) * SPAN]
        totals = [None] * REPEAT
        for n in range(GROUP):
            kn, vn = key_of(kg, n), value_of(vg, n)
            for r in range(REPEAT):
                at = g * REPEAT + r
                s = nt(q_ref[:, at * SPAN : (at + 1) * SPAN], kn) + shut
                peak = jnp.max(s, axis=-1, keepdims=True)
                p = jnp.exp(s - peak)
                total = jnp.sum(p, axis=-1, keepdims=True)
                logs = jnp.where(lane == at * GROUP + n, peak + jnp.log(total), logs)
                probs = (p * (1.0 / total)).astype(bf16)
                term = nn(probs, vn)
                totals[r] = term if n == 0 else totals[r] + term
        for r in range(REPEAT):
            at = g * REPEAT + r
            att_ref[:, at * SPAN : (at + 1) * SPAN] = totals[r].astype(bf16)
    lse_ref[...] = logs
    att = att_ref[...]
    merge_in = take_rows(oth_ref[5], query_order(), HD)
    out_lora = (nn(att, merge_in) * mask).astype(bf16)
    olora_ref[...] = out_lora
    residual = hidden + nn(att, exit_ref[...]) + nt(out_lora, oth_ref[6])
    res_ref[...] = residual
    moe = (residual * scale_rows(residual) * gain_ref[1:2, :]).astype(bf16)
    for ref in sent_refs:
        ref[EXTRA : EXTRA + length] = moe
    route_lora = (nn(moe, oth_ref[7]) * mask).astype(bf16)
    rlora_ref[...] = route_lora
    logits = nn(moe, oth_ref[8]) + nn(route_lora, rout_ref[...])
    shown = jnp.where(chosen_ref[...] > 0, logits, -1e30)
    weight = jnp.where(
        chosen_ref[...] > 0, jnp.exp(shown - jnp.max(shown, axis=1, keepdims=True)), 0.0
    )
    gates = weight / jnp.sum(weight, axis=1, keepdims=True)
    gate_ref[0] = gates.T[: gate_ref.shape[1]]
    own = gate_ref.shape[1] // (len(sent_refs) + 1)

    def numbers(k):
        group = pl.ds(pl.multiple_of((me_ref[0] ^ k) * own, own), own)
        return jnp.concatenate([rank_ref[0, group, :], *pieces_of(gate_ref[0, group, :])], axis=0)

    for k, ref in enumerate(sent_refs):
        put_extra(ref, 0, length, numbers(len(sent_refs)))
        put_extra(ref, EXTRA + length, length, numbers(k))


def attn_forward(step, me, hidden, chosen, rank, rows, mask, cos, sin, weights, peers):
    _, experts, length = rank.shape
    width = hidden.shape[1]

    def by_row(a):
        return pl.BlockSpec((length, a.shape[1]), lambda i: (step, 0))

    def by_step(a):
        return pl.BlockSpec((1,) + a.shape[1:], lambda i: (step,) + (0,) * (a.ndim - 1))

    def whole(a):
        return pl.BlockSpec(a.shape, lambda i: (0,) * a.ndim)

    qw, kw = H * HD, KVH * HD
    shapes = [
        ((length, width), f32), ((length, qw), bf16), ((length, kw), bf16), ((length, kw), bf16),
         ((length, LANES), f32), ((length, qw), bf16), ((length, 3 * LANES), bf16),
        ((length, LANES), bf16), ((length, LANES), bf16), ((1, experts, length), f32),
    ] + [((length + 2 * EXTRA, width), bf16)] * (peers - 1)
    shapes = [jax.ShapeDtypeStruct(*shape) for shape in shapes]
    return pl.pallas_call(
        attn_forward_kernel,
        grid=(1,),
        in_specs=[pl.BlockSpec(memory_space=pltpu.SMEM), by_row(hidden), by_row(chosen)]
        + [by_step(a) for a in (rank, rows, mask)]
        + [whole(a) for a in (cos, sin, *weights)],
        out_specs=[whole(a) for a in shapes],
        out_shape=shapes,
        compiler_params=pltpu.CompilerParams(vmem_limit_bytes=VMEM),
        cost_estimate=pl.CostEstimate(
            flops=2 * length * (5 * width * width + 4 * H * HD * length),
            bytes_accessed=20 * width * width,
            transcendentals=H * length * length,
        ),
        name="attention_forward",
    )(me, hidden, chosen, rank, rows, mask, cos, sin, *weights)


def last_hits(rank_ref, count, capacity):
    return [hits_of(rank_ref[0, i : i + 1, :], capacity) for i in range(count)]


def attn_backward_kernel(
    step, peers, last, parts, older, me_ref, x_ref, cot_ref, row_ref, mask_ref, cos_ref, sin_ref,
    qkv_ref, exit_ref, oth_ref, kout_ref, vout_ref, rout_ref, gain_ref,
    res_ref, q_ref, k_ref, v_ref, lse_ref, att_ref, lora_ref, olora_ref, rlora_ref, gate_ref, moe_ref,
    rank_ref, *refs,
):
    part_refs, tail_refs = refs[:parts], refs[parts : parts + peers]
    at = parts + peers
    old_grads = refs[at : at + older]
    out_ref, grad_ref, product_ref, dq_ref, dk_ref, dv_ref, hold_ref = refs[at + 2 * older :]
    length, width = x_ref.shape
    experts = gate_ref.shape[1]
    own = experts // peers
    capacity = (tail_refs[0].shape[0] - EXTRA) // last
    qw, kw = H * HD, KVH * HD
    mask = mask_ref[0]
    cos, sin = cos_ref[...], sin_ref[...]

    hits = last_hits(rank_ref, peers * last, capacity)
    hot = jnp.concatenate([jnp.where(h, 1.0, 0.0).astype(bf16) for h in hits], axis=0)
    tails = jnp.concatenate([ref[: last * capacity] for ref in tail_refs], axis=0)
    upstream = tn(hot, tails)
    for ref in part_refs:
        upstream = upstream + ref[...].astype(f32)
    for k in range(peers):
        group = pl.ds(pl.multiple_of((me_ref[0] ^ k) * own, own), own)
        value = get_extra(tail_refs[k], last * capacity, length)
        product_ref[group, :] = value[:own] + value[own : 2 * own] + value[2 * own : 3 * own]
    product = product_ref[...]
    gates = gate_ref[0]
    weighted = gates * product
    select = weighted - gates * jnp.sum(weighted, axis=0, keepdims=True)
    select = jnp.concatenate([select, jnp.zeros((LANES - experts, length), f32)], axis=0)
    logit_grad = select.T.astype(bf16)

    route_lora_grad = (nt(logit_grad, rout_ref[...]) * mask).astype(bf16)
    upstream = upstream + nt(logit_grad, oth_ref[8]) + nt(route_lora_grad, oth_ref[7])
    residual = res_ref[...]
    scale = scale_rows(residual)
    scaled = gain_ref[1:2, :] * upstream
    inner = jnp.sum(residual * scaled, axis=-1, keepdims=True) * (1.0 / width)
    res_grad = cot_ref[...].astype(f32) + scale * scaled - residual * (scale * scale * scale * inner)
    att_grad = res_grad.astype(bf16)
    merge_out = oth_ref[6]
    merge_in = take_rows(oth_ref[5], query_order(), HD)
    out_lora_grad = (nn(att_grad, merge_out) * mask).astype(bf16)
    head_grad = (nt(att_grad, exit_ref[...]) + nt(out_lora_grad, merge_in)).astype(bf16)

    shut = shut_of(row_ref[0])
    logs = lse_ref[...]
    for g in range(NGROUPS):
        kg = k_ref[:, g * SPAN : (g + 1) * SPAN]
        vg = v_ref[:, g * SPAN : (g + 1) * SPAN]
        dq = [None] * REPEAT
        qs = [q_ref[:, (g * REPEAT + r) * SPAN : (g * REPEAT + r + 1) * SPAN] for r in range(REPEAT)]
        dos = [
            head_grad[:, (g * REPEAT + r) * SPAN : (g * REPEAT + r + 1) * SPAN]
            for r in range(REPEAT)
        ]
        qts = [a.T for a in qs]
        dots = [a.T for a in dos]
        lead, trail, dvs = [], [], []
        for n in range(GROUP):
            kn, vn = key_of(kg, n), value_of(vg, n)
            dk, dv = None, None
            for r in range(REPEAT):
                at = (g * REPEAT + r) * GROUP + n
                s = nt(qs[r], kn) + (shut - logs[:, at : at + 1])
                p = jnp.exp(s)
                dp = nt(dos[r], vn)
                weight = p * dp
                ds = (weight - p * jnp.sum(weight, axis=-1, keepdims=True)).astype(bf16)
                term = nn(ds, kn)
                dq[r] = term if n == 0 else dq[r] + term
                qt = jnp.concatenate(
                    [
                        qts[r][n * HALF : (n + 1) * HALF],
                        qts[r][LANES + n * HALF : LANES + (n + 1) * HALF],
                    ],
                    axis=0,
                )
                term = nn(qt, ds)
                dk = term if r == 0 else dk + term
                term = nn(dots[r][n * HD : (n + 1) * HD], p.astype(bf16))
                dv = term if r == 0 else dv + term
            lead.append(dk[:HALF])
            trail.append(dk[HALF:])
            dvs.append(dv)
        for r in range(REPEAT):
            at = g * REPEAT + r
            back = rope(dq[r] * HD ** (-0.5), cos, sin, -1.0)
            dq_ref[:, at * SPAN : (at + 1) * SPAN] = back.astype(bf16)
        dk = jnp.concatenate(lead + trail, axis=0).T
        dk_ref[:, g * SPAN : (g + 1) * SPAN] = rope(dk, cos, sin, -1.0).astype(bf16)
        dv_ref[:, g * SPAN : (g + 1) * SPAN] = jnp.concatenate(dvs, axis=0).T.astype(bf16)

    dq, dk, dv = dq_ref[...], dk_ref[...], dv_ref[...]
    q_out = take_rows(oth_ref[3], query_halves(), HALF)
    k_out = take_rows(kout_ref[...], key_halves(), HALF)
    lora_grads = [
        (nn(dq, q_out) * mask).astype(bf16),
        (nn(dk, k_out) * mask).astype(bf16),
        (nn(dv, vout_ref[...]) * mask).astype(bf16),
    ]
    back = (
        nt(dq, qkv_ref[:, :qw]) + nt(dk, qkv_ref[:, qw : qw + kw]) + nt(dv, qkv_ref[:, qw + kw :])
    )
    for i in range(3):
        back = back + nt(lora_grads[i], oth_ref[i])
    hidden = x_ref[...].astype(f32)
    scale = scale_rows(hidden)
    normed = (hidden * scale * gain_ref[0:1, :]).astype(bf16)
    scaled = gain_ref[0:1, :] * back
    inner = jnp.sum(hidden * scaled, axis=-1, keepdims=True) * (1.0 / width)
    out_ref[...] = (
        res_grad + scale * scaled - hidden * (scale * scale * scale * inner)
    ).astype(bf16)

    ru = width // SHARDS
    top = step * GRAD_ROWS
    for old in old_grads:
        grad_ref[:, :top] = old[...]
    adapter = me_ref[3 + step]

    def own_rows(a, b):
        term = tn(a, b)
        hold_ref[:, : term.shape[1]] = term
        rows = pl.ds(pl.multiple_of(adapter * REDUCED_DIM, REDUCED_DIM), REDUCED_DIM)
        return hold_ref[rows, : term.shape[1]]

    lora = [lora_ref[:, i * LANES : (i + 1) * LANES] for i in range(3)]
    pieces = [own_rows(g, normed) for g in lora_grads]
    pieces.append(columns_back(own_rows(lora[0], dq), query_halves(), HALF))
    key_piece = columns_back(own_rows(lora[1], dk), key_halves(), HALF)
    value_piece = own_rows(lora[2], dv)
    pieces.append(
        jnp.concatenate(
            [
                part[:, h * HD : (h + 1) * HD]
                for h in range(KVH)
                for part in (key_piece, value_piece)
            ],
            axis=1,
        )
    )
    pieces.append(columns_back(own_rows(out_lora_grad, att_ref[...]), query_order(), HD))
    pieces.append(own_rows(olora_ref[...], att_grad))
    pieces.append(own_rows(route_lora_grad, moe_ref[EXTRA : EXTRA + length]))
    for i, piece in enumerate(pieces):
        rows = slice(top + i * REDUCED_DIM, top + (i + 1) * REDUCED_DIM)
        for s in range(SHARDS):
            grad_ref[s, rows] = piece[:, s * ru : (s + 1) * ru].astype(bf16)
    piece = own_rows(rlora_ref[...], logit_grad)
    lane = lax.broadcasted_iota(jnp.int32, piece.shape, 1)
    number = jnp.broadcast_to(adapter, piece.shape).astype(f32)
    piece = jnp.where(lane < LANES // 2, piece, number).astype(bf16)
    for s in range(SHARDS):
        grad_ref[s, top + GRAD_ROWS - REDUCED_DIM : top + GRAD_ROWS] = piece


def attn_backward(
    step, last, me, hidden, cotangent, rows, mask, cos, sin, weights, saved, moe, rank, parts, tails, older
):
    length = rows.shape[2]
    width = hidden.shape[1]
    peers = len(tails)
    experts = saved[-1].shape[1]
    grads = jax.ShapeDtypeStruct((SHARDS, (step + 1) * GRAD_ROWS, LANES), bf16)

    def by_row(a):
        return pl.BlockSpec((length, a.shape[1]), lambda i: (step, 0))

    def by_step(a):
        return pl.BlockSpec((1,) + a.shape[1:], lambda i: (step,) + (0,) * (a.ndim - 1))

    def whole(a):
        return pl.BlockSpec(a.shape, lambda i: (0,) * a.ndim)

    qw, kw = H * HD, KVH * HD
    ahead = 7 + len(weights) + len(saved) + 2 + len(parts) + peers
    return pl.pallas_call(
        functools.partial(attn_backward_kernel, step, peers, last, len(parts), len(older) // 2),
        grid=(1,),
        in_specs=[pl.BlockSpec(memory_space=pltpu.SMEM), by_row(hidden), by_row(cotangent)]
        + [by_step(a) for a in (rows, mask)]
        + [whole(a) for a in (cos, sin, *weights, *saved)]
        + [whole(moe), by_step(rank)]
        + [by_row(a) for a in parts]
        + [whole(a) for a in tails]
        + ([whole(older[0]), pl.BlockSpec(memory_space=pl.ANY)] if older else []),
        out_specs=[by_row(hidden), whole(grads)],
        out_shape=[jax.ShapeDtypeStruct(hidden.shape, bf16), grads],
        scratch_shapes=[
            pltpu.VMEM((experts, length), f32),
            pltpu.VMEM((length, qw), bf16),
            pltpu.VMEM((length, kw), bf16),
            pltpu.VMEM((length, kw), bf16),
            pltpu.VMEM((LANES, max(width, qw)), f32),
        ],
        compiler_params=pltpu.CompilerParams(vmem_limit_bytes=VMEM),
        cost_estimate=pl.CostEstimate(
            flops=2 * length * (6 * width * width + 10 * H * HD * length),
            bytes_accessed=30 * width * width,
            transcendentals=H * length * length,
        ),
        input_output_aliases={ahead + 1: 0} if older else {},
        name="attention_backward",
    )(
        me, hidden, cotangent, rows, mask, cos, sin, *weights, *saved, moe, rank, *parts, *tails, *older
    )


def mixture_kernel(res_ref, rank_ref, own_ref, far_ref, *refs):
    parts, out_ref = refs[:3], refs[-1]
    last, capacity, width = far_ref.shape[1:]
    hits = last_hits(rank_ref, 2 * last, capacity)
    hot = jnp.concatenate([jnp.where(h, 1.0, 0.0).astype(bf16) for h in hits], axis=0)
    rows = [ref[0].reshape(last * capacity, width) for ref in (own_ref, far_ref)]
    total = tn(hot, jnp.concatenate(rows, axis=0))
    for ref in parts:
        total = total + ref[...].astype(f32)
    out_ref[...] = (res_ref[...] + total).astype(bf16)


def add_mixture(step, total, residual, rank, own, far, parts, older):
    length, width = residual.shape

    def by_step(a):
        return pl.BlockSpec((1,) + a.shape[1:], lambda i: (step,) + (0,) * (a.ndim - 1))

    def whole(a):
        return pl.BlockSpec(a.shape, lambda i: (0,) * a.ndim)

    return pl.pallas_call(
        mixture_kernel,
        grid=(1,),
        in_specs=[whole(residual), by_step(rank), by_step(own), by_step(far)]
        + [pl.BlockSpec((length, width), lambda i: (step, 0))] * len(parts)
        + [pl.BlockSpec(memory_space=pl.ANY)] * len(older),
        out_specs=pl.BlockSpec((length, width), lambda i: (step, 0)),
        out_shape=jax.ShapeDtypeStruct((total * length, width), bf16),
        compiler_params=pltpu.CompilerParams(vmem_limit_bytes=VMEM),
        cost_estimate=pl.CostEstimate(
            flops=2 * length * 256 * width, bytes_accessed=16 * length * width, transcendentals=0
        ),
        input_output_aliases={4 + len(parts): 0} if older else {},
        name="mixture",
    )(residual, rank, own, far, *parts, *older)


def finish_experts_kernel(chunks, *refs):
    parts = refs[:chunks]
    reduce_ref, expand_ref, deep_ref, last_ref = refs[chunks:]
    wide = reduce_ref.shape[2]
    rd = deep_ref.shape[1]
    e = 0
    for ref in parts:
        for i in range(ref.shape[0]):
            g = ref[i].astype(f32)
            reduce_ref[e] = g[:wide].T
            for j in range(2):
                expand_ref[e, j] = g[wide + j * rd : wide + (j + 1) * rd].T
            deep_ref[e] = g[wide + 2 * rd : wide + 3 * rd]
            last_ref[e] = g[wide + 3 * rd :]
            e += 1


def finish_experts(parts, width, inner_width):
    count = sum(a.shape[0] for a in parts)
    ru, rd = width // SHARDS, inner_width // SHARDS
    whole = pl.BlockSpec(memory_space=pltpu.VMEM)
    return pl.pallas_call(
        functools.partial(finish_experts_kernel, len(parts)),
        in_specs=[whole] * len(parts),
        out_specs=[whole] * 4,
        out_shape=[
            jax.ShapeDtypeStruct((count, ru, 2 * LANES), f32),
            jax.ShapeDtypeStruct((count, 2, LANES, rd), f32),
            jax.ShapeDtypeStruct((count, rd, LANES), f32),
            jax.ShapeDtypeStruct((count, LANES, ru), f32),
        ],
        compiler_params=pltpu.CompilerParams(vmem_limit_bytes=VMEM),
        name="finish_experts",
    )(*parts)


def gather_grads_kernel(g_ref, out_ref, sums_ref):
    sources, rows, _ = g_ref.shape
    sums_ref[...] = jnp.zeros_like(sums_ref)
    for source in range(sources):
        for at in range(0, rows, GRAD_ROWS):
            piece = g_ref[source, at : at + GRAD_ROWS].astype(f32)
            number = piece[GRAD_ROWS - 1 :, LANES - 1 :]
            for a in range(PLUGIN_CHOICES):
                sums_ref[a] += jnp.where(number == a, piece, 0.0)
    for a in range(PLUGIN_CHOICES):
        for at in range(0, GRAD_ROWS, REDUCED_DIM):
            rows = slice((at // REDUCED_DIM * PLUGIN_CHOICES + a) * REDUCED_DIM, None)
            rows = slice(rows.start, rows.start + REDUCED_DIM)
            out_ref[rows] = sums_ref[a, at : at + REDUCED_DIM].astype(bf16)


def gather_grads(received):
    whole = pl.BlockSpec(memory_space=pltpu.VMEM)
    return pl.pallas_call(
        gather_grads_kernel,
        in_specs=[whole],
        out_specs=whole,
        out_shape=jax.ShapeDtypeStruct((GRAD_ROWS * PLUGIN_CHOICES, LANES), bf16),
        scratch_shapes=[pltpu.VMEM((PLUGIN_CHOICES, GRAD_ROWS, LANES), f32)],
        compiler_params=pltpu.CompilerParams(vmem_limit_bytes=VMEM),
        name="gather_grads",
    )(received)


def finish_attention_kernel(peers, shard_ref, *refs):
    parts, outs = refs[:peers], refs[peers:-1]
    hold = refs[-1]
    total = parts[0][...].astype(f32)
    for ref in parts[1:]:
        total = total + ref[...].astype(f32)
    piece = [total[i * LANES : (i + 1) * LANES] for i in range(9)]
    for i in range(3):
        outs[0][:, i * LANES : (i + 1) * LANES] = piece[i].T
    outs[1][...] = piece[3]
    turned = piece[4].T
    outs[2][...] = turned[: outs[2].shape[0]]
    outs[3][...] = turned[outs[2].shape[0] :]
    outs[4][...] = piece[5].T
    outs[5][...] = piece[6]
    outs[6][...] = piece[7].T
    hold[...] = piece[8]
    size = outs[7].shape[0]
    rows = pl.ds(pl.multiple_of(shard_ref[0] * size, size), size)
    outs[7][...] = hold[rows, : outs[7].shape[1]]


def finish_attention(shard, parts, experts):
    adapters, size = LANES, LANES // SHARDS
    half = KVH * HD // SHARDS
    shapes = [
        (LANES, 3 * adapters), (adapters, LANES), (half, adapters), (half, adapters),
        (LANES, adapters), (adapters, LANES), (LANES, adapters), (size, experts),
    ]
    whole = pl.BlockSpec(memory_space=pltpu.VMEM)
    out = pl.pallas_call(
        functools.partial(finish_attention_kernel, len(parts)),
        in_specs=[pl.BlockSpec(memory_space=pltpu.SMEM)] + [whole] * len(parts),
        out_specs=[whole] * len(shapes),
        out_shape=[jax.ShapeDtypeStruct(s, f32) for s in shapes],
        scratch_shapes=[pltpu.VMEM((LANES, LANES), f32)],
        compiler_params=pltpu.CompilerParams(vmem_limit_bytes=VMEM),
        name="finish_attention",
    )(shard, *parts)
    return [a.T if i in (2, 3) else a for i, a in enumerate(out)]


def exchange(a, k):
    if k == 0:
        return a
    size = lax.axis_size("dp")
    return lax.ppermute(a, "dp", [(i, i ^ k) for i in range(size)])


def local(
    layer_entering_state,
    exit_cotangent,
    attend_norm_scaling,
    branch_norm_scaling,
    triple_coefficients,
    attend_exit_coefficients,
    dispatch_coefficients,
    branch_widen_coefficients,
    branch_contract_coefficients,
    triple_plugin_source,
    asking_plugin_target,
    lookup_plugin_target,
    content_plugin_target,
    merge_plugin_source,
    merge_plugin_target,
    dispatch_plugin_source,
    dispatch_plugin_target,
    branch_plugin_source,
    branch_plugin_target,
    contract_plugin_source,
    contract_plugin_target,
    branch_choice_labels,
    plugin_choice_per_text,
    section_labels,
):
    dp_count = lax.axis_size("dp")
    shard_count = lax.axis_size("fsdp")
    dp_rank = lax.axis_index("dp")
    micro_count, seq_len = section_labels.shape
    local_experts = branch_widen_coefficients.shape[0]
    expert_count = local_experts * dp_count
    top_count = branch_choice_labels.shape[1]
    most = seq_len * top_count * 9 // (expert_count * 8)
    capacity = -(-most // 16) * 16
    model_width = layer_entering_state.shape[1]
    inner_width = contract_plugin_source.shape[1] * shard_count
    adapter_width = PLUGIN_CHOICES * REDUCED_DIM
    cos_table, sin_table = rotation(seq_len)
    column_holder = jnp.arange(adapter_width, dtype=jnp.int32) // REDUCED_DIM
    peers = range(dp_count)
    last = CHUNKS[-1]
    core = lax.axis_index("fsdp") % 2
    chip = lax.axis_index("fsdp") // 2 if shard_count == SHARDS else jnp.zeros_like(core)
    me = jnp.concatenate([jnp.stack([dp_rank, core, chip]), plugin_choice_per_text[dp_rank]])
    me = me.astype(jnp.int32)
    shard = lax.axis_index("fsdp").astype(jnp.int32).reshape(1)
    cot_rows = [exit_cotangent[m * seq_len : (m + 1) * seq_len] for m in range(micro_count)]
    cot_from = [[exchange(cot_rows[0], k)] for k in peers]

    labels = branch_choice_labels.reshape(micro_count, seq_len, top_count)
    lane_range = jnp.arange(LANES, dtype=jnp.int32)
    chosen = jnp.any(labels[..., None] == lane_range, axis=2)
    before = jnp.tril(jnp.ones((seq_len, seq_len), bf16), -1)
    chosen_e = chosen[..., :expert_count]
    rank = jnp.einsum("mse,ts->met", chosen_e.astype(bf16), before, preferred_element_type=f32)
    rank = jnp.where(jnp.swapaxes(chosen_e, 1, 2), rank, -1.0)
    chosen = chosen.astype(f32).reshape(micro_count * seq_len, LANES)

    def of_group(a, k):
        return lax.dynamic_slice_in_dim(a, (dp_rank ^ k) * local_experts, local_experts, 1)

    rank_last = jnp.concatenate([of_group(rank, k)[:, -last:] for k in peers], axis=1)
    adapters = [plugin_choice_per_text[dp_rank ^ k] for k in peers]
    masks = jnp.stack(
        [(column_holder[None, :] == own[:, None]).astype(f32) for own in adapters], axis=1
    )
    own_mask = masks[:, :1]
    section_rows = section_labels[:, None, :]

    chunk_weights = []

    def gather_chunk(first, size, before_it, cot_from):
        here = slice(first, first + size)
        shards = (
            branch_widen_coefficients[here],
            branch_contract_coefficients[here],
            branch_plugin_source[here],
            branch_plugin_target[here],
            contract_plugin_source[here],
            contract_plugin_target[here],
        )
        if first:
            shards, before_it, cot_from[1] = lax.optimization_barrier((shards, before_it, cot_from[1]))
        packed = pack_experts(*shards)
        gathered = lax.all_gather(packed, "fsdp", axis=0)
        chunk_weights.append(regroup(gathered, model_width, inner_width))
        return packed

    ru = model_width // shard_count
    kv_cols = lookup_plugin_target.shape[1]
    route_rows = dispatch_plugin_target.shape[0]
    small = jnp.concatenate(
        [
            pad_lanes(dispatch_plugin_target),
            pad_lanes(attend_norm_scaling[None]),
            pad_lanes(branch_norm_scaling[None]),
        ],
        axis=0,
    )
    small = jnp.pad(small, ((0, ru - small.shape[0]), (0, 0)))
    others = jnp.concatenate(
        [
            columns_to_rows(triple_plugin_source),
            asking_plugin_target.T,
            lookup_plugin_target.T,
            content_plugin_target.T,
            merge_plugin_source,
            merge_plugin_target.T,
            dispatch_plugin_source,
            pad_lanes(dispatch_coefficients),
            small,
        ],
        axis=0,
    )
    other_count = others.shape[0] // ru
    other_slots = -(-other_count // dp_count) * dp_count
    others = jnp.pad(others, ((0, (other_slots - other_count) * ru), (0, 0)))

    def own_part(a, axis):
        size = a.shape[axis] // dp_count
        return lax.dynamic_slice_in_dim(a, dp_rank * size, size, axis)

    before_it = gather_chunk(0, CHUNKS[0], None, cot_from)
    parts = (triple_coefficients, attend_exit_coefficients, others)
    parts, before_it = lax.optimization_barrier((parts, before_it))
    part = jnp.concatenate(
        [
            columns_to_rows(own_part(lay_out_columns(parts[0]), 1)),
            columns_to_rows(own_part(parts[1], 1)),
            own_part(parts[2], 0),
        ],
        axis=0,
    )
    if shard_count == SHARDS:
        chips = [part]
        for d in range(1, shard_count // 2):
            pairs = [(i, i ^ (2 * d)) for i in range(shard_count)]
            chips.append(lax.ppermute(part, "fsdp", pairs))
        mine = jnp.stack(chips)
    else:
        part_all = lax.all_gather(part, "fsdp", axis=0)
        mine = part_all.reshape(shard_count // 2, 2, *part.shape)
        mine = lax.dynamic_index_in_dim(mine, core, 1, keepdims=False)
    rank_far = jnp.concatenate([rank_last[:, :last], rank_last[:, 3 * last :]], axis=1)
    (mine, cot_from, rank, rank_last, rank_far, chosen, masks, own_mask, me) = lax.optimization_barrier(
        (mine, cot_from, rank, rank_last, rank_far, chosen, masks, own_mask, me)
    )
    half = mine.shape[0] // 2
    beside = [exchange(mine, 1), exchange(mine, 2)]
    near = [mine, *beside, exchange(beside[1][:half], 1), exchange(beside[0][half:], 2)]
    pairs = [(i, i ^ 1) for i in range(shard_count)]
    far = [lax.ppermute(a, "fsdp", pairs) for a in near]
    places = [(k, c, first) for c in range(2) for k, first in ((0, 0), (1, 0), (2, 0), (3, 0), (3, half))]

    first = CHUNKS[0]
    for size in CHUNKS[1:]:
        before_it = gather_chunk(first, size, before_it, cot_from)
        first += size

    later, near = lax.optimization_barrier((cot_rows[1:], near))
    for k in peers:
        cot_from[k] += [exchange(a, k) for a in later]

    qkv, exit_full, other_full = unpack(
        me, near + far, places, dp_count, model_width, triple_coefficients.shape[1], other_slots
    )
    kv_out = other_full[4].reshape(shard_count, 2, kv_cols, LANES)
    k_out = kv_out[:, 0].reshape(-1, LANES)
    v_out = kv_out[:, 1].reshape(-1, LANES)
    small_full = other_full[9].reshape(shard_count, ru, LANES)
    route_out = small_full[:, :route_rows].reshape(adapter_width, LANES)
    gains = jnp.stack(
        [small_full[:, route_rows + i, :ru].reshape(model_width) for i in range(2)]
    ).astype(f32)
    weights = (qkv, exit_full, other_full, k_out, v_out, route_out, gains)

    micro = range(micro_count)
    saved, sent, slots = [], [], []
    me_then = me
    for m in micro:
        if m > 0:
            me_then, sent[-1] = lax.optimization_barrier((me_then, sent[-1]))
        out = attn_forward(
            m, me_then, layer_entering_state, chosen, rank, section_rows, own_mask,
            cos_table, sin_table, weights, dp_count,
        )
        saved.append(out[: 1 - dp_count])
        sent.append(list(out[1 - dp_count :]))
    first_rows, cot_from = lax.optimization_barrier((sent[0], cot_from))
    sent[0] = first_rows
    rows_from = None
    half = EXTRA + seq_len // 2
    for m in micro:
        if m > 0:
            sent[m], rows_from = lax.optimization_barrier((sent[m], rows_from))
        beside = [exchange(sent[m][1], 1), exchange(sent[m][2], 2)]
        if m + 1 < micro_count:
            beside, sent[m + 1] = lax.optimization_barrier((beside, sent[m + 1]))
        else:
            beside, slots[-1] = lax.optimization_barrier((beside, slots[-1]))
        rows_from = [sent[m][0], *beside]
        rows_from += [exchange(beside[1][:half], 1), exchange(beside[0][half : EXTRA + seq_len], 2)]
        cots = [cot_from[k][m] for k in peers]
        slots.append(dispatch(rows_from, cots, local_experts, capacity))

    n = dp_count
    head = CHUNKS[0]
    outs, first, grads, products = [], 0, None, None
    for size, chunk in zip(CHUNKS[:-1], chunk_weights):
        at = first if first < head else first - head
        count = head if first < head else local_experts - head
        outs.append(
            expert_chunk(
                slots, chunk, masks, first, inner_width, at, count, grads, products, False
            )
        )
        grads, products = outs[-1][2 * n], list(outs[-1][2 * n + 1 :])
        if first == 0:
            head_grads, grads = grads, None
        first += size
    if shard_count == SHARDS:
        head_sum = lax.psum_scatter(head_grads, "fsdp", scatter_dimension=0, tiled=False)
    else:
        head_sum = head_grads

    def rows_of(place):
        return [o[place] for o in outs]

    back_rows = [rows_of(n + k) for k in range(4)]
    far_backs = combine(slots, [(3, back_rows[3], m) for m in micro], apart=True)
    passed = [exchange(a, 1 + m) for m, a in enumerate(far_backs)]
    far_mixes = combine(slots, [(3, rows_of(3), m) for m in micro], apart=True)
    far_mixes, passed = lax.optimization_barrier((far_mixes, passed))
    backs = [
        combine(slots, [(k, back_rows[k], m) for m in micro], add=(2 - k, passed[2 - k], 0))
        for k in (1, 2)
    ]
    passed_mixes = [exchange(a, 1 + m) for m, a in enumerate(far_mixes)]
    back_home = [exchange(a, k) for k, a in zip((1, 2), backs)]
    own_back = combine(slots, [(0, back_rows[0], m) for m in micro])
    own_mix = combine(slots, [(0, rows_of(0), m) for m in micro])
    chunk, _, passed_mixes = lax.optimization_barrier(
        (chunk_weights[-1], (backs, own_back, own_mix), passed_mixes)
    )
    tails, filled = [], []

    for m in micro:
        if m == micro_count - 1:
            chunk, back_home = lax.optimization_barrier((chunk, back_home))
        out = expert_chunk(
            [slots[m]], chunk, masks[m : m + 1], first, inner_width, first - head,
            local_experts - head, grads, [products[m]], m > 0, (micro_count, m), filled,
        )
        filled, grads = list(out[:n]), out[2 * n]
        tails.append(out)
    back_last = []
    for m in micro:
        tail = list(tails[m][n : 2 * n])
        if m == 0:
            tail, back_home = lax.optimization_barrier((tail, back_home))
        else:
            tail, back_last[-1] = lax.optimization_barrier((tail, back_last[-1]))
        back_last.append([exchange(tail[k], k) for k in peers])
    grads, back_last[0] = lax.optimization_barrier((grads, back_last[0]))
    if shard_count == SHARDS:
        tail_sum = lax.psum_scatter(grads, "fsdp", scatter_dimension=0, tiled=False)
    else:
        tail_sum = grads
    outs.append(filled)
    mix_rows = [rows_of(k) for k in range(3)]
    older = []
    for m in micro:
        if m == micro_count - 1:
            back_last[m], head_sum, older, mix_rows = lax.optimization_barrier(
                (back_last[m], head_sum, older, mix_rows)
            )
            mixes = [
                combine(slots, [(k, mix_rows[k], i) for i in micro], add=(2 - k, passed_mixes[2 - k], 0))
                for k in (1, 2)
            ]
            mix_home = [exchange(a, k) for k, a in zip((1, 2), mixes)]
            back_last[m], mixes, far_last = lax.optimization_barrier(
                (back_last[m], mixes, filled[3])
            )
            far_last = exchange(far_last, 3)
        grad_input, attn_grads = attn_backward(
            m, last, me, layer_entering_state, exit_cotangent, section_rows, own_mask,
            cos_table, sin_table, weights, saved[m], sent[m][0], rank_last, [own_back, *back_home], back_last[m],
            older,
        )
        older = [attn_grads, grad_input]
    attn_grads, mix_home = lax.optimization_barrier((attn_grads, mix_home))

    if shard_count == SHARDS:
        received = lax.all_to_all(attn_grads, "fsdp", split_axis=0, concat_axis=0, tiled=True)
        expert_out = finish_experts([head_sum, tail_sum], model_width, inner_width)
        received, expert_out = lax.optimization_barrier((received, expert_out))
        own_sum = gather_grads(received)
        attn_out = finish_attention(shard, [exchange(own_sum, k) for k in peers], expert_count)
    else:
        expert_out = scatter_experts([head_sum, tail_sum], inner_width)
        holds = [(column_holder == me[3 + m]).astype(f32)[:, None] for m in micro]
        attn_out = scatter_attention(attn_grads, holds, expert_count)
    block_out = []
    for m in micro:
        block_out = [
            add_mixture(
                m, micro_count, saved[m][0], rank_far, filled[0], far_last, [own_mix, *mix_home],
                block_out,
            )
        ]
    return (*block_out, grad_input, *attn_out, *expert_out)


def scatter_experts(parts, inner_width):
    g = jnp.concatenate(parts, axis=1).astype(f32)
    count, rd, wide = g.shape[1], inner_width // SHARDS, 2 * LANES
    cuts = [wide + i * rd for i in range(4)]

    def rows_joined(a):
        return jnp.swapaxes(a, 0, 1).reshape(a.shape[1], -1, LANES)

    reduce = g[:, :, :wide].transpose(1, 0, 3, 2).reshape(count, -1, wide)
    expand = jnp.stack(
        [jnp.swapaxes(rows_joined(g[:, :, cuts[i] : cuts[i + 1]]), 1, 2) for i in range(2)],
        axis=1,
    )
    deep = rows_joined(g[:, :, cuts[2] : cuts[3]])
    last = g[:, :, cuts[3] :].transpose(1, 2, 0, 3).reshape(count, LANES, -1)
    return (
        lax.psum_scatter(reduce, "fsdp", scatter_dimension=1, tiled=True),
        lax.psum_scatter(expand, "fsdp", scatter_dimension=3, tiled=True),
        lax.psum_scatter(deep, "fsdp", scatter_dimension=1, tiled=True),
        lax.psum_scatter(last, "fsdp", scatter_dimension=2, tiled=True),
    )


def scatter_attention(packed, holds, experts):
    dense = [0.0] * 9
    for m, hold in enumerate(holds):
        for i in range(9):
            at = m * GRAD_ROWS + i * REDUCED_DIM
            piece = jnp.swapaxes(packed[:, at : at + REDUCED_DIM], 0, 1).astype(f32)
            dense[i] = dense[i] + jnp.tile(piece, (PLUGIN_CHOICES, 1, 1)) * hold[:, :, None]
    flat = [a.reshape(a.shape[0], -1) for a in dense]
    full = (
        (jnp.concatenate([a.T for a in flat[:3]], axis=1), 0),
        (flat[3], 1),
        (dense[4][..., :HD].reshape(LANES, -1), 1),
        (dense[4][..., HD:].reshape(LANES, -1), 1),
        (flat[5].T, 0),
        (flat[6], 1),
        (flat[7].T, 0),
        (dense[8][:, 0, :experts], 0),
    )
    return [
        lax.psum(lax.psum_scatter(a, "fsdp", scatter_dimension=d, tiled=True), "dp")
        for a, d in full
    ]


def solution(mesh):
    placed = (
        P(("dp", "fsdp"), None),
        P(("dp", "fsdp"), None),
        P("fsdp"),
        P("fsdp"),
        P("fsdp", None),
        P("fsdp", None),
        P("fsdp", None),
        P("dp", "fsdp", None),
        P("dp", "fsdp", None),
        P("fsdp", None),
        P(None, "fsdp"),
        P(None, "fsdp"),
        P(None, "fsdp"),
        P("fsdp", None),
        P(None, "fsdp"),
        P("fsdp", None),
        P("fsdp", None),
        P("dp", "fsdp", None),
        P("dp", None, None, "fsdp"),
        P("dp", "fsdp", None),
        P("dp", None, "fsdp"),
        P(("dp", "fsdp"), None),
        P(None, "fsdp"),
        P(("dp", "fsdp"), None),
    )
    return jax.shard_map(
        local,
        mesh=mesh,
        in_specs=placed,
        out_specs=(
            P(("dp", "fsdp"), None),
            P(("dp", "fsdp"), None),
            P("fsdp", None),
            P(None, "fsdp"),
            P(None, "fsdp"),
            P(None, "fsdp"),
            P("fsdp", None),
            P(None, "fsdp"),
            P("fsdp", None),
            P("fsdp", None),
            P("dp", "fsdp", None),
            P("dp", None, None, "fsdp"),
            P("dp", "fsdp", None),
            P("dp", None, "fsdp"),
        ),
        check_vma=False,
    )
```

```python
import functools

import jax
import jax.numpy as jnp
import numpy as np
from jax import lax
from jax.experimental import pallas as pl
from jax.experimental.pallas import tpu as pltpu
from jax.sharding import PartitionSpec as P

H = 16
KVH = 8
HD = 64
FEEDFORWARD_SIZE = 512
PLUGIN_CHOICES = 8
REDUCED_DIM = 16

eps_norm = 1e-06
rope_base = 10000.0

LANES = 128
SHARDS = 8
CHUNKS = (4, 2, 2)
EXTRA = 16
VMEM = 60 * 1024 * 1024

f32 = jnp.float32
bf16 = jnp.bfloat16


def nn(a, b):
    return lax.dot_general(a, b, (((1,), (0,)), ((), ())), preferred_element_type=f32)


def nt(a, b):
    return lax.dot_general(a, b, (((1,), (1,)), ((), ())), preferred_element_type=f32)


def tn(a, b):
    return lax.dot_general(a, b, (((0,), (0,)), ((), ())), preferred_element_type=f32)


def rotation(length):
    half_size = HD // 2
    frequency = rope_base ** (-2.0 * np.arange(half_size) / HD)
    angles = np.arange(length)[:, None] * frequency[None, :]
    return tuple(
        jnp.asarray(np.tile(f(angles), (1, LANES // half_size)), f32) for f in (np.cos, np.sin)
    )


def columns_to_rows(a):
    r, c = a.shape[-2:]
    b = c // LANES
    a = a.reshape(a.shape[:-1] + (b, LANES))
    return jnp.swapaxes(a, -3, -2).reshape(a.shape[:-3] + (b * r, LANES))


def pad_lanes(a):
    return jnp.pad(a, ((0, 0), (0, LANES - a.shape[-1])))


def pack_experts(widen, contract, up_source, up_target, down_source, down_target):
    count = widen.shape[0]
    return jnp.concatenate(
        [
            columns_to_rows(widen),
            columns_to_rows(contract),
            columns_to_rows(up_source),
            jnp.swapaxes(up_target, 2, 3).reshape(count, -1, LANES),
            down_source,
            jnp.swapaxes(down_target, 1, 2),
        ],
        axis=1,
    )


def regroup(gathered, width, inner):
    n, count = gathered.shape[:2]
    if n == SHARDS:
        return gathered
    per = n // SHARDS
    pieces, at = [], 0
    ru, rd = width // n, inner // n
    blocks = ((width // LANES, ru), (width // LANES, rd), (2, ru), (2, rd), (1, rd), (1, ru))
    for b, r in blocks:
        piece = gathered[:, :, at : at + b * r].reshape(SHARDS, per, count, b, r, LANES)
        at += b * r
        pieces.append(piece.transpose(0, 2, 3, 1, 4, 5).reshape(SHARDS, count, b * per * r, LANES))
    return jnp.concatenate(pieces, axis=2)


def hits_of(rank_row, capacity):
    rows = lax.broadcasted_iota(jnp.int32, (capacity, rank_row.shape[1]), 0)
    return rows == rank_row.astype(jnp.int32)


def pieces_of(value):
    high = value.astype(bf16).astype(f32)
    rest = value - high
    middle = rest.astype(bf16).astype(f32)
    return [high, middle, rest - middle]


def put_extra(ref, rows, length, value):
    spare = 2 * EXTRA - value.shape[0]
    if spare:
        value = jnp.concatenate([value, jnp.zeros((spare, length), f32)], axis=0)
    value = value.astype(bf16)
    for i in range(2):
        ref[rows : rows + EXTRA, i * length : (i + 1) * length] = value[i * EXTRA : (i + 1) * EXTRA]
    ref[rows : rows + EXTRA, 2 * length :] = jnp.zeros((EXTRA, ref.shape[1] - 2 * length), bf16)


def get_extra(ref, rows, length):
    return jnp.concatenate(
        [ref[rows : rows + EXTRA, i * length : (i + 1) * length] for i in range(2)], axis=0
    ).astype(f32)


def dispatch_kernel(peers, capacity, *refs):
    x_refs, cots = refs[: peers + 1], refs[peers + 1 : 2 * peers + 1]
    xs_ref, cs_ref, gs_ref, rank_ref, column_ref = refs[2 * peers + 1 :]
    count, _, width = xs_ref.shape[1:]
    length = cots[0].shape[0]
    shape = xs_ref.shape[1:]
    for i in range(peers):

        @pl.when(pl.program_id(0) == i)
        def _():
            if i < peers - 1:
                table = get_extra(x_refs[i], EXTRA + length, length)
                x = x_refs[i][EXTRA : EXTRA + length]
            else:
                table = get_extra(x_refs[i], 0, length)
                x = jnp.concatenate([x_refs[i][EXTRA:], x_refs[i + 1][...]], axis=0)
            rank_ref[0] = table[:count]
            spare = jnp.zeros((LANES - count, length), f32)
            column_ref[0] = jnp.concatenate([table[:count], spare], axis=0).T
            gates = table[count : 2 * count] + table[2 * count : 3 * count] + table[3 * count :]
            hot = []
            for e in range(count):
                hits = hits_of(table[e : e + 1], capacity)
                hot.append(jnp.where(hits, 1.0, 0.0).astype(bf16))
                gate = jnp.sum(jnp.where(hits, gates[e : e + 1], 0.0), axis=1, keepdims=True)
                gs_ref[0, e] = jnp.broadcast_to(gate, (capacity, LANES))
            hot = jnp.concatenate(hot, axis=0)
            xs_ref[0] = nn(hot, x).astype(bf16).reshape(shape)
            cs_ref[0] = nn(hot, cots[i][...]).astype(bf16).reshape(shape)


def dispatch(rows, cots, count, capacity):
    peers = len(cots)
    length, width = cots[0].shape

    def out_spec(lanes):
        return pl.BlockSpec((1, count, capacity, lanes), lambda k: (k, 0, 0, 0))

    def shaped(lanes, dtype):
        return jax.ShapeDtypeStruct((peers, count, capacity, lanes), dtype)

    slots = peers * count * capacity
    return pl.pallas_call(
        functools.partial(dispatch_kernel, peers, capacity),
        grid=(peers,),
        in_specs=[pl.BlockSpec(a.shape, lambda k: (0, 0)) for a in (*rows, *cots)],
        out_specs=[
            out_spec(width),
            out_spec(width),
            out_spec(LANES),
            pl.BlockSpec((1, count, length), lambda k: (k, 0, 0)),
            pl.BlockSpec((1, length, LANES), lambda k: (k, 0, 0)),
        ],
        out_shape=[
            shaped(width, bf16),
            shaped(width, bf16),
            shaped(LANES, f32),
            jax.ShapeDtypeStruct((peers, count, length), f32),
            jax.ShapeDtypeStruct((peers, length, LANES), f32),
        ],
        compiler_params=pltpu.CompilerParams(vmem_limit_bytes=VMEM),
        cost_estimate=pl.CostEstimate(
            flops=4 * slots * length * width, bytes_accessed=8 * slots * width, transcendentals=0
        ),
        name="dispatch",
    )(*rows, *cots)


def expert_kernel(first, micro, held, add, final, filled, *refs):
    tables, x_refs, c_refs, g_refs = (refs[i * micro : (i + 1) * micro] for i in range(4))
    w_ref, mask_ref = refs[4 * micro : 4 * micro + 2]
    n, _, capacity, width = x_refs[0].shape
    at = 4 * micro + 2
    old_products = refs[at : at + held]
    old_grads = refs[at + held]
    outs = refs[at + held + 1 + filled :]
    y_refs, m_refs = outs[:n], outs[n : 2 * n]
    grad_ref = outs[2 * n]
    prod_refs = outs[2 * n + 1 : 2 * n + 1 + micro]
    wide, deep, source, sums_a, sums_b, sums_c, sums_d, sums_e = outs[2 * n + 1 + micro :]
    expert = pl.program_id(0)
    if held:

        @pl.when(expert == 0)
        def _():
            for old, new in zip(old_products, prod_refs):
                new[...] = old[...]

    inner_width = deep.shape[0]
    ru, rd = width // SHARDS, inner_width // SHARDS
    blocks = width // LANES
    at = 0

    def part(rows):
        nonlocal at
        value = w_ref[:, 0, at : at + rows, :].reshape(SHARDS * rows, LANES)
        at += rows
        return value

    for j in range(blocks):
        wide[:, j * LANES : (j + 1) * LANES] = part(ru)
    for j in range(blocks):
        deep[:, j * LANES : (j + 1) * LANES] = part(rd)
    for j in range(2):
        source[:, j * LANES : (j + 1) * LANES] = part(ru)
    target_gate, target_up = part(rd), part(rd)
    down_source = part(rd)
    down_target = part(ru)

    size = n * capacity
    for m in range(micro):
        x = x_refs[m][:, 0].reshape(size, width)
        cot = c_refs[m][:, 0].reshape(size, width)
        gate_of_slot = g_refs[m][:, 0].reshape(size, LANES)[:, :1]
        mask = jnp.concatenate(
            [jnp.broadcast_to(mask_ref[m, k : k + 1, :], (capacity, LANES)) for k in range(n)],
            axis=0,
        )
        mask2 = jnp.concatenate([mask, mask], axis=1)
        lora = (nn(x, source[...]) * mask2).astype(bf16)
        gate_up = nn(x, wide[...])
        gate = gate_up[:, :inner_width] + nt(lora[:, :LANES], target_gate)
        up = gate_up[:, inner_width:] + nt(lora[:, LANES:], target_up)
        sig = jax.nn.sigmoid(gate)
        silu = gate * sig
        inner = (silu * up).astype(bf16)
        down_lora = (nn(inner, down_source) * mask).astype(bf16)
        rows = (nn(inner, deep[...]) + nt(down_lora, down_target)).astype(bf16)
        rows_f = rows.astype(f32)
        cot_f = cot.astype(f32)
        product = jnp.sum(rows_f * cot_f, axis=1, keepdims=True)
        weighted = (rows_f * gate_of_slot).astype(bf16)
        row_grad = (cot_f * gate_of_slot).astype(bf16)
        down_lora_grad = (nn(row_grad, down_target) * mask).astype(bf16)
        inner_grad = nt(row_grad, deep[...]) + nt(down_lora_grad, down_source)
        gate_grad = (inner_grad * up * (sig * (1.0 + gate * (1.0 - sig)))).astype(bf16)
        up_grad = (inner_grad * silu).astype(bf16)
        lora_grad = (
            jnp.concatenate([nn(gate_grad, target_gate), nn(up_grad, target_up)], axis=1) * mask2
        ).astype(bf16)
        back = (
            nt(gate_grad, wide[:, :inner_width])
            + nt(up_grad, wide[:, inner_width:])
            + nt(lora_grad, source[...])
        ).astype(bf16)
        for k in range(n):
            here = slice(k * capacity, (k + 1) * capacity)
            y_refs[k][m, 0] = weighted[here]
            if final:
                place = pl.ds(pl.multiple_of(expert * capacity, EXTRA), capacity)
                m_refs[k][place, :] = back[here]
            else:
                m_refs[k][m, 0] = back[here]
            hits = hits_of(tables[m][k, pl.ds(first + expert, 1), :], capacity)
            prod_refs[m][k, pl.ds(first + expert, 1), :] = jnp.sum(
                jnp.where(hits, product[here], 0.0), axis=0, keepdims=True
            )
        terms = (
            tn(lora_grad, x),
            tn(lora[:, :LANES], gate_grad),
            tn(lora[:, LANES:], up_grad),
            tn(down_lora_grad, inner),
            tn(down_lora, row_grad),
        )
        for ref, term in zip((sums_a, sums_b, sums_c, sums_d, sums_e), terms):
            ref[...] = term if m == 0 else ref[...] + term
    if final:

        @pl.when(expert == pl.num_programs(0) - 1)
        def _():
            for k in range(n):
                rows = m_refs[k].shape[0] - EXTRA
                value = jnp.concatenate(pieces_of(prod_refs[0][k]), axis=0)
                put_extra(m_refs[k], rows, value.shape[1], value)

    def put(place, value):
        if add:
            value = value + old_grads[place].astype(f32)
        grad_ref[place] = value.astype(bf16)

    for s in range(SHARDS):
        put((s, 0, slice(0, 2 * LANES)), sums_a[:, s * ru : (s + 1) * ru])
    out = 2 * LANES
    for ref in (sums_b, sums_c, sums_d):
        put((slice(None), 0, slice(out, out + rd)), ref[...].T.reshape(SHARDS, rd, LANES))
        out += rd
    for s in range(SHARDS):
        put((s, 0, slice(out, out + LANES)), sums_e[:, s * ru : (s + 1) * ru])


def expert_chunk(
    slots, weights, masks, first, inner_width, grad_at, grad_count, grads, products, add, final=None, filled=()
):
    micro = len(slots)
    tables = [t[3] for t in slots]
    n, local_count, capacity, width = slots[0][0].shape
    count, rows = weights.shape[1:3]
    rd = inner_width // SHARDS
    grad_rows = 2 * LANES + 3 * rd + LANES
    prod_shape = (n, local_count, tables[0].shape[2])

    def slot_spec(lanes):
        return pl.BlockSpec((n, 1, capacity, lanes), lambda e: (0, first + e, 0, 0))

    out_spec = pl.BlockSpec((micro, 1, capacity, width), lambda e: (0, e, 0, 0))
    out_shape = jax.ShapeDtypeStruct((micro, count, capacity, width), bf16)
    back_spec, back_shape = out_spec, out_shape
    if final:
        total, step = final
        out_shape = jax.ShapeDtypeStruct((total, count, capacity, width), bf16)
        out_spec = pl.BlockSpec((1, 1, capacity, width), lambda e: (step, e, 0, 0))
        back_shape = jax.ShapeDtypeStruct((count * capacity + EXTRA, width), bf16)
        back_spec = pl.BlockSpec(back_shape.shape, lambda e: (0, 0))
    grad_spec = pl.BlockSpec((SHARDS, 1, grad_rows, LANES), lambda e: (0, grad_at + e, 0, 0))
    prod_spec = pl.BlockSpec(prod_shape, lambda e: (0, 0, 0))
    work = n * micro * capacity * count
    held = products or []
    kept = jnp.zeros((8, LANES), f32) if grads is None else grads
    at = 2 + 4 * micro + len(held)
    aliases = {} if grads is None else {at: 2 * n}
    aliases.update({at + 1 + k: k for k in range(len(filled))})
    return pl.pallas_call(
        functools.partial(expert_kernel, first, micro, len(held), add, bool(final), len(filled)),
        grid=(count,),
        in_specs=[pl.BlockSpec(tables[0].shape, lambda e: (0, 0, 0))] * micro
        + [slot_spec(width)] * (2 * micro)
        + [slot_spec(LANES)] * micro
        + [
            pl.BlockSpec((SHARDS, 1, rows, LANES), lambda e: (0, e, 0, 0)),
            pl.BlockSpec(masks.shape, lambda e: (0, 0, 0)),
        ]
        + [prod_spec] * len(held)
        + [grad_spec if add else pl.BlockSpec(memory_space=pl.ANY)]
        + [pl.BlockSpec(memory_space=pl.ANY)] * len(filled),
        out_specs=[out_spec] * n + [back_spec] * n + [grad_spec] + [prod_spec] * micro,
        out_shape=[out_shape] * n
        + [back_shape] * n
        + [jax.ShapeDtypeStruct((SHARDS, grad_count, grad_rows, LANES), bf16)]
        + [jax.ShapeDtypeStruct(prod_shape, f32)] * micro,
        scratch_shapes=[
            pltpu.VMEM((width, 2 * inner_width), bf16),
            pltpu.VMEM((inner_width, width), bf16),
            pltpu.VMEM((width, 2 * LANES), bf16),
            pltpu.VMEM((2 * LANES, width), f32),
            pltpu.VMEM((LANES, inner_width), f32),
            pltpu.VMEM((LANES, inner_width), f32),
            pltpu.VMEM((LANES, inner_width), f32),
            pltpu.VMEM((LANES, width), f32),
        ],
        compiler_params=pltpu.CompilerParams(vmem_limit_bytes=VMEM),
        cost_estimate=pl.CostEstimate(
            flops=10 * 1000 * 1000 * work,
            bytes_accessed=8 * work * width + 6 * count * rows * LANES * SHARDS,
            transcendentals=work * inner_width,
        ),
        input_output_aliases=aliases,
        name="experts",
    )(
        *tables, *[t[0] for t in slots], *[t[1] for t in slots], *[t[2] for t in slots],
        weights, masks, *held, kept, *filled,
    )


def combine_kernel(chunks, jobs, added, *refs):
    columns, refs = refs[:jobs], refs[jobs:]
    row_refs, refs = refs[: jobs * chunks], refs[jobs * chunks :]
    outs = refs[added is not None :]
    capacity, width = row_refs[0].shape[2:]
    length = columns[0].shape[1]
    slot = lax.broadcasted_iota(jnp.int32, (length, LANES), 1)
    spare = jnp.zeros((LANES - capacity, width), bf16)
    for job in range(jobs):
        place = columns[job][0].astype(jnp.int32)
        hot, rows = [], []
        for ref in row_refs[job * chunks : (job + 1) * chunks]:
            for i in range(ref.shape[1]):
                e = len(hot)
                hits = slot == place[:, e : e + 1]
                hot.append(jnp.where(hits, 1.0, 0.0).astype(bf16))
                rows += [ref[0, i], spare]
        total = nn(jnp.concatenate(hot, axis=1), jnp.concatenate(rows, axis=0))
        if added == job:
            total = total + refs[0][...].astype(f32)
        if len(outs) > 1:
            outs[job][...] = total.astype(bf16)
        else:
            outs[0][job * length : (job + 1) * length] = total.astype(bf16)


def combine(slots, jobs, apart=False, add=None):
    columns = [slots[m][4] for _, _, m in jobs]
    length = columns[0].shape[1]
    chunks = len(jobs[0][1])
    capacity, width = jobs[0][1][0].shape[2:]
    work = len(jobs) * sum(a.shape[1] for a in jobs[0][1]) * capacity

    def at(place, a):
        return pl.BlockSpec((1,) + a.shape[1:], lambda i: (place,) + (0,) * (a.ndim - 1))

    added, spec, operand = None, [], []
    if add is not None:
        added, block, place = add
        operand = [block]
        spec = [pl.BlockSpec((length, width), lambda i: (place, 0))]
    shapes = [(length, width)] * len(jobs) if apart else [(len(jobs) * length, width)]
    out = pl.pallas_call(
        functools.partial(combine_kernel, chunks, len(jobs), added),
        grid=(1,),
        in_specs=[at(job[0], a) for job, a in zip(jobs, columns)]
        + [at(m, a) for _, rows, m in jobs for a in rows]
        + spec,
        out_specs=[pl.BlockSpec(shape, lambda i: (0, 0)) for shape in shapes],
        out_shape=[jax.ShapeDtypeStruct(shape, bf16) for shape in shapes],
        compiler_params=pltpu.CompilerParams(vmem_limit_bytes=VMEM),
        cost_estimate=pl.CostEstimate(
            flops=2 * work * length * width, bytes_accessed=3 * work * width, transcendentals=0
        ),
        name="combine",
    )(*columns, *[a for _, rows, _ in jobs for a in rows], *operand)
    return out if apart else out[0]


GROUP = 4
HALF = HD // 2
SPAN = GROUP * HD
REPEAT = H // KVH
NGROUPS = KVH // GROUP
GRAD_ROWS = 9 * REDUCED_DIM


def query_order():
    return [
        (g * GROUP + n) * REPEAT + r
        for g in range(NGROUPS)
        for r in range(REPEAT)
        for n in range(GROUP)
    ]


def halves_order(heads_in_group):
    return [
        heads[n] * 2 + t for heads in heads_in_group for t in range(2) for n in range(GROUP)
    ]


def query_halves():
    order = query_order()
    return halves_order([order[i : i + GROUP] for i in range(0, H, GROUP)])


def key_halves():
    return halves_order([list(range(g * GROUP, (g + 1) * GROUP)) for g in range(NGROUPS)])


def take_rows(a, order, size):
    return jnp.concatenate([a[o * size : (o + 1) * size] for o in order], axis=0)


def columns_back(a, order, size):
    inverse = sorted(range(len(order)), key=lambda i: order[i])
    return jnp.concatenate([a[:, o * size : (o + 1) * size] for o in inverse], axis=1)


def lay_out_columns(a):
    rows = a.shape[0]
    q = a[:, : H * HD].reshape(rows, NGROUPS, GROUP, REPEAT, 2, HALF)
    k = a[:, H * HD : (H + KVH) * HD].reshape(rows, NGROUPS, GROUP, 2, HALF)
    q = q.transpose(0, 1, 3, 4, 2, 5).reshape(rows, H * HD)
    k = k.transpose(0, 1, 3, 2, 4).reshape(rows, KVH * HD)
    return jnp.concatenate([q, k, a[:, (H + KVH) * HD :]], axis=1)


def rope(a, cos, sin, sign):
    out = []
    for at in range(0, a.shape[1], SPAN):
        lead, trail = a[:, at : at + LANES], a[:, at + LANES : at + SPAN]
        out.append(lead * cos - sign * (trail * sin))
        out.append(trail * cos + sign * (lead * sin))
    return jnp.concatenate(out, axis=1)


def lanes_like(a):
    return lax.broadcasted_iota(jnp.int32, a.shape, 1)


def key_of(a, n):
    return jnp.where((lanes_like(a) % LANES) // HALF == n, a, jnp.zeros_like(a))


def value_of(a, n):
    return jnp.where(lanes_like(a) // HD == n, a, jnp.zeros_like(a))


def unpack_kernel(peers, places, me_ref, *refs):
    packed = refs[: len(places)]
    qkv_ref, exit_ref, other_ref = refs[len(places) :]
    width = qkv_ref.shape[0]
    a, b = qkv_ref.shape[1] // LANES // peers, exit_ref.shape[1] // LANES // peers
    c = other_ref.shape[0] // peers
    ru = packed[0].shape[1] // (a + b + c)
    step = min(ru, HD)
    me, core, chip = me_ref[0], me_ref[1], me_ref[2]
    for (k, other_core, first), part in zip(places, packed):
        q = me ^ k
        for i in range(part.shape[0]):
            shard = (chip ^ (first + i)) * 2 + (core ^ other_core)

            def block(j):
                return part[i, j * ru : (j + 1) * ru, :]

            def columns(j):
                return pl.ds(pl.multiple_of(j * LANES, LANES), LANES)

            rows = pl.ds(pl.multiple_of(shard * ru, ru), ru)
            for j in range(a):
                qkv_ref[rows, columns(q * a + j)] = block(j)
            for sub in range(ru // step):
                row = shard * ru + sub * step
                head, within = row // HD, row % HD
                g, n, r = head // (GROUP * REPEAT), head // REPEAT % GROUP, head % REPEAT
                row = ((g * REPEAT + r) * GROUP + n) * HD + within
                rows_out = pl.ds(pl.multiple_of(row, step), step)
                for j in range(b):
                    exit_ref[rows_out, columns(q * b + j)] = block(a + j)[
                        sub * step : (sub + 1) * step
                    ]
            for j in range(c):
                other_ref[q * c + j, rows, :] = block(a + b + j)


def unpack(me, packed, places, peers, width, qkv_width, others):
    whole = pl.BlockSpec(memory_space=pltpu.VMEM)
    return pl.pallas_call(
        functools.partial(unpack_kernel, peers, places),
        in_specs=[pl.BlockSpec(memory_space=pltpu.SMEM)] + [whole] * len(packed),
        out_specs=[whole] * 3,
        out_shape=[
            jax.ShapeDtypeStruct((width, qkv_width), bf16),
            jax.ShapeDtypeStruct((width, width), bf16),
            jax.ShapeDtypeStruct((others, width, LANES), bf16),
        ],
        compiler_params=pltpu.CompilerParams(vmem_limit_bytes=VMEM),
        name="unpack",
    )(me, *packed)


def scale_rows(values):
    return lax.rsqrt(jnp.mean(values * values, axis=-1, keepdims=True) + eps_norm)


def shut_of(labels):
    labels = labels.astype(f32)
    of_query = jnp.broadcast_to(labels, (LANES, labels.shape[1])).T[:, :1]
    return jnp.where(labels <= of_query, 0.0, -1e30)


def attn_forward_kernel(
    me_ref, x_ref, chosen_ref, rank_ref, row_ref, mask_ref, cos_ref, sin_ref, qkv_ref,
    exit_ref, oth_ref, kout_ref, vout_ref, rout_ref, gain_ref,
    res_ref, q_ref, k_ref, v_ref, lse_ref, att_ref, lora_ref, olora_ref, rlora_ref, gate_ref,
    *sent_refs,
):
    length, width = x_ref.shape
    qw, kw = H * HD, KVH * HD
    mask = mask_ref[0]
    cos, sin = cos_ref[...], sin_ref[...]
    hidden = x_ref[...].astype(f32)
    normed = (hidden * scale_rows(hidden) * gain_ref[0:1, :]).astype(bf16)
    lora = [(nn(normed, oth_ref[i]) * mask).astype(bf16) for i in range(3)]
    for i in range(3):
        lora_ref[:, i * LANES : (i + 1) * LANES] = lora[i]
    q_out = take_rows(oth_ref[3], query_halves(), HALF)
    k_out = take_rows(kout_ref[...], key_halves(), HALF)
    q = nn(normed, qkv_ref[:, :qw]) + nt(lora[0], q_out)
    q_ref[...] = (rope(q, cos, sin, 1.0) * HD ** (-0.5)).astype(bf16)
    k = nn(normed, qkv_ref[:, qw : qw + kw]) + nt(lora[1], k_out)
    k_ref[...] = rope(k, cos, sin, 1.0).astype(bf16)
    v_ref[...] = (nn(normed, qkv_ref[:, qw + kw :]) + nt(lora[2], vout_ref[...])).astype(bf16)
    shut = shut_of(row_ref[0])
    lane = lax.broadcasted_iota(jnp.int32, (length, LANES), 1)
    logs = jnp.zeros((length, LANES), f32)
    for g in range(NGROUPS):
        kg = k_ref[:, g * SPAN : (g + 1) * SPAN]
        vg = v_ref[:, g * SPAN : (g + 1) * SPAN]
        totals = [None] * REPEAT
        for n in range(GROUP):
            kn, vn = key_of(kg, n), value_of(vg, n)
            for r in range(REPEAT):
                at = g * REPEAT + r
                s = nt(q_ref[:, at * SPAN : (at + 1) * SPAN], kn) + shut
                peak = jnp.max(s, axis=-1, keepdims=True)
                p = jnp.exp(s - peak)
                total = jnp.sum(p, axis=-1, keepdims=True)
                logs = jnp.where(lane == at * GROUP + n, peak + jnp.log(total), logs)
                probs = (p * (1.0 / total)).astype(bf16)
                term = nn(probs, vn)
                totals[r] = term if n == 0 else totals[r] + term
        for r in range(REPEAT):
            at = g * REPEAT + r
            att_ref[:, at * SPAN : (at + 1) * SPAN] = totals[r].astype(bf16)
    lse_ref[...] = logs
    att = att_ref[...]
    merge_in = take_rows(oth_ref[5], query_order(), HD)
    out_lora = (nn(att, merge_in) * mask).astype(bf16)
    olora_ref[...] = out_lora
    residual = hidden + nn(att, exit_ref[...]) + nt(out_lora, oth_ref[6])
    res_ref[...] = residual
    moe = (residual * scale_rows(residual) * gain_ref[1:2, :]).astype(bf16)
    for ref in sent_refs:
        ref[EXTRA : EXTRA + length] = moe
    route_lora = (nn(moe, oth_ref[7]) * mask).astype(bf16)
    rlora_ref[...] = route_lora
    logits = nn(moe, oth_ref[8]) + nn(route_lora, rout_ref[...])
    shown = jnp.where(chosen_ref[...] > 0, logits, -1e30)
    weight = jnp.where(
        chosen_ref[...] > 0, jnp.exp(shown - jnp.max(shown, axis=1, keepdims=True)), 0.0
    )
    gates = weight / jnp.sum(weight, axis=1, keepdims=True)
    gate_ref[0] = gates.T[: gate_ref.shape[1]]
    own = gate_ref.shape[1] // (len(sent_refs) + 1)

    def numbers(k):
        group = pl.ds(pl.multiple_of((me_ref[0] ^ k) * own, own), own)
        return jnp.concatenate([rank_ref[0, group, :], *pieces_of(gate_ref[0, group, :])], axis=0)

    for k, ref in enumerate(sent_refs):
        put_extra(ref, 0, length, numbers(len(sent_refs)))
        put_extra(ref, EXTRA + length, length, numbers(k))


def attn_forward(step, me, hidden, chosen, rank, rows, mask, cos, sin, weights, peers):
    _, experts, length = rank.shape
    width = hidden.shape[1]

    def by_row(a):
        return pl.BlockSpec((length, a.shape[1]), lambda i: (step, 0))

    def by_step(a):
        return pl.BlockSpec((1,) + a.shape[1:], lambda i: (step,) + (0,) * (a.ndim - 1))

    def whole(a):
        return pl.BlockSpec(a.shape, lambda i: (0,) * a.ndim)

    qw, kw = H * HD, KVH * HD
    shapes = [
        ((length, width), f32), ((length, qw), bf16), ((length, kw), bf16), ((length, kw), bf16),
         ((length, LANES), f32), ((length, qw), bf16), ((length, 3 * LANES), bf16),
        ((length, LANES), bf16), ((length, LANES), bf16), ((1, experts, length), f32),
    ] + [((length + 2 * EXTRA, width), bf16)] * (peers - 1)
    shapes = [jax.ShapeDtypeStruct(*shape) for shape in shapes]
    return pl.pallas_call(
        attn_forward_kernel,
        grid=(1,),
        in_specs=[pl.BlockSpec(memory_space=pltpu.SMEM), by_row(hidden), by_row(chosen)]
        + [by_step(a) for a in (rank, rows, mask)]
        + [whole(a) for a in (cos, sin, *weights)],
        out_specs=[whole(a) for a in shapes],
        out_shape=shapes,
        compiler_params=pltpu.CompilerParams(vmem_limit_bytes=VMEM),
        cost_estimate=pl.CostEstimate(
            flops=2 * length * (5 * width * width + 4 * H * HD * length),
            bytes_accessed=20 * width * width,
            transcendentals=H * length * length,
        ),
        name="attention_forward",
    )(me, hidden, chosen, rank, rows, mask, cos, sin, *weights)


def last_hits(rank_ref, count, capacity):
    return [hits_of(rank_ref[0, i : i + 1, :], capacity) for i in range(count)]


def attn_backward_kernel(
    step, peers, last, parts, older, me_ref, x_ref, cot_ref, row_ref, mask_ref, cos_ref, sin_ref,
    qkv_ref, exit_ref, oth_ref, kout_ref, vout_ref, rout_ref, gain_ref,
    res_ref, q_ref, k_ref, v_ref, lse_ref, att_ref, lora_ref, olora_ref, rlora_ref, gate_ref, moe_ref,
    rank_ref, *refs,
):
    part_refs, tail_refs = refs[:parts], refs[parts : parts + peers]
    at = parts + peers
    old_grads = refs[at : at + older]
    out_ref, grad_ref, product_ref, dq_ref, dk_ref, dv_ref, hold_ref = refs[
        at + 2 * older : at + 2 * older + 7
    ]
    here, sems = refs[at + 2 * older + 7 : -1], refs[-1]
    length, width = lse_ref.shape[0], x_ref.shape[1]
    rows_here = pl.ds(step * length, length)
    late_refs = here[parts + peers :]
    oth_here, exit_here, qkv_here, res_here, cot_here, q_here, k_here, v_here, x_here = late_refs[:9]
    att_here, moe_here = late_refs[9:]
    copies = [
        *zip(tail_refs, here[parts:]),
        *[(a.at[rows_here], b) for a, b in zip(part_refs, here)],
        (oth_ref.at[5:9], oth_here.at[5:9]),
        (res_ref, res_here),
        (cot_ref.at[rows_here], cot_here),
        (exit_ref, exit_here),
        (q_ref, q_here),
        (k_ref, k_here),
        (v_ref, v_here),
        (oth_ref.at[0:4], oth_here.at[0:4]),
        (qkv_ref, qkv_here),
        (x_ref.at[rows_here], x_here),
        (att_ref, att_here),
        (moe_ref, moe_here),
    ]
    copies = [pltpu.make_async_copy(a, b, sems.at[i]) for i, (a, b) in enumerate(copies)]
    for copy in copies:
        copy.start()
    waiting = iter(copies)

    def await_next(count):
        for _ in range(count):
            next(waiting).wait()

    part_refs, tail_refs = here[:parts], here[parts : parts + peers]
    oth_ref, exit_ref, qkv_ref, res_ref, cot_ref = oth_here, exit_here, qkv_here, res_here, cot_here
    q_ref, k_ref, v_ref, x_ref, att_ref, moe_ref = q_here, k_here, v_here, x_here, att_here, moe_here
    experts = gate_ref.shape[1]
    own = experts // peers
    capacity = (tail_refs[0].shape[0] - EXTRA) // last
    qw, kw = H * HD, KVH * HD
    mask = mask_ref[0]
    cos, sin = cos_ref[...], sin_ref[...]

    hits = last_hits(rank_ref, peers * last, capacity)
    hot = jnp.concatenate([jnp.where(h, 1.0, 0.0).astype(bf16) for h in hits], axis=0)
    await_next(peers)
    tails = jnp.concatenate([ref[: last * capacity] for ref in tail_refs], axis=0)
    upstream = tn(hot, tails)
    for ref in part_refs:
        await_next(1)
        upstream = upstream + ref[...].astype(f32)
    for k in range(peers):
        group = pl.ds(pl.multiple_of((me_ref[0] ^ k) * own, own), own)
        value = get_extra(tail_refs[k], last * capacity, length)
        product_ref[group, :] = value[:own] + value[own : 2 * own] + value[2 * own : 3 * own]
    product = product_ref[...]
    gates = gate_ref[0]
    weighted = gates * product
    select = weighted - gates * jnp.sum(weighted, axis=0, keepdims=True)
    select = jnp.concatenate([select, jnp.zeros((LANES - experts, length), f32)], axis=0)
    logit_grad = select.T.astype(bf16)

    await_next(3)
    route_lora_grad = (nt(logit_grad, rout_ref[...]) * mask).astype(bf16)
    upstream = upstream + nt(logit_grad, oth_ref[8]) + nt(route_lora_grad, oth_ref[7])
    residual = res_ref[...]
    scale = scale_rows(residual)
    scaled = gain_ref[1:2, :] * upstream
    inner = jnp.sum(residual * scaled, axis=-1, keepdims=True) * (1.0 / width)
    res_grad = cot_ref[...].astype(f32) + scale * scaled - residual * (scale * scale * scale * inner)
    att_grad = res_grad.astype(bf16)
    merge_out = oth_ref[6]
    merge_in = take_rows(oth_ref[5], query_order(), HD)
    out_lora_grad = (nn(att_grad, merge_out) * mask).astype(bf16)
    await_next(1)
    head_grad = (nt(att_grad, exit_ref[...]) + nt(out_lora_grad, merge_in)).astype(bf16)

    await_next(3)
    shut = shut_of(row_ref[0])
    logs = lse_ref[...]
    for g in range(NGROUPS):
        kg = k_ref[:, g * SPAN : (g + 1) * SPAN]
        vg = v_ref[:, g * SPAN : (g + 1) * SPAN]
        dq = [None] * REPEAT
        qs = [q_ref[:, (g * REPEAT + r) * SPAN : (g * REPEAT + r + 1) * SPAN] for r in range(REPEAT)]
        dos = [
            head_grad[:, (g * REPEAT + r) * SPAN : (g * REPEAT + r + 1) * SPAN]
            for r in range(REPEAT)
        ]
        qts = [a.T for a in qs]
        dots = [a.T for a in dos]
        lead, trail, dvs = [], [], []
        for n in range(GROUP):
            kn, vn = key_of(kg, n), value_of(vg, n)
            dk, dv = None, None
            for r in range(REPEAT):
                at = (g * REPEAT + r) * GROUP + n
                s = nt(qs[r], kn) + (shut - logs[:, at : at + 1])
                p = jnp.exp(s)
                dp = nt(dos[r], vn)
                weight = p * dp
                ds = (weight - p * jnp.sum(weight, axis=-1, keepdims=True)).astype(bf16)
                term = nn(ds, kn)
                dq[r] = term if n == 0 else dq[r] + term
                qt = jnp.concatenate(
                    [
                        qts[r][n * HALF : (n + 1) * HALF],
                        qts[r][LANES + n * HALF : LANES + (n + 1) * HALF],
                    ],
                    axis=0,
                )
                term = nn(qt, ds)
                dk = term if r == 0 else dk + term
                term = nn(dots[r][n * HD : (n + 1) * HD], p.astype(bf16))
                dv = term if r == 0 else dv + term
            lead.append(dk[:HALF])
            trail.append(dk[HALF:])
            dvs.append(dv)
        for r in range(REPEAT):
            at = g * REPEAT + r
            back = rope(dq[r] * HD ** (-0.5), cos, sin, -1.0)
            dq_ref[:, at * SPAN : (at + 1) * SPAN] = back.astype(bf16)
        dk = jnp.concatenate(lead + trail, axis=0).T
        dk_ref[:, g * SPAN : (g + 1) * SPAN] = rope(dk, cos, sin, -1.0).astype(bf16)
        dv_ref[:, g * SPAN : (g + 1) * SPAN] = jnp.concatenate(dvs, axis=0).T.astype(bf16)

    await_next(5)
    dq, dk, dv = dq_ref[...], dk_ref[...], dv_ref[...]
    q_out = take_rows(oth_ref[3], query_halves(), HALF)
    k_out = take_rows(kout_ref[...], key_halves(), HALF)
    lora_grads = [
        (nn(dq, q_out) * mask).astype(bf16),
        (nn(dk, k_out) * mask).astype(bf16),
        (nn(dv, vout_ref[...]) * mask).astype(bf16),
    ]
    back = (
        nt(dq, qkv_ref[:, :qw]) + nt(dk, qkv_ref[:, qw : qw + kw]) + nt(dv, qkv_ref[:, qw + kw :])
    )
    for i in range(3):
        back = back + nt(lora_grads[i], oth_ref[i])
    hidden = x_ref[...].astype(f32)
    scale = scale_rows(hidden)
    normed = (hidden * scale * gain_ref[0:1, :]).astype(bf16)
    scaled = gain_ref[0:1, :] * back
    inner = jnp.sum(hidden * scaled, axis=-1, keepdims=True) * (1.0 / width)
    out_ref[...] = (
        res_grad + scale * scaled - hidden * (scale * scale * scale * inner)
    ).astype(bf16)

    ru = width // SHARDS
    top = step * GRAD_ROWS
    for old in old_grads:
        grad_ref[:, :top] = old[...]
    adapter = me_ref[3 + step]

    def own_rows(a, b):
        term = tn(a, b)
        hold_ref[:, : term.shape[1]] = term
        rows = pl.ds(pl.multiple_of(adapter * REDUCED_DIM, REDUCED_DIM), REDUCED_DIM)
        return hold_ref[rows, : term.shape[1]]

    lora = [lora_ref[:, i * LANES : (i + 1) * LANES] for i in range(3)]
    pieces = [own_rows(g, normed) for g in lora_grads]
    pieces.append(columns_back(own_rows(lora[0], dq), query_halves(), HALF))
    key_piece = columns_back(own_rows(lora[1], dk), key_halves(), HALF)
    value_piece = own_rows(lora[2], dv)
    pieces.append(
        jnp.concatenate(
            [
                part[:, h * HD : (h + 1) * HD]
                for h in range(KVH)
                for part in (key_piece, value_piece)
            ],
            axis=1,
        )
    )
    pieces.append(columns_back(own_rows(out_lora_grad, att_ref[...]), query_order(), HD))
    pieces.append(own_rows(olora_ref[...], att_grad))
    pieces.append(own_rows(route_lora_grad, moe_ref[EXTRA : EXTRA + length]))
    for i, piece in enumerate(pieces):
        rows = slice(top + i * REDUCED_DIM, top + (i + 1) * REDUCED_DIM)
        for s in range(SHARDS):
            grad_ref[s, rows] = piece[:, s * ru : (s + 1) * ru].astype(bf16)
    piece = own_rows(rlora_ref[...], logit_grad)
    lane = lax.broadcasted_iota(jnp.int32, piece.shape, 1)
    number = jnp.broadcast_to(adapter, piece.shape).astype(f32)
    piece = jnp.where(lane < LANES // 2, piece, number).astype(bf16)
    for s in range(SHARDS):
        grad_ref[s, top + GRAD_ROWS - REDUCED_DIM : top + GRAD_ROWS] = piece


def attn_backward(
    step, last, me, hidden, cotangent, rows, mask, cos, sin, weights, saved, moe, rank, parts, tails, older
):
    length = rows.shape[2]
    width = hidden.shape[1]
    peers = len(tails)
    experts = saved[-1].shape[1]
    grads = jax.ShapeDtypeStruct((SHARDS, (step + 1) * GRAD_ROWS, LANES), bf16)

    def by_row(a):
        return pl.BlockSpec((length, a.shape[1]), lambda i: (step, 0))

    def by_step(a):
        return pl.BlockSpec((1,) + a.shape[1:], lambda i: (step,) + (0,) * (a.ndim - 1))

    def whole(a):
        return pl.BlockSpec(a.shape, lambda i: (0,) * a.ndim)

    far = pl.BlockSpec(memory_space=pl.ANY)
    qkv, exit_full, other = weights[:3]
    res, q, k, v, lse, att = saved[:6]
    qw, kw = H * HD, KVH * HD
    here = [((length, width), bf16)] * len(parts) + [(a.shape, bf16) for a in tails]
    here += [((9,) + other.shape[1:], bf16), (exit_full.shape, bf16), (qkv.shape, bf16)]
    here += [(res.shape, f32), ((length, width), bf16), (q.shape, bf16), (k.shape, bf16)]
    here += [(v.shape, bf16), ((length, width), bf16), (att.shape, bf16), (moe.shape, bf16)]
    ahead = 7 + len(weights) + len(saved) + 2 + len(parts) + peers
    return pl.pallas_call(
        functools.partial(attn_backward_kernel, step, peers, last, len(parts), len(older) // 2),
        grid=(1,),
        in_specs=[pl.BlockSpec(memory_space=pltpu.SMEM), far, far]
        + [by_step(a) for a in (rows, mask)]
        + [whole(a) for a in (cos, sin)]
        + [far] * 3
        + [whole(a) for a in weights[3:]]
        + [far] * 4
        + [whole(lse), far]
        + [whole(a) for a in saved[6:]]
        + [far, by_step(rank)]
        + [far] * (len(parts) + peers)
        + ([whole(older[0]), pl.BlockSpec(memory_space=pl.ANY)] if older else []),
        out_specs=[by_row(hidden), whole(grads)],
        out_shape=[jax.ShapeDtypeStruct(hidden.shape, bf16), grads],
        scratch_shapes=[
            pltpu.VMEM((experts, length), f32),
            pltpu.VMEM((length, qw), bf16),
            pltpu.VMEM((length, kw), bf16),
            pltpu.VMEM((length, kw), bf16),
            pltpu.VMEM((LANES, max(width, qw)), f32),
            *[pltpu.VMEM(*a) for a in here],
            pltpu.SemaphoreType.DMA((len(here) + 1,)),
        ],
        compiler_params=pltpu.CompilerParams(vmem_limit_bytes=VMEM),
        cost_estimate=pl.CostEstimate(
            flops=2 * length * (6 * width * width + 10 * H * HD * length),
            bytes_accessed=30 * width * width,
            transcendentals=H * length * length,
        ),
        input_output_aliases={ahead + 1: 0} if older else {},
        name="attention_backward",
    )(
        me, hidden, cotangent, rows, mask, cos, sin, *weights, *saved, moe, rank, *parts, *tails, *older
    )


def mixture_kernel(res_ref, rank_ref, own_ref, far_ref, *refs):
    parts, out_ref = refs[:3], refs[-1]
    last, capacity, width = far_ref.shape[1:]
    hits = last_hits(rank_ref, 2 * last, capacity)
    hot = jnp.concatenate([jnp.where(h, 1.0, 0.0).astype(bf16) for h in hits], axis=0)
    rows = [ref[0].reshape(last * capacity, width) for ref in (own_ref, far_ref)]
    total = tn(hot, jnp.concatenate(rows, axis=0))
    for ref in parts:
        total = total + ref[...].astype(f32)
    out_ref[...] = (res_ref[...] + total).astype(bf16)


def add_mixture(step, total, residual, rank, own, far, early, parts, older):
    length, width = residual.shape

    def by_step(a):
        return pl.BlockSpec((1,) + a.shape[1:], lambda i: (step,) + (0,) * (a.ndim - 1))

    def whole(a):
        return pl.BlockSpec(a.shape, lambda i: (0,) * a.ndim)

    return pl.pallas_call(
        mixture_kernel,
        grid=(1,),
        in_specs=[whole(residual), by_step(rank), by_step(own), by_step(far)]
        + [pl.BlockSpec((length, width), lambda i: (step, 0))]
        + [whole(a) for a in parts]
        + [pl.BlockSpec(memory_space=pl.ANY)] * len(older),
        out_specs=pl.BlockSpec((length, width), lambda i: (step, 0)),
        out_shape=jax.ShapeDtypeStruct((total * length, width), bf16),
        compiler_params=pltpu.CompilerParams(vmem_limit_bytes=VMEM),
        cost_estimate=pl.CostEstimate(
            flops=2 * length * 256 * width, bytes_accessed=16 * length * width, transcendentals=0
        ),
        input_output_aliases={5 + len(parts): 0} if older else {},
        name="mixture",
    )(residual, rank, own, far, early, *parts, *older)


def finish_experts_kernel(chunks, *refs):
    parts = refs[:chunks]
    reduce_ref, expand_ref, deep_ref, last_ref = refs[chunks:]
    wide = reduce_ref.shape[2]
    rd = deep_ref.shape[1]
    e = 0
    for ref in parts:
        for i in range(ref.shape[0]):
            g = ref[i].astype(f32)
            reduce_ref[e] = g[:wide].T
            for j in range(2):
                expand_ref[e, j] = g[wide + j * rd : wide + (j + 1) * rd].T
            deep_ref[e] = g[wide + 2 * rd : wide + 3 * rd]
            last_ref[e] = g[wide + 3 * rd :]
            e += 1


def finish_experts(parts, width, inner_width):
    count = sum(a.shape[0] for a in parts)
    ru, rd = width // SHARDS, inner_width // SHARDS
    whole = pl.BlockSpec(memory_space=pltpu.VMEM)
    return pl.pallas_call(
        functools.partial(finish_experts_kernel, len(parts)),
        in_specs=[whole] * len(parts),
        out_specs=[whole] * 4,
        out_shape=[
            jax.ShapeDtypeStruct((count, ru, 2 * LANES), f32),
            jax.ShapeDtypeStruct((count, 2, LANES, rd), f32),
            jax.ShapeDtypeStruct((count, rd, LANES), f32),
            jax.ShapeDtypeStruct((count, LANES, ru), f32),
        ],
        compiler_params=pltpu.CompilerParams(vmem_limit_bytes=VMEM),
        name="finish_experts",
    )(*parts)


def gather_grads_kernel(g_ref, out_ref, sums_ref):
    sources, rows, _ = g_ref.shape
    sums_ref[...] = jnp.zeros_like(sums_ref)
    for source in range(sources):
        for at in range(0, rows, GRAD_ROWS):
            piece = g_ref[source, at : at + GRAD_ROWS].astype(f32)
            number = piece[GRAD_ROWS - 1 :, LANES - 1 :]
            for a in range(PLUGIN_CHOICES):
                sums_ref[a] += jnp.where(number == a, piece, 0.0)
    for a in range(PLUGIN_CHOICES):
        for at in range(0, GRAD_ROWS, REDUCED_DIM):
            rows = slice((at // REDUCED_DIM * PLUGIN_CHOICES + a) * REDUCED_DIM, None)
            rows = slice(rows.start, rows.start + REDUCED_DIM)
            out_ref[rows] = sums_ref[a, at : at + REDUCED_DIM].astype(bf16)


def gather_grads(received):
    whole = pl.BlockSpec(memory_space=pltpu.VMEM)
    return pl.pallas_call(
        gather_grads_kernel,
        in_specs=[whole],
        out_specs=whole,
        out_shape=jax.ShapeDtypeStruct((GRAD_ROWS * PLUGIN_CHOICES, LANES), bf16),
        scratch_shapes=[pltpu.VMEM((PLUGIN_CHOICES, GRAD_ROWS, LANES), f32)],
        compiler_params=pltpu.CompilerParams(vmem_limit_bytes=VMEM),
        name="gather_grads",
    )(received)


def finish_attention_kernel(peers, shard_ref, *refs):
    parts, outs = refs[:peers], refs[peers:-1]
    hold = refs[-1]
    total = parts[0][...].astype(f32)
    for ref in parts[1:]:
        total = total + ref[...].astype(f32)
    piece = [total[i * LANES : (i + 1) * LANES] for i in range(9)]
    for i in range(3):
        outs[0][:, i * LANES : (i + 1) * LANES] = piece[i].T
    outs[1][...] = piece[3]
    turned = piece[4].T
    outs[2][...] = turned[: outs[2].shape[0]]
    outs[3][...] = turned[outs[2].shape[0] :]
    outs[4][...] = piece[5].T
    outs[5][...] = piece[6]
    outs[6][...] = piece[7].T
    hold[...] = piece[8]
    size = outs[7].shape[0]
    rows = pl.ds(pl.multiple_of(shard_ref[0] * size, size), size)
    outs[7][...] = hold[rows, : outs[7].shape[1]]


def finish_attention(shard, parts, experts):
    adapters, size = LANES, LANES // SHARDS
    half = KVH * HD // SHARDS
    shapes = [
        (LANES, 3 * adapters), (adapters, LANES), (half, adapters), (half, adapters),
        (LANES, adapters), (adapters, LANES), (LANES, adapters), (size, experts),
    ]
    whole = pl.BlockSpec(memory_space=pltpu.VMEM)
    out = pl.pallas_call(
        functools.partial(finish_attention_kernel, len(parts)),
        in_specs=[pl.BlockSpec(memory_space=pltpu.SMEM)] + [whole] * len(parts),
        out_specs=[whole] * len(shapes),
        out_shape=[jax.ShapeDtypeStruct(s, f32) for s in shapes],
        scratch_shapes=[pltpu.VMEM((LANES, LANES), f32)],
        compiler_params=pltpu.CompilerParams(vmem_limit_bytes=VMEM),
        name="finish_attention",
    )(shard, *parts)
    return [a.T if i in (2, 3) else a for i, a in enumerate(out)]


def exchange(a, k):
    if k == 0:
        return a
    size = lax.axis_size("dp")
    return lax.ppermute(a, "dp", [(i, i ^ k) for i in range(size)])


def local(
    layer_entering_state,
    exit_cotangent,
    attend_norm_scaling,
    branch_norm_scaling,
    triple_coefficients,
    attend_exit_coefficients,
    dispatch_coefficients,
    branch_widen_coefficients,
    branch_contract_coefficients,
    triple_plugin_source,
    asking_plugin_target,
    lookup_plugin_target,
    content_plugin_target,
    merge_plugin_source,
    merge_plugin_target,
    dispatch_plugin_source,
    dispatch_plugin_target,
    branch_plugin_source,
    branch_plugin_target,
    contract_plugin_source,
    contract_plugin_target,
    branch_choice_labels,
    plugin_choice_per_text,
    section_labels,
):
    dp_count = lax.axis_size("dp")
    shard_count = lax.axis_size("fsdp")
    dp_rank = lax.axis_index("dp")
    micro_count, seq_len = section_labels.shape
    local_experts = branch_widen_coefficients.shape[0]
    expert_count = local_experts * dp_count
    top_count = branch_choice_labels.shape[1]
    most = seq_len * top_count * 9 // (expert_count * 8)
    capacity = -(-most // 16) * 16
    model_width = layer_entering_state.shape[1]
    inner_width = contract_plugin_source.shape[1] * shard_count
    adapter_width = PLUGIN_CHOICES * REDUCED_DIM
    cos_table, sin_table = rotation(seq_len)
    column_holder = jnp.arange(adapter_width, dtype=jnp.int32) // REDUCED_DIM
    peers = range(dp_count)
    last = CHUNKS[-1]
    core = lax.axis_index("fsdp") % 2
    chip = lax.axis_index("fsdp") // 2 if shard_count == SHARDS else jnp.zeros_like(core)
    me = jnp.concatenate([jnp.stack([dp_rank, core, chip]), plugin_choice_per_text[dp_rank]])
    me = me.astype(jnp.int32)
    shard = lax.axis_index("fsdp").astype(jnp.int32).reshape(1)
    cot_rows = [exit_cotangent[m * seq_len : (m + 1) * seq_len] for m in range(micro_count)]
    cot_from = [[exchange(cot_rows[0], k)] for k in peers]

    labels = branch_choice_labels.reshape(micro_count, seq_len, top_count)
    lane_range = jnp.arange(LANES, dtype=jnp.int32)
    chosen = jnp.any(labels[..., None] == lane_range, axis=2)
    before = jnp.tril(jnp.ones((seq_len, seq_len), bf16), -1)
    chosen_e = chosen[..., :expert_count]
    rank = jnp.einsum("mse,ts->met", chosen_e.astype(bf16), before, preferred_element_type=f32)
    rank = jnp.where(jnp.swapaxes(chosen_e, 1, 2), rank, -1.0)
    chosen = chosen.astype(f32).reshape(micro_count * seq_len, LANES)

    def of_group(a, k):
        return lax.dynamic_slice_in_dim(a, (dp_rank ^ k) * local_experts, local_experts, 1)

    rank_last = jnp.concatenate([of_group(rank, k)[:, -last:] for k in peers], axis=1)
    adapters = [plugin_choice_per_text[dp_rank ^ k] for k in peers]
    masks = jnp.stack(
        [(column_holder[None, :] == own[:, None]).astype(f32) for own in adapters], axis=1
    )
    own_mask = masks[:, :1]
    section_rows = section_labels[:, None, :]

    chunk_weights = []

    def gather_chunk(first, size, before_it, cot_from):
        here = slice(first, first + size)
        shards = (
            branch_widen_coefficients[here],
            branch_contract_coefficients[here],
            branch_plugin_source[here],
            branch_plugin_target[here],
            contract_plugin_source[here],
            contract_plugin_target[here],
        )
        if first:
            shards, before_it, cot_from[1] = lax.optimization_barrier((shards, before_it, cot_from[1]))
        packed = pack_experts(*shards)
        gathered = lax.all_gather(packed, "fsdp", axis=0)
        chunk_weights.append(regroup(gathered, model_width, inner_width))
        return packed

    ru = model_width // shard_count
    kv_cols = lookup_plugin_target.shape[1]
    route_rows = dispatch_plugin_target.shape[0]
    small = jnp.concatenate(
        [
            pad_lanes(dispatch_plugin_target),
            pad_lanes(attend_norm_scaling[None]),
            pad_lanes(branch_norm_scaling[None]),
        ],
        axis=0,
    )
    small = jnp.pad(small, ((0, ru - small.shape[0]), (0, 0)))
    others = jnp.concatenate(
        [
            columns_to_rows(triple_plugin_source),
            asking_plugin_target.T,
            lookup_plugin_target.T,
            content_plugin_target.T,
            merge_plugin_source,
            merge_plugin_target.T,
            dispatch_plugin_source,
            pad_lanes(dispatch_coefficients),
            small,
        ],
        axis=0,
    )
    other_count = others.shape[0] // ru
    other_slots = -(-other_count // dp_count) * dp_count
    others = jnp.pad(others, ((0, (other_slots - other_count) * ru), (0, 0)))

    def own_part(a, axis):
        size = a.shape[axis] // dp_count
        return lax.dynamic_slice_in_dim(a, dp_rank * size, size, axis)

    before_it = gather_chunk(0, CHUNKS[0], None, cot_from)
    parts = (triple_coefficients, attend_exit_coefficients, others)
    parts, before_it = lax.optimization_barrier((parts, before_it))
    part = jnp.concatenate(
        [
            columns_to_rows(own_part(lay_out_columns(parts[0]), 1)),
            columns_to_rows(own_part(parts[1], 1)),
            own_part(parts[2], 0),
        ],
        axis=0,
    )
    if shard_count == SHARDS:
        chips = [part]
        for d in range(1, shard_count // 2):
            pairs = [(i, i ^ (2 * d)) for i in range(shard_count)]
            chips.append(lax.ppermute(part, "fsdp", pairs))
        mine = jnp.stack(chips)
    else:
        part_all = lax.all_gather(part, "fsdp", axis=0)
        mine = part_all.reshape(shard_count // 2, 2, *part.shape)
        mine = lax.dynamic_index_in_dim(mine, core, 1, keepdims=False)
    rank_far = jnp.concatenate([rank_last[:, :last], rank_last[:, 3 * last :]], axis=1)
    (mine, cot_from, rank, rank_last, rank_far, chosen, masks, own_mask, me) = lax.optimization_barrier(
        (mine, cot_from, rank, rank_last, rank_far, chosen, masks, own_mask, me)
    )
    half = mine.shape[0] // 2
    beside = [exchange(mine, 1), exchange(mine, 2)]
    near = [mine, *beside, exchange(beside[1][:half], 1), exchange(beside[0][half:], 2)]
    pairs = [(i, i ^ 1) for i in range(shard_count)]
    far = [lax.ppermute(a, "fsdp", pairs) for a in near]
    places = [(k, c, first) for c in range(2) for k, first in ((0, 0), (1, 0), (2, 0), (3, 0), (3, half))]

    first = CHUNKS[0]
    for size in CHUNKS[1:]:
        before_it = gather_chunk(first, size, before_it, cot_from)
        first += size

    later, near = lax.optimization_barrier((cot_rows[1:], near))
    for k in peers:
        cot_from[k] += [exchange(a, k) for a in later]

    qkv, exit_full, other_full = unpack(
        me, near + far, places, dp_count, model_width, triple_coefficients.shape[1], other_slots
    )
    kv_out = other_full[4].reshape(shard_count, 2, kv_cols, LANES)
    k_out = kv_out[:, 0].reshape(-1, LANES)
    v_out = kv_out[:, 1].reshape(-1, LANES)
    small_full = other_full[9].reshape(shard_count, ru, LANES)
    route_out = small_full[:, :route_rows].reshape(adapter_width, LANES)
    gains = jnp.stack(
        [small_full[:, route_rows + i, :ru].reshape(model_width) for i in range(2)]
    ).astype(f32)
    weights = (qkv, exit_full, other_full, k_out, v_out, route_out, gains)

    micro = range(micro_count)
    saved, sent, slots = [], [], []
    me_then = me
    for m in micro:
        if m > 0:
            me_then, sent[-1] = lax.optimization_barrier((me_then, sent[-1]))
        out = attn_forward(
            m, me_then, layer_entering_state, chosen, rank, section_rows, own_mask,
            cos_table, sin_table, weights, dp_count,
        )
        saved.append(out[: 1 - dp_count])
        sent.append(list(out[1 - dp_count :]))
    first_rows, cot_from = lax.optimization_barrier((sent[0], cot_from))
    sent[0] = first_rows
    rows_from = None
    half = EXTRA + seq_len // 2
    for m in micro:
        if m > 0:
            sent[m], rows_from = lax.optimization_barrier((sent[m], rows_from))
        beside = [exchange(sent[m][1], 1), exchange(sent[m][2], 2)]
        if m + 1 < micro_count:
            beside, sent[m + 1] = lax.optimization_barrier((beside, sent[m + 1]))
        else:
            beside, slots[-1] = lax.optimization_barrier((beside, slots[-1]))
        rows_from = [sent[m][0], *beside]
        rows_from += [exchange(beside[1][:half], 1), exchange(beside[0][half : EXTRA + seq_len], 2)]
        cots = [cot_from[k][m] for k in peers]
        slots.append(dispatch(rows_from, cots, local_experts, capacity))

    n = dp_count
    head = CHUNKS[0]
    outs, first, grads, products = [], 0, None, None
    for size, chunk in zip(CHUNKS[:-1], chunk_weights):
        at = first if first < head else first - head
        count = head if first < head else local_experts - head
        outs.append(
            expert_chunk(
                slots, chunk, masks, first, inner_width, at, count, grads, products, False
            )
        )
        grads, products = outs[-1][2 * n], list(outs[-1][2 * n + 1 :])
        if first == 0:
            head_grads, grads = grads, None
        first += size
    if shard_count == SHARDS:
        head_sum = lax.psum_scatter(head_grads, "fsdp", scatter_dimension=0, tiled=False)
    else:
        head_sum = head_grads

    def rows_of(place):
        return [o[place] for o in outs]

    back_rows = [rows_of(n + k) for k in range(4)]
    far_backs = combine(slots, [(3, back_rows[3], m) for m in micro], apart=True)
    passed = [exchange(a, 1 + m) for m, a in enumerate(far_backs)]
    far_mixes = combine(slots, [(3, rows_of(3), m) for m in micro], apart=True)
    far_mixes, passed = lax.optimization_barrier((far_mixes, passed))
    backs = [
        combine(slots, [(k, back_rows[k], m) for m in micro], add=(2 - k, passed[2 - k], 0))
        for k in (1, 2)
    ]
    passed_mixes = [exchange(a, 1 + m) for m, a in enumerate(far_mixes)]
    back_home = [exchange(a, k) for k, a in zip((1, 2), backs)]
    own_back = combine(slots, [(0, back_rows[0], m) for m in micro])
    own_mix = combine(slots, [(0, rows_of(0), m) for m in micro])
    chunk, _, passed_mixes = lax.optimization_barrier(
        (chunk_weights[-1], (backs, own_back, own_mix), passed_mixes)
    )
    tails, filled = [], []


    def mixes_of(m, rows):
        return combine(slots, [(k, rows[k], m) for k in (1, 2)], apart=True, add=(1 - m, passed_mixes[m], 0))

    for m in micro:
        if m == micro_count - 1:
            mixes = mixes_of(0, {k: rows_of(k) + [filled[k]] for k in (1, 2)})
            chunk, back_home, mixes = lax.optimization_barrier((chunk, back_home, mixes))
        out = expert_chunk(
            [slots[m]], chunk, masks[m : m + 1], first, inner_width, first - head,
            local_experts - head, grads, [products[m]], m > 0, (micro_count, m), filled,
        )
        filled, grads = list(out[:n]), out[2 * n]
        tails.append(out)
    back_last = []
    for m in micro:
        tail = list(tails[m][n : 2 * n])
        if m == 0:
            tail, back_home = lax.optimization_barrier((tail, back_home))
        else:
            tail, back_last[-1] = lax.optimization_barrier((tail, back_last[-1]))
        back_last.append([exchange(tail[k], k) for k in peers])
    grads, back_last[0] = lax.optimization_barrier((grads, back_last[0]))
    if shard_count == SHARDS:
        tail_sum = lax.psum_scatter(grads, "fsdp", scatter_dimension=0, tiled=False)
    else:
        tail_sum = grads
    outs.append(filled)
    mix_rows = [rows_of(k) for k in range(3)]
    older = []
    for m in micro:
        if m == micro_count - 1:
            mix_rows, older = lax.optimization_barrier((mix_rows, older))
            then = mixes_of(1, mix_rows)
            back_last[m], head_sum, older, mixes, then = lax.optimization_barrier(
                (back_last[m], head_sum, older, mixes, then)
            )
            mix_home = [[exchange(a, k) for k, a in zip((1, 2), pair)] for pair in (mixes, then)]
        grad_input, attn_grads = attn_backward(
            m, last, me, layer_entering_state, exit_cotangent, section_rows, own_mask,
            cos_table, sin_table, weights, saved[m], sent[m][0], rank_last, [own_back, *back_home], back_last[m],
            older,
        )
        older = [attn_grads, grad_input]
    attn_grads, mix_home, far_last = lax.optimization_barrier((attn_grads, mix_home, filled[3]))
    far_last = exchange(far_last, 3)

    if shard_count == SHARDS:
        received = lax.all_to_all(attn_grads, "fsdp", split_axis=0, concat_axis=0, tiled=True)
        expert_out = finish_experts([head_sum, tail_sum], model_width, inner_width)
        received, expert_out = lax.optimization_barrier((received, expert_out))
        own_sum = gather_grads(received)
        attn_out = finish_attention(shard, [exchange(own_sum, k) for k in peers], expert_count)
    else:
        expert_out = scatter_experts([head_sum, tail_sum], inner_width)
        holds = [(column_holder == me[3 + m]).astype(f32)[:, None] for m in micro]
        attn_out = scatter_attention(attn_grads, holds, expert_count)
    block_out = []
    for m in micro:
        block_out = [
            add_mixture(
                m, micro_count, saved[m][0], rank_far, filled[0], far_last, own_mix, mix_home[m], block_out,
            )
        ]
    return (*block_out, grad_input, *attn_out, *expert_out)


def scatter_experts(parts, inner_width):
    g = jnp.concatenate(parts, axis=1).astype(f32)
    count, rd, wide = g.shape[1], inner_width // SHARDS, 2 * LANES
    cuts = [wide + i * rd for i in range(4)]

    def rows_joined(a):
        return jnp.swapaxes(a, 0, 1).reshape(a.shape[1], -1, LANES)

    reduce = g[:, :, :wide].transpose(1, 0, 3, 2).reshape(count, -1, wide)
    expand = jnp.stack(
        [jnp.swapaxes(rows_joined(g[:, :, cuts[i] : cuts[i + 1]]), 1, 2) for i in range(2)],
        axis=1,
    )
    deep = rows_joined(g[:, :, cuts[2] : cuts[3]])
    last = g[:, :, cuts[3] :].transpose(1, 2, 0, 3).reshape(count, LANES, -1)
    return (
        lax.psum_scatter(reduce, "fsdp", scatter_dimension=1, tiled=True),
        lax.psum_scatter(expand, "fsdp", scatter_dimension=3, tiled=True),
        lax.psum_scatter(deep, "fsdp", scatter_dimension=1, tiled=True),
        lax.psum_scatter(last, "fsdp", scatter_dimension=2, tiled=True),
    )


def scatter_attention(packed, holds, experts):
    dense = [0.0] * 9
    for m, hold in enumerate(holds):
        for i in range(9):
            at = m * GRAD_ROWS + i * REDUCED_DIM
            piece = jnp.swapaxes(packed[:, at : at + REDUCED_DIM], 0, 1).astype(f32)
            dense[i] = dense[i] + jnp.tile(piece, (PLUGIN_CHOICES, 1, 1)) * hold[:, :, None]
    flat = [a.reshape(a.shape[0], -1) for a in dense]
    full = (
        (jnp.concatenate([a.T for a in flat[:3]], axis=1), 0),
        (flat[3], 1),
        (dense[4][..., :HD].reshape(LANES, -1), 1),
        (dense[4][..., HD:].reshape(LANES, -1), 1),
        (flat[5].T, 0),
        (flat[6], 1),
        (flat[7].T, 0),
        (dense[8][:, 0, :experts], 0),
    )
    return [
        lax.psum(lax.psum_scatter(a, "fsdp", scatter_dimension=d, tiled=True), "dp")
        for a, d in full
    ]


def solution(mesh):
    placed = (
        P(("dp", "fsdp"), None),
        P(("dp", "fsdp"), None),
        P("fsdp"),
        P("fsdp"),
        P("fsdp", None),
        P("fsdp", None),
        P("fsdp", None),
        P("dp", "fsdp", None),
        P("dp", "fsdp", None),
        P("fsdp", None),
        P(None, "fsdp"),
        P(None, "fsdp"),
        P(None, "fsdp"),
        P("fsdp", None),
        P(None, "fsdp"),
        P("fsdp", None),
        P("fsdp", None),
        P("dp", "fsdp", None),
        P("dp", None, None, "fsdp"),
        P("dp", "fsdp", None),
        P("dp", None, "fsdp"),
        P(("dp", "fsdp"), None),
        P(None, "fsdp"),
        P(("dp", "fsdp"), None),
    )
    return jax.shard_map(
        local,
        mesh=mesh,
        in_specs=placed,
        out_specs=(
            P(("dp", "fsdp"), None),
            P(("dp", "fsdp"), None),
            P("fsdp", None),
            P(None, "fsdp"),
            P(None, "fsdp"),
            P(None, "fsdp"),
            P("fsdp", None),
            P(None, "fsdp"),
            P("fsdp", None),
            P("fsdp", None),
            P("dp", "fsdp", None),
            P("dp", None, None, "fsdp"),
            P("dp", "fsdp", None),
            P("dp", None, "fsdp"),
        ),
        check_vma=False,
    )
```
